128 devices in a mesh: section: 2 (over core), dp: 16 (over x, z), tensor: 4 (over y).
Axes of the slice: x: 4, y: 4, z: 4, core: 2. Of those that a mesh axis runs over, the one named last changes fastest.
Arguments:
- pipe_in: bfloat16 [2, 2, 4096, 1024], P('section', None, 'dp'), may hold values from -6 to 6
- doc_lengths: int32 [32, 4], P('dp'), may hold values from 1 to 128, 256 in all within a row
- norm_in: bfloat16 [2, 1024], P('section', ('dp', 'tensor')), may hold values from 0.5 to 1.5
- w_query: bfloat16 [2, 1024, 512], P('section', 'dp', 'tensor'), may hold values from -0.1875 to 0.1875
- w_key: bfloat16 [2, 1024, 512], P('section', 'dp', 'tensor'), may hold values from -0.1875 to 0.1875
- w_value: bfloat16 [2, 1024, 1024], P('section', 'dp', 'tensor'), may hold values from -0.1875 to 0.1875
- w_out_gate: bfloat16 [2, 1024, 1024], P('section', 'dp', 'tensor'), may hold values from -0.1875 to 0.1875
- w_rank_down: bfloat16 [2, 1024, 16], P('section', ('dp', 'tensor')), may hold values from -0.1875 to 0.1875
- w_rank_up: bfloat16 [2, 16, 512], P('section', 'dp', 'tensor'), may hold values from -1.5 to 1.5
- rank_bias: bfloat16 [2, 512], P('section', ('dp', 'tensor')), may hold values from -2 to 4
- head_gain: bfloat16 [2, 256], P('section', ('dp', 'tensor')), may hold values from 0.5 to 1.5
- w_out: bfloat16 [2, 1024, 1024], P('section', 'tensor', 'dp'), may hold values from -0.375 to 0.375
- norm_mid: bfloat16 [2, 1024], P('section', ('dp', 'tensor')), may hold values from 0.5 to 1.5
- w_gate: bfloat16 [2, 1024, 2816], P('section', 'dp', 'tensor'), may hold values from -0.1875 to 0.1875
- w_up: bfloat16 [2, 1024, 2816], P('section', 'dp', 'tensor'), may hold values from -0.1875 to 0.1875
- w_down: bfloat16 [2, 2816, 1024], P('section', 'tensor', 'dp'), may hold values from -0.21875 to 0.21875
Outputs:
- pipe_ends: float32 [2, 2, 4096, 1024], P('section', None, 'dp')
- grad_norm_in: float32 [2, 1024], P('section', ('dp', 'tensor'))
- grad_query: float32 [2, 1024, 512], P('section', 'dp', 'tensor')
- grad_key: float32 [2, 1024, 512], P('section', 'dp', 'tensor')
- grad_value: float32 [2, 1024, 1024], P('section', 'dp', 'tensor')
- grad_out_gate: float32 [2, 1024, 1024], P('section', 'dp', 'tensor')
- grad_rank_down: float32 [2, 1024, 16], P('section', ('dp', 'tensor'))
- grad_rank_up: float32 [2, 16, 512], P('section', 'dp', 'tensor')
- grad_rank_bias: float32 [2, 512], P('section', ('dp', 'tensor'))
- grad_head_gain: float32 [2, 256], P('section', ('dp', 'tensor'))
- grad_out: float32 [2, 1024, 1024], P('section', 'tensor', 'dp')
- grad_norm_mid: float32 [2, 1024], P('section', ('dp', 'tensor'))
- grad_gate: float32 [2, 1024, 2816], P('section', 'dp', 'tensor')
- grad_up: float32 [2, 1024, 2816], P('section', 'dp', 'tensor')
- grad_down: float32 [2, 2816, 1024], P('section', 'tensor', 'dp')
The draws below stay inside these ranges and needn't reach their ends.
Inputs may be any that keep to these rules, and one draw needn't show every extreme that they name: `doc_lengths`: each row holds the lengths of 4 documents that fill one device's 256 tokens of one micro-batch exactly; the longest of every row is exactly 128.
All inputs are finite; a program needn't handle non-finite values.
Results may differ from the reference program's by a relative error of at most 0.03.
Values may be sent and summed in bfloat16 or wider, within the bound.
A program may use at most 192 MiB of HBM per device.

```python
import math
import jax
import jax.numpy as jnp
import numpy as np
from jax import lax

D = 1024
KD = 512
VD = 1024
GR = 16
FF = 2816
CH = 64
MICRO = 2
SEQS = 4
TOK_DEV = 256
HK = 128
HV = 256
LONGEST = 128
TOKENS = 4096
N_SECTION = 2
N_DP = 16


def steps_of(rng, dims, pieces, smallest, high):
    def one(position, blocks):
        draws = jax.random.uniform(jax.random.fold_in(jax.random.fold_in(rng, 6), position), (blocks,), jnp.float32, smallest / len(pieces), high / len(pieces))
        return jnp.repeat(jnp.exp(draws), dims[position] // blocks).reshape((-1,) + (1,) * (len(dims) - position - 1))

    factor_of = one(*pieces[0])
    for cut in pieces[1:]:
        factor_of = factor_of * one(*cut)
    return factor_of


def length_profile(count, total, limit, skew):
    portions = [(1 << 20) // math.isqrt(grade ** skew) + 1 for grade in range(2, count + 1)]
    rest, counts = total - limit - (count - 1), [1] * (count - 1)
    while rest > 0:
        free = [i for i in range(count - 1) if counts[i] < limit]
        mass, budget = sum([portions[i] for i in free]), rest
        for i in free:
            addition = min(limit - counts[i], max(1, budget * portions[i] // mass), rest)
            counts[i] = counts[i] + addition
            rest = rest - addition
    return np.array([limit] + counts)


def uneven_parts(key, amount, total, most, slope):
    if amount == 2:
        one = jax.random.randint(key, (), max(1, total - most), min(most, total - 1) + 1)
        return jnp.stack([one, total - one])
    sizes = jnp.asarray(length_profile(amount, total, most, slope), jnp.int32)
    twos = (amount - 1) // 2
    source_of, receiver = sizes[1:1 + 2 * twos:2], sizes[2:2 + 2 * twos:2]
    slack = jnp.minimum(source_of - 1, most - receiver)
    shifted = jax.random.randint(jax.random.fold_in(key, 1), (twos,), 0, 1 << 20) % (slack + 1)
    sizes = sizes.at[1:1 + 2 * twos:2].set(source_of - shifted).at[2:2 + 2 * twos:2].set(receiver + shifted)
    return sizes[jax.random.permutation(jax.random.fold_in(key, 2), amount)]


def normal_values(own_key, dims, spread, most, pieces=(), kind=jnp.bfloat16):
    result = spread * jax.random.normal(own_key, dims, jnp.float32)
    if pieces:
        result = result * steps_of(own_key, dims, pieces, -0.22, 0.18)
    return jnp.clip(result, -most, most).astype(kind)


def setup_inputs(seed: int = 0) -> dict:
    arg_keys = jax.random.split(jax.random.key(seed), 17)
    return {
        "pipe_in": normal_values(arg_keys[0], (N_SECTION, MICRO, TOKENS, D), 1.0, 6.0, ((0, 2), (2, 16))),
        "doc_lengths": jax.vmap(lambda own: uneven_parts(own, SEQS, TOK_DEV, LONGEST, 2))(jax.random.split(arg_keys[1], (N_DP * MICRO))).reshape((N_DP * MICRO, SEQS)).astype(jnp.int32),
        "norm_in": jnp.clip(1.0 + 0.1 * jax.random.normal(arg_keys[2], (N_SECTION, D), jnp.float32), 0.5, 1.5).astype(jnp.bfloat16),
        "w_query": normal_values(arg_keys[3], (N_SECTION, D, KD), D ** -0.5, 0.1875, ((0, 2), (1, 16), (2, 4))),
        "w_key": normal_values(arg_keys[4], (N_SECTION, D, KD), D ** -0.5, 0.1875, ((0, 2), (1, 16), (2, 4))),
        "w_value": normal_values(arg_keys[5], (N_SECTION, D, VD), D ** -0.5, 0.1875, ((0, 2), (1, 16), (2, 4))),
        "w_out_gate": normal_values(arg_keys[6], (N_SECTION, D, VD), D ** -0.5, 0.1875, ((0, 2), (1, 16), (2, 4))),
        "w_rank_down": normal_values(arg_keys[7], (N_SECTION, D, GR), D ** -0.5, 0.1875, ((0, 2), (1, 64))),
        "w_rank_up": normal_values(arg_keys[8], (N_SECTION, GR, KD), GR ** -0.5, 1.5, ((0, 2), (1, 16), (2, 4))),
        "rank_bias": jnp.clip(-2.0 + 6.0 * jax.random.uniform(arg_keys[9], (N_SECTION, KD), jnp.float32) ** steps_of(arg_keys[9], (N_SECTION, KD), ((0, 2), (1, 64)), -0.2, 0.2), -2.0, 4.0).astype(jnp.bfloat16),
        "head_gain": jnp.clip(1.0 + 0.1 * jax.random.normal(arg_keys[10], (N_SECTION, HV), jnp.float32), 0.5, 1.5).astype(jnp.bfloat16),
        "w_out": normal_values(arg_keys[11], (N_SECTION, VD, D), (VD // 4) ** -0.5, 0.375, ((0, 2), (1, 4), (2, 16))),
        "norm_mid": jnp.clip(1.0 + 0.1 * jax.random.normal(arg_keys[12], (N_SECTION, D), jnp.float32), 0.5, 1.5).astype(jnp.bfloat16),
        "w_gate": normal_values(arg_keys[13], (N_SECTION, D, FF), D ** -0.5, 0.1875, ((0, 2), (1, 16), (2, 4))),
        "w_up": normal_values(arg_keys[14], (N_SECTION, D, FF), D ** -0.5, 0.1875, ((0, 2), (1, 16), (2, 4))),
        "w_down": normal_values(arg_keys[15], (N_SECTION, FF, D), (FF // 4) ** -0.5, 0.21875, ((0, 2), (1, 4), (2, 16))),
    }


@jax.custom_vjp
def low(v):
    return lax.optimization_barrier(v.astype(jnp.bfloat16)).astype(jnp.float32)

@jax.custom_vjp
def low_back(v):
    return v

def low_keep(v):
    return (low(v), None)

def low_pass(kept, grad):
    return (grad,)

def back_keep(v):
    return (v, None)

def back_low(kept, grad):
    return (low(grad),)
low.defvjp(low_keep, low_pass)
low_back.defvjp(back_keep, back_low)
epsilon = 1e-06
head_floor = 1.0

def matmul(left, right):
    return jnp.dot(left, right, precision=lax.Precision.HIGHEST, preferred_element_type=jnp.float32)

def rms_scale(values):
    return lax.rsqrt(lax.optimization_barrier(jnp.mean(values * values, axis=-1, keepdims=True)) + epsilon)

def segment_ids(lengths, count):
    bounds = jnp.cumsum(lengths).astype(jnp.int32)
    places = jnp.arange(count, dtype=jnp.int32)
    return lax.optimization_barrier(jnp.sum((bounds[None, :] <= places[:, None]).astype(jnp.int32), axis=1)).astype(jnp.int32)

def mixer(queries, keys_in, values_in, decay_pre, gates, head_scale, segments):
    token_count = queries.shape[0]
    head_count = queries.shape[1] // HK
    block_count = token_count // CH
    log_decay = jax.nn.log_sigmoid(decay_pre) / 16.0
    query_blocks = (queries * HK ** (-0.5)).reshape(block_count, CH, head_count, HK)
    key_blocks = keys_in.reshape(block_count, CH, head_count, HK)
    decay_blocks = log_decay.reshape(block_count, CH, head_count, HK)
    value_blocks = values_in.reshape(block_count, CH, head_count, HV)
    segment_blocks = segments.reshape(block_count, CH)
    causal = jnp.arange(CH)[:, None] >= jnp.arange(CH)[None, :]

    def advance(carry, block):
        state, previous = carry
        query_blk, key_blk, decay_blk, value_blk, segment_blk = block
        cumulative = jnp.cumsum(decay_blk, axis=0)
        query_dec = query_blk * jnp.exp(cumulative)
        key_dec = key_blk * jnp.exp(-cumulative)
        scores = jnp.einsum('ihc,jhc->hij', query_dec, key_dec, precision=lax.Precision.HIGHEST)
        allowed = jnp.logical_and(causal, segment_blk[:, None] == segment_blk[None, :]).astype(jnp.float32)
        within = jnp.einsum('hij,jhv->ihv', scores * allowed[None], value_blk, precision=lax.Precision.HIGHEST)
        carried = (segment_blk == previous).astype(jnp.float32)
        across = jnp.einsum('ihc,hcv->ihv', query_dec, state, precision=lax.Precision.HIGHEST) * carried[:, None, None]
        last_segment = segment_blk[CH - 1]
        last_cumulative = cumulative[CH - 1]
        in_tail = (segment_blk == last_segment).astype(jnp.float32)
        key_tail = key_blk * jnp.exp(last_cumulative[None] - cumulative) * in_tail[:, None, None]
        retain = (last_segment == previous).astype(jnp.float32)
        state = retain * jnp.exp(last_cumulative)[:, :, None] * state + jnp.einsum('jhc,jhv->hcv', key_tail, value_blk, precision=lax.Precision.HIGHEST)
        return ((state, last_segment), within + across)
    start = (jnp.zeros((head_count, HK, HV), jnp.float32), jnp.array(-1, jnp.int32))
    finish, outputs = lax.scan(jax.checkpoint(advance), start, (query_blocks, key_blocks, decay_blocks, value_blocks, segment_blocks))
    outputs = outputs.reshape(token_count, head_count, HV)
    head_norm = lax.rsqrt(lax.optimization_barrier(jnp.mean(outputs * outputs, axis=-1, keepdims=True)) + head_floor)
    normed = outputs * head_norm * head_scale
    gate_heads = gates.reshape(token_count, head_count, HV)
    return (normed * gate_heads * jax.nn.sigmoid(gate_heads)).reshape(token_count, head_count * HV)

def layer(inputs, weights, segments):
    norm_in, w_query, w_key, w_value, w_out_gate, w_rank_down, w_rank_up, rank_bias, head_gain, w_out, norm_mid, w_gate, w_up, w_down = weights
    normed = low(inputs * rms_scale(inputs) * norm_in)
    queries = low_back(matmul(normed, w_query))
    keys_in = low_back(matmul(normed, w_key))
    values_in = low_back(matmul(normed, w_value))
    gates = low_back(matmul(normed, w_out_gate))
    rank_act = low_back(low(matmul(normed, w_rank_down)))
    decay_pre = low_back(matmul(rank_act, w_rank_up) + rank_bias)
    mixed = mixer(queries, keys_in, values_in, decay_pre, gates, head_gain, segments)
    attended = low_back(matmul(low(mixed), w_out))
    hidden = inputs + attended
    normed_mid = low(hidden * rms_scale(hidden) * norm_mid)
    gate_act = low_back(matmul(normed_mid, w_gate))
    up_act = low_back(matmul(normed_mid, w_up))
    inner = low(jax.nn.silu(gate_act) * up_act)
    return hidden + low_back(matmul(inner, w_down))

def reference(pipe_in, doc_lengths, norm_in, w_query, w_key, w_value, w_out_gate, w_rank_down, w_rank_up, rank_bias, head_gain, w_out, norm_mid, w_gate, w_up, w_down):
    weights = tuple((weight.astype(jnp.float32) for weight in (norm_in, w_query, w_key, w_value, w_out_gate, w_rank_down, w_rank_up, rank_bias, head_gain, w_out, norm_mid, w_gate, w_up, w_down)))
    block_inputs = pipe_in[0].astype(jnp.float32).reshape(MICRO * N_DP, TOK_DEV, D)
    block_cotangent = pipe_in[1].astype(jnp.float32).reshape(MICRO * N_DP, TOK_DEV, D)
    ordered = doc_lengths.reshape(N_DP, MICRO, SEQS).transpose(1, 0, 2).reshape(MICRO * N_DP, SEQS)
    segments = jax.vmap(lambda row: segment_ids(row, TOK_DEV))(ordered)

    def forward(inputs_all, layer_weights):

        def one_block(pair):
            block_in, block_segments = pair
            first = layer(block_in, tuple((weight[0] for weight in layer_weights)), block_segments)
            passed = low_back(low(first))
            return layer(passed, tuple((weight[1] for weight in layer_weights)), block_segments)
        return lax.map(one_block, (inputs_all, segments))
    outputs, pullback = jax.vjp(forward, block_inputs, weights)
    grad_inputs, grad_weights = pullback(block_cotangent)
    ends = jnp.stack([grad_inputs.reshape(MICRO, TOKENS, D), outputs.reshape(MICRO, TOKENS, D)]).astype(jnp.float32)
    return (ends, grad_weights[0], grad_weights[1], grad_weights[2], grad_weights[3], grad_weights[4], grad_weights[5], grad_weights[6], grad_weights[7], grad_weights[8], grad_weights[9], grad_weights[10], grad_weights[11], grad_weights[12], grad_weights[13])
```

```python
import functools

import jax
import jax.numpy as jnp
from jax import lax
from jax.experimental import pallas as pl
from jax.experimental.pallas import tpu as pltpu
from jax.sharding import PartitionSpec as P

CH = 64
HK = 128
HV = 256
TOK = 256
BLOCKS = TOK // CH
FFD = 704
FFM = 640
QKVG = (0, 768)
OUT = (768, 256)
GU = (1024, 1408)
DOWN = (2432, 768)
WIDE = 3200
epsilon = 1e-06
head_floor = 1.0
MESH = pl.DeviceIdType.MESH
f32 = jnp.float32
bf16 = jnp.bfloat16

GATHER = (
    (0, 384, 0),
    (384, 384, 1),
    (768, 768, 0),
    (1536, 896, 1),
    (2432, 384, 0),
    (2816, 384, 1),
)
SCATTER = (
    (1024, 1408, 0),
    (2432, 768, 1),
    (768, 256, 0),
    (0, 384, 0),
    (384, 384, 1),
)


def dot(a, b):
    return lax.dot_general(a, b, (((1,), (0,)), ((), ())), preferred_element_type=f32)


def dot_back(a, b):
    return lax.dot_general(a, b, (((1,), (1,)), ((), ())), preferred_element_type=f32)


def dot_grad(a, b):
    return lax.dot_general(a, b, (((0,), (0,)), ((), ())), preferred_element_type=f32)


def low(a):
    return a.astype(bf16)


def wide(a):
    return a.astype(f32)


def rms_scale(v):
    return lax.rsqrt(jnp.mean(v * v, axis=-1, keepdims=True) + epsilon)


def kernel(
    X,
    Z,
    T,
    own,
    shard,
    norm_in,
    norm_mid,
    gain,
    bias,
    rank_down,
    rank_up,
    allowed,
    aux,
    ends,
    og,
    sg,
    W,
    xbuf,
    x1,
    normed,
    nm,
    qkvg,
    cum,
    slope,
    amat,
    states,
    attn,
    mixed,
    hid,
    gu,
    inner,
    rank,
    dh,
    dy0,
    res,
    res_in,
    pbuf,
    rbuf,
    G,
    GA,
    GB,
    GC,
    Q,
    RF,
    dqkvg,
    dmix,
    a_sem,
    gs,
    gr,
    ys,
    yr,
    ss,
    sr,
    e_sem,
):
    c = lax.axis_index("section")
    d = lax.axis_index("dp")
    t = lax.axis_index("tensor")
    x, z = d // Z, d % Z
    o = 1 - c
    D = own.shape[-1]
    R = shard.shape[0]
    H = R // 2
    TL = TOK // T
    size = (X, Z)
    here = (x, z)

    def dp_peer(axis, k):
        if axis == 0:
            return ((x + k) % X) * Z + z
        return x * Z + (z + k) % Z

    def remote(src, dst, s, r, **device):
        return pltpu.make_async_remote_copy(
            src_ref=src, dst_ref=dst, send_sem=s, recv_sem=r, device_id=device, device_id_type=MESH
        )

    barrier = pltpu.get_barrier_semaphore()
    for k in range(1, X):
        pl.semaphore_signal(barrier, inc=1, device_id={"dp": dp_peer(0, k)}, device_id_type=MESH)
    for k in range(1, Z):
        pl.semaphore_signal(barrier, inc=1, device_id={"dp": dp_peer(1, k)}, device_id_type=MESH)
    for k in range(1, T):
        pl.semaphore_signal(barrier, inc=1, device_id={"tensor": (t + k) % T}, device_id_type=MESH)
    pl.semaphore_signal(barrier, inc=1, device_id={"section": o}, device_id_type=MESH)
    pl.semaphore_wait(barrier, X + Z + T - 2)

    half = lambda h: pl.ds(pl.multiple_of(h * H, H), H)
    swap_w = remote(shard.at[half(o)], W.at[c, x, z, o], a_sem.at[0], a_sem.at[1], section=o)
    swap_x = remote(own.at[o], xbuf.at[c], a_sem.at[2], a_sem.at[3], section=o)
    keep_w = pltpu.make_async_copy(shard.at[half(c)], W.at[c, x, z, c], a_sem.at[4])
    keep_x = pltpu.make_async_copy(own.at[c], xbuf.at[c], a_sem.at[5])
    swap_w.start()
    swap_x.start()
    keep_w.start()
    keep_x.start()
    got_w = remote(shard.at[half(o)], W.at[o, x, z, c], a_sem.at[0], a_sem.at[1], section=o)
    got_x = remote(own.at[o], xbuf.at[o], a_sem.at[2], a_sem.at[3], section=o)

    def w_first(l, j, k):
        c0, n, axis = GATHER[j]
        at = W.at[l, x, z, c, :, pl.ds(c0, n)]
        if axis == 0:
            into = W.at[l, (x - k) % X, z, c, :, pl.ds(c0, n)]
        else:
            into = W.at[l, x, (z - k) % Z, c, :, pl.ds(c0, n)]
        s, r = gs.at[l, j, k - 1], gr.at[l, j, k - 1]
        return remote(at, at, s, r, dp=dp_peer(axis, k)), remote(into, into, s, r, dp=dp_peer(axis, k))

    def w_second(l, j, k):
        c0, n, axis = GATHER[j]
        cols = pl.ds(c0, n)
        if axis == 0:
            at, into = W.at[l, :, z, c, :, cols], W.at[l, :, (z - k) % Z, c, :, cols]
        else:
            at, into = W.at[l, x, :, c, :, cols], W.at[l, (x - k) % X, :, c, :, cols]
        s, r = gs.at[l, j, 2 + k], gr.at[l, j, 2 + k]
        return remote(at, at, s, r, dp=dp_peer(1 - axis, k)), remote(
            into, into, s, r, dp=dp_peer(1 - axis, k)
        )

    def w_third(l, j):
        c0, n, _ = GATHER[j]
        cols = pl.ds(c0, n)
        at, into = W.at[l, :, :, c, :, cols], W.at[l, :, :, o, :, cols]
        s, r = gs.at[l, j, 6], gr.at[l, j, 6]
        return remote(at, at, s, r, section=o), remote(into, into, s, r, section=o)

    def gather_first(l, j):
        for k in range(1, size[GATHER[j][2]]):
            w_first(l, j, k)[0].start()

    def gather_second(l, j):
        axis = GATHER[j][2]
        for k in range(1, size[axis]):
            w_first(l, j, k)[1].wait_recv()
        for k in range(1, size[1 - axis]):
            w_second(l, j, k)[0].start()

    def gather_third(l, j):
        axis = GATHER[j][2]
        for k in range(1, size[1 - axis]):
            w_second(l, j, k)[1].wait_recv()
        w_third(l, j)[0].start()

    arrived = set()

    def weight(l, part):
        c0, n = part
        for j, (g0, gn, _) in enumerate(GATHER):
            if g0 < c0 + n and c0 < g0 + gn and (l, j) not in arrived:
                arrived.add((l, j))
                w_third(l, j)[1].wait_recv()
        return W[l, :, :, :, :, c0 : c0 + n].reshape(D, n)

    def rows(p):
        return pl.ds(pl.multiple_of(p * TL, TL), TL)

    def sum_copy(i, k):
        peer = (t + k) % T
        return remote(
            pbuf.at[i // 2 % 2, rows(peer)], rbuf.at[i // 2 % 2, k - 1], ys.at[i, k - 1], yr.at[i, k - 1], tensor=peer
        )

    def sum_start(i, part):
        pbuf[i // 2 % 2] = low(part)
        for k in range(1, T):
            sum_copy(i, k).start()

    def sum_wait(i):
        total = wide(pbuf[i // 2 % 2, rows(t)])
        for k in range(1, T):
            sum_copy(i, k).wait_recv()
            total = total + wide(rbuf[i // 2 % 2, k - 1])
        for k in range(1, T):
            sum_copy(i, k).wait_send()
        return total

    def share_copy(i, ref, k):
        peer = (t + k) % T
        s, r = ys.at[i, k - 1], yr.at[i, k - 1]
        mine, into = ref.at[rows(t)], ref.at[rows((t - k) % T)]
        return remote(mine, mine, s, r, tensor=peer), remote(into, into, s, r, tensor=peer)

    def share_start(i, ref, value):
        ref[rows(t)] = low(value)
        for k in range(1, T):
            share_copy(i, ref, k)[0].start()

    def share_wait(i, ref):
        for k in range(1, T):
            share_copy(i, ref, k)[1].wait_recv()
        for k in range(1, T):
            share_copy(i, ref, k)[0].wait_send()

    def s_swap(l, j):
        c0, n, _ = SCATTER[j]
        cols = pl.ds(c0, n)
        return remote(
            G.at[:, :, o, :, cols], GA.at[l, :, :, :, cols], ss.at[l, j, 0], sr.at[l, j, 0], section=o
        )

    def s_first(l, j, k):
        c0, n, axis = SCATTER[j]
        cols = pl.ds(c0, n)
        src = G.at[(x + k) % X, :, c, :, cols] if axis == 0 else G.at[:, (z + k) % Z, c, :, cols]
        return remote(
            src, GB.at[l, k - 1, :, :, cols], ss.at[l, j, k], sr.at[l, j, k], dp=dp_peer(axis, k)
        )

    def s_second(l, j, k):
        c0, n, axis = SCATTER[j]
        cols = pl.ds(c0, n)
        place = (here[1 - axis] + k) % size[1 - axis]
        return remote(
            Q.at[l, place, :, cols],
            GC.at[l, k - 1, :, cols],
            ss.at[l, j, 3 + k],
            sr.at[l, j, 3 + k],
            dp=dp_peer(1 - axis, k),
        )

    def scatter_swap(l, j):
        s_swap(l, j).start()

    def scatter_first(l, j):
        c0, n, axis = SCATTER[j]
        s_swap(l, j).wait()
        for a in range(X):
            G[a, :, c, :, c0 : c0 + n] = low(
                wide(G[a, :, c, :, c0 : c0 + n]) + wide(GA[l, a, :, :, c0 : c0 + n])
            )
        for k in range(1, size[axis]):
            s_first(l, j, k).start()

    def scatter_second(l, j):
        c0, n, axis = SCATTER[j]
        cols = slice(c0, c0 + n)
        total = wide(G[x, :, c, :, cols] if axis == 0 else G[:, z, c, :, cols])
        for k in range(1, size[axis]):
            s_first(l, j, k).wait()
            total = total + wide(GB[l, k - 1, :, :, cols])
        Q[l, :, :, cols] = low(total)
        for k in range(1, size[1 - axis]):
            s_second(l, j, k).start()

    def scatter_third(l, j):
        c0, n, axis = SCATTER[j]
        cols = slice(c0, c0 + n)
        total = wide(Q[l, here[1 - axis], :, cols])
        for k in range(1, size[1 - axis]):
            s_second(l, j, k).wait()
            total = total + wide(GC[l, k - 1, :, cols])
        RF[l, :, cols] = total

    scale = HK**-0.5
    sub = lambda v, n: v[n * CH : (n + 1) * CH]

    def mixer_forward(l):
        qk = qkvg[l]
        b = cum[l]
        qd = low(qk[:, 0:128] * scale * jnp.exp(b))
        kd = low(qk[:, 128:256] * jnp.exp(-b))
        v = low(qk[:, 256:512])
        scores = low(jnp.where(allowed[...] > 0.0, dot_back(qd, kd), 0.0))
        amat[l] = scores
        within = dot(scores, v)
        out = [sub(within, 0)]
        state = None
        for n in range(BLOCKS - 1):
            bn = sub(b, n)
            last = bn[CH - 1 : CH]
            tail = sub(aux[...], n)[:, 1:2]
            kt = low(sub(qk, n)[:, 128:256] * jnp.exp(last - bn) * tail)
            fresh = dot_grad(sub(v, n), kt)
            if state is None:
                state = fresh
            else:
                state = aux[n * CH : n * CH + 1, 2:3] * jnp.exp(last) * state + fresh
            states[l, n] = state
            carried = sub(aux[...], n + 1)[:, 0:1]
            out.append(sub(within, n + 1) + carried * dot_back(sub(qd, n + 1), low(state)))
        attn[l] = jnp.concatenate(out, axis=0)

    def running(v, upper):
        row = lax.broadcasted_iota(jnp.int32, (TOK, TOK), 0)
        col = lax.broadcasted_iota(jnp.int32, (TOK, TOK), 1)
        order = (row <= col) if upper else (row >= col)
        tri = jnp.where(jnp.logical_and(order, row // CH == col // CH), 1.0, 0.0).astype(bf16)
        first = low(v)
        rest = v - wide(first)
        second = low(rest)
        third = low(rest - wide(second))
        return dot(tri, first) + (dot(tri, second) + dot(tri, third))

    def forward(l, i, x_ref, out_ref, hooks):
        xin = wide(x_ref[...])
        normed[l] = low(xin * rms_scale(xin) * norm_in[l])
        hooks[0]()
        nrm = normed[l]
        qkvg[l] = dot(nrm, weight(l, QKVG))
        rank[l] = low(dot(nrm, rank_down[l]))
        pre = dot(rank[l], rank_up[l]) + bias[l]
        soft = jnp.log1p(jnp.exp(-jnp.abs(pre)))
        slope[l] = jax.nn.sigmoid(-pre) / 16.0
        cum[l] = running((jnp.minimum(pre, 0.0) - soft) / 16.0, False)
        mixer_forward(l)
        at = attn[l]
        g = qkvg[l, :, 512:768]
        head = lax.rsqrt(jnp.mean(at * at, axis=-1, keepdims=True) + head_floor)
        mixed[l] = low(at * head * gain[l] * g * jax.nn.sigmoid(g))
        sum_start(i, dot_back(mixed[l], weight(l, OUT)))
        hooks[1]()
        hidden = wide(x_ref[rows(t)]) + sum_wait(i)
        hid[l] = hidden
        share_start(i + 1, nm.at[l], hidden * rms_scale(hidden) * norm_mid[l])
        hooks[2]()
        w_gu = weight(l, GU)
        share_wait(i + 1, nm.at[l])
        acts = dot(nm[l], w_gu)
        gu[l] = acts
        first = jax.nn.silu(acts[:, :FFM]) * acts[:, FFM : 2 * FFM]
        both = acts[:, 2 * FFM :]
        lane = lax.broadcasted_iota(jnp.int32, (TOK, 128), 1)
        last = jnp.where(lane < 64, jax.nn.silu(both) * pltpu.roll(both, 64, 1), 0.0)
        inner[l, :, :FFM] = low(first)
        inner[l, :, FFM:] = low(last)
        sum_start(i + 2, dot_back(inner[l], weight(l, DOWN)))
        hooks[3]()
        y = hid[l] + sum_wait(i + 2)
        share_start(i + 3, out_ref, y)

    def silu_parts(v):
        sig = jax.nn.sigmoid(v)
        return v * sig, sig * (1.0 + v * (1.0 - sig))

    def put(part, left, right):
        c0, n = part
        step = D // X
        for a in range(X):
            G[a, :, :, :, c0 : c0 + n] = low(
                dot_grad(left[:, a * step : (a + 1) * step], right)
            ).reshape(Z, 2, H, n)

    def mixer_backward(l):
        at = attn[l]
        g = qkvg[l, :, 512:768]
        head = lax.rsqrt(jnp.mean(at * at, axis=-1, keepdims=True) + head_floor)
        unit = at * head
        act, act_slope = silu_parts(g)
        dm = dmix[...]
        dqkvg[:, 512:768] = low(dm * unit * gain[l] * act_slope)
        du = dm * act
        d_gain = jnp.sum(du * unit, axis=0, keepdims=True)
        w = du * gain[l]
        do = low(head * (w - unit * jnp.mean(w * unit, axis=-1, keepdims=True)))
        q, k = qkvg[l, :, 0:128], qkvg[l, :, 128:256]
        b = cum[l]
        grow, shrink = jnp.exp(b), jnp.exp(-b)
        qd = low(q * scale * grow)
        kd = low(k * shrink)
        v = low(qkvg[l, :, 256:512])
        d_scores = low(jnp.where(allowed[...] > 0.0, dot_back(do, v), 0.0))
        d_qd = dot(d_scores, kd)
        d_kd = dot_grad(d_scores, qd)
        d_v = dot_grad(amat[l], do)
        d_b = wide(qd) * d_qd - wide(kd) * d_kd
        d_k = d_kd * shrink
        out_q, out_k, out_v, out_b = [None] * BLOCKS, [None] * BLOCKS, [None] * BLOCKS, [None] * BLOCKS
        d_state = None
        for n in reversed(range(BLOCKS)):
            dq_n, dk_n, dv_n, db_n = sub(d_qd, n), sub(d_k, n), sub(d_v, n), sub(d_b, n)
            if n < BLOCKS - 1:
                bn = sub(b, n)
                last = bn[CH - 1 : CH]
                fade = jnp.exp(last - bn) * sub(aux[...], n)[:, 1:2]
                kt = low(sub(k, n) * fade)
                d_low = low(d_state)
                d_kt = dot(sub(v, n), d_low)
                dv_n = dv_n + dot_back(kt, d_low)
                dk_n = dk_n + d_kt * fade
                moved = wide(kt) * d_kt
                db_n = db_n - moved
                d_last = jnp.sum(moved, axis=0, keepdims=True)
                if n > 0:
                    keep = aux[n * CH : n * CH + 1, 2:3] * jnp.exp(last)
                    d_last = d_last + keep * jnp.sum(
                        states[l, n - 1] * d_state, axis=0, keepdims=True
                    )
                place = lax.broadcasted_iota(jnp.int32, (CH, HK), 0)
                db_n = db_n + jnp.where(place == CH - 1, d_last, 0.0)
            if n > 0:
                do_n = low(wide(sub(do, n)) * sub(aux[...], n)[:, 0:1])
                d_across = dot(do_n, low(states[l, n - 1]))
                dq_n = dq_n + d_across
                db_n = db_n + wide(sub(qd, n)) * d_across
                fresh = dot_grad(do_n, sub(qd, n))
                d_state = fresh if n == BLOCKS - 1 else keep * d_state + fresh
            out_q[n], out_k[n], out_v[n], out_b[n] = dq_n, dk_n, dv_n, db_n
        dqkvg[:, 0:128] = low(jnp.concatenate(out_q, axis=0) * scale * grow)
        dqkvg[:, 128:256] = low(jnp.concatenate(out_k, axis=0))
        dqkvg[:, 256:512] = low(jnp.concatenate(out_v, axis=0))
        d_decay = running(jnp.concatenate(out_b, axis=0), True)
        return low(d_decay * slope[l]), d_gain

    def backward(l, i, x_ref, dy_ref, out_ref, hooks):
        dy = dy_ref[...]
        d_inner = dot(dy, weight(l, DOWN))
        gate, up, both = gu[l, :, :FFM], gu[l, :, FFM : 2 * FFM], gu[l, :, 2 * FFM :]
        act, act_slope = silu_parts(gate)
        act_b, slope_b = silu_parts(both)
        rest = d_inner[:, FFM:]
        mix_b = rest * pltpu.roll(both, 64, 1) * slope_b + pltpu.roll(rest * act_b, 64, 1)
        d_gu = jnp.concatenate(
            [low(d_inner[:, :FFM] * up * act_slope), low(d_inner[:, :FFM] * act), low(mix_b)], axis=1
        )
        sum_start(i, dot_back(d_gu, weight(l, GU)))
        put(DOWN, dy, inner[l])
        scatter_swap(l, 1)
        put(GU, nm[l], d_gu)
        scatter_swap(l, 0)
        hooks[0]()
        d_mid = sum_wait(i)
        hidden = hid[l]
        scale_mid = rms_scale(hidden)
        unit = hidden * scale_mid
        sg[l, 17:18, :] = jnp.sum(d_mid * unit, axis=0, keepdims=True)
        scaled = d_mid * norm_mid[l]
        d_hidden = wide(dy_ref[rows(t)]) + scale_mid * (
            scaled - unit * jnp.mean(scaled * unit, axis=-1, keepdims=True)
        )
        hid[l] = d_hidden
        share_start(i + 1, dh.at[l], d_hidden)
        hooks[1]()
        share_wait(i + 1, dh.at[l])
        dmix[...] = dot(dh[l], weight(l, OUT))
        d_pre, d_gain = mixer_backward(l)
        d_rank = low(dot_back(d_pre, rank_up[l]))
        sum_start(i + 2, dot_back(dqkvg[...], weight(l, QKVG)) + dot_back(d_rank, rank_down[l]))
        hooks[2]()
        put(OUT, dh[l], mixed[l])
        scatter_swap(l, 2)
        put(QKVG, normed[l], dqkvg[...])
        scatter_swap(l, 3)
        scatter_swap(l, 4)
        sg[l, 0:16, :] = dot_grad(d_rank, normed[l])[0:16]
        sg[l, 18:19, 0:HV] = d_gain
        sg[l, 19:20, 0:HK] = jnp.sum(wide(d_pre), axis=0, keepdims=True)
        sg[l, 24:40, 0:HK] = dot_grad(rank[l], d_pre)[0:16]
        hooks[3]()
        d_normed = sum_wait(i + 2)
        xin = wide(x_ref[rows(t)])
        scale_in = rms_scale(xin)
        unit = xin * scale_in
        sg[l, 16:17, :] = jnp.sum(d_normed * unit, axis=0, keepdims=True)
        scaled = d_normed * norm_in[l]
        dx = hid[l] + scale_in * (scaled - unit * jnp.mean(scaled * unit, axis=-1, keepdims=True))
        share_start(i + 3, out_ref, dx)

    def nothing():
        pass

    count = len(GATHER)

    def first_weights():
        got_w.wait_recv()
        keep_w.wait()
        for j in range(count):
            gather_first(0, j)
        for j in range(count):
            gather_second(0, j)
        for j in range(count):
            gather_third(0, j)
        for j in range(count):
            gather_first(1, j)

    def each(step, l, which):
        def run():
            for j in which:
                step(l, j)

        return run

    sg[...] = jnp.zeros_like(sg)
    got_x.wait_recv()
    keep_x.wait()
    everything = range(count)
    forward(
        0,
        0,
        xbuf.at[0],
        x1,
        (first_weights, each(gather_second, 1, everything), nothing, each(gather_third, 1, everything)),
    )
    share_wait(3, x1)
    forward(1, 4, x1, res.at[1], (nothing, nothing, nothing, nothing))

    def send_y():
        share_wait(7, res.at[1])

    ff, mix = (0, 1), (2, 3, 4)
    backward(
        1,
        8,
        x1,
        xbuf.at[1],
        dy0,
        (
            send_y,
            each(scatter_first, 1, ff),
            each(scatter_second, 1, ff),
            each(scatter_third, 1, ff),
        ),
    )
    each(scatter_first, 1, mix)()
    share_wait(11, dy0)

    def in_second():
        each(scatter_first, 0, ff)()
        each(scatter_third, 1, mix)()

    backward(
        0,
        12,
        xbuf.at[0],
        dy0,
        res.at[0],
        (each(scatter_second, 1, mix), in_second, each(scatter_second, 0, ff), each(scatter_third, 0, ff)),
    )
    each(scatter_first, 0, mix)()
    share_wait(15, res.at[0])
    give_end = remote(res.at[o], res_in, e_sem.at[0], e_sem.at[1], section=o)
    give_end.start()
    each(scatter_second, 0, mix)()
    ends[c] = wide(res[c])
    each(scatter_third, 0, mix)()
    give_grad = remote(RF.at[o], og.at[c], e_sem.at[2], e_sem.at[3], section=o)
    got_grad = remote(RF.at[o], og.at[o], e_sem.at[2], e_sem.at[3], section=o)
    give_grad.start()
    og[c] = RF[c]
    give_end.wait_recv()
    ends[o] = wide(res_in[...])
    got_grad.wait_recv()
    give_end.wait_send()
    give_grad.wait_send()
    swap_w.wait_send()
    swap_x.wait_send()
    for l in range(2):
        for j, (_, _, axis) in enumerate(GATHER):
            for k in range(1, size[axis]):
                w_first(l, j, k)[0].wait_send()
            for k in range(1, size[1 - axis]):
                w_second(l, j, k)[0].wait_send()
            w_third(l, j)[0].wait_send()


def run_kernel(X, Z, T, D, R, operands):
    H = R // 2
    TL = TOK // T
    top = max(X, Z)
    scratch = [
        pltpu.VMEM((2, X, Z, 2, H, WIDE), bf16),
        pltpu.VMEM((2, TOK, D), bf16),
        pltpu.VMEM((TOK, D), bf16),
        pltpu.VMEM((2, TOK, D), bf16),
        pltpu.VMEM((2, TOK, D), bf16),
        pltpu.VMEM((2, TOK, 768), f32),
        pltpu.VMEM((2, TOK, HK), f32),
        pltpu.VMEM((2, TOK, HK), f32),
        pltpu.VMEM((2, TOK, TOK), bf16),
        pltpu.VMEM((2, BLOCKS - 1, HV, HK), f32),
        pltpu.VMEM((2, TOK, HV), f32),
        pltpu.VMEM((2, TOK, HV), bf16),
        pltpu.VMEM((2, TL, D), f32),
        pltpu.VMEM((2, TOK, GU[1]), f32),
        pltpu.VMEM((2, TOK, DOWN[1]), bf16),
        pltpu.VMEM((2, TOK, 128), bf16),
        pltpu.VMEM((2, TOK, D), bf16),
        pltpu.VMEM((TOK, D), bf16),
        pltpu.VMEM((2, TOK, D), bf16),
        pltpu.VMEM((TOK, D), bf16),
        pltpu.VMEM((2, TOK, D), bf16),
        pltpu.VMEM((2, T - 1, TL, D), bf16),
        pltpu.VMEM((X, Z, 2, H, WIDE), bf16),
        pltpu.VMEM((2, X, Z, H, WIDE), bf16),
        pltpu.VMEM((2, top - 1, top, H, WIDE), bf16),
        pltpu.VMEM((2, top - 1, H, WIDE), bf16),
        pltpu.VMEM((2, top, H, WIDE), bf16),
        pltpu.VMEM((2, H, WIDE), f32),
        pltpu.VMEM((TOK, 768), bf16),
        pltpu.VMEM((TOK, HV), f32),
        pltpu.SemaphoreType.DMA((6,)),
        pltpu.SemaphoreType.DMA((2, len(GATHER), 7)),
        pltpu.SemaphoreType.DMA((2, len(GATHER), 7)),
        pltpu.SemaphoreType.DMA((16, T - 1)),
        pltpu.SemaphoreType.DMA((16, T - 1)),
        pltpu.SemaphoreType.DMA((2, len(SCATTER), 7)),
        pltpu.SemaphoreType.DMA((2, len(SCATTER), 7)),
        pltpu.SemaphoreType.DMA((4,)),
    ]
    vmem = pl.BlockSpec(memory_space=pltpu.VMEM)
    return pl.pallas_call(
        functools.partial(kernel, X, Z, T),
        out_shape=(
            jax.ShapeDtypeStruct((2, TOK, D), f32),
            jax.ShapeDtypeStruct((2, H, WIDE), f32),
            jax.ShapeDtypeStruct((2, 40, D), f32),
        ),
        in_specs=[vmem] * len(operands),
        out_specs=(vmem,) * 3,
        scratch_shapes=scratch,
        compiler_params=pltpu.CompilerParams(
            collective_id=0, has_side_effects=True, vmem_limit_bytes=63 * 1024 * 1024
        ),
    )(*operands)


def mask_arrays(lengths):
    bounds = jnp.cumsum(lengths)
    places = jnp.arange(TOK, dtype=jnp.int32)
    seg = jnp.sum((bounds[None, :] <= places[:, None]).astype(jnp.int32), axis=1)
    by_block = seg.reshape(BLOCKS, CH)
    last = by_block[:, CH - 1]
    before = jnp.concatenate([jnp.full((1,), -1, jnp.int32), last[:-1]])
    carried = (by_block == before[:, None]).reshape(TOK).astype(f32)
    tail = (by_block == last[:, None]).reshape(TOK).astype(f32)
    retain = jnp.broadcast_to((last == before)[:, None], (BLOCKS, CH)).reshape(TOK).astype(f32)
    block = places // CH
    allowed = (
        (places[:, None] >= places[None, :])
        & (block[:, None] == block[None, :])
        & (seg[:, None] == seg[None, :])
    ).astype(f32)
    aux = jnp.pad(jnp.stack([carried, tail, retain], axis=1), ((0, 0), (0, 125)))
    return allowed, aux


def on_device(
    X,
    Z,
    pipe_in,
    doc_lengths,
    norm_in,
    w_query,
    w_key,
    w_value,
    w_out_gate,
    w_rank_down,
    w_rank_up,
    rank_bias,
    head_gain,
    w_out,
    norm_mid,
    w_gate,
    w_up,
    w_down,
):
    T = lax.axis_size("tensor")
    N = X * Z
    c = lax.axis_index("section")
    d = lax.axis_index("dp")
    t = lax.axis_index("tensor")
    R = w_query.shape[1]
    D = R * N
    shard = jnp.concatenate(
        [
            w_query[0],
            w_key[0],
            w_value[0],
            w_out_gate[0],
            w_out[0].T,
            w_gate[0, :, :FFM],
            w_up[0, :, :FFM],
            w_gate[0, :, FFM:],
            w_up[0, :, FFM:],
            w_down[0].T,
            jnp.zeros((R, 2 * FFM + 128 - 2 * FFD + DOWN[1] - FFD), bf16),
        ],
        axis=1,
    )
    mine = [norm_in[0], norm_mid[0], head_gain[0], rank_bias[0], w_rank_down[0].reshape(-1), w_rank_up[0, 0]]
    widths = [a.shape[0] for a in mine]
    smalls = lax.all_gather(jnp.concatenate(mine), ("section", "dp", "tensor"), axis=0, tiled=False)
    smalls = smalls.reshape(2, N, T, -1)
    parts, at = [], 0
    for w in widths:
        parts.append(smalls[..., at : at + w])
        at += w
    g_in = parts[0].reshape(2, 1, D).astype(f32)
    g_mid = parts[1].reshape(2, 1, D).astype(f32)
    g_head = parts[2].reshape(2, 1, HV).astype(f32)
    bias = lax.dynamic_slice_in_dim(parts[3].reshape(2, 1, T * HK).astype(f32), t * HK, HK, 2)
    G = w_rank_down.shape[2]
    down = jnp.pad(parts[4].reshape(2, D, G), ((0, 0), (0, 0), (0, 128 - G)))
    up = lax.dynamic_index_in_dim(parts[5], t, 2, keepdims=False)
    up = jnp.pad(up, ((0, 0), (0, 128 - N), (0, 0)))
    allowed, aux = mask_arrays(lax.dynamic_index_in_dim(doc_lengths, c, 0, keepdims=False))
    operands = (pipe_in[0], shard, g_in, g_mid, g_head, bias, down, up, allowed, aux)
    ends, og, sg = run_kernel(X, Z, T, D, R, operands)
    og = og.reshape(R, WIDE)
    head = jnp.zeros((2, 1, T * HK), f32)
    head = lax.dynamic_update_slice_in_dim(head, sg[:, 19:20, 0:HK], t * HK, 2)
    ups = jnp.zeros((2, T, N * HK), f32)
    ups = lax.dynamic_update_slice_in_dim(ups, sg[:, 24 : 24 + N, 0:HK].reshape(2, 1, N * HK), t, 1)
    flat = jnp.concatenate(
        [sg[:, 0:18].reshape(2, -1), sg[:, 18, 0:HV], head.reshape(2, -1), ups.reshape(2, -1)], axis=1
    )
    flat = lax.psum(flat, ("section", "dp", "tensor"))
    flat = lax.dynamic_index_in_dim(flat, c, 0, keepdims=False)
    place = d * T + t
    block = D // (N * T)
    table = flat[: 18 * D].reshape(18, D)
    table = lax.dynamic_slice_in_dim(table, place * block, block, 1)
    at = 18 * D
    o_gain = lax.dynamic_slice_in_dim(flat[at : at + HV], place * (HV // (N * T)), HV // (N * T), 0)
    at += HV
    o_bias = lax.dynamic_slice_in_dim(
        flat[at : at + T * HK], place * (T * HK // (N * T)), T * HK // (N * T), 0
    )
    at += T * HK
    o_up = lax.dynamic_index_in_dim(flat[at:].reshape(T, N, HK), t, 0, keepdims=False)
    o_up = lax.dynamic_slice_in_dim(o_up, d, 1, 0)
    gates = og[:, GU[0] : GU[0] + GU[1]]
    return (
        ends[None],
        table[16][None],
        og[None, :, 0:128],
        og[None, :, 128:256],
        og[None, :, 256:512],
        og[None, :, 512:768],
        table[0:G].T[None],
        o_up[None],
        o_bias[None],
        o_gain[None],
        og[:, OUT[0] : OUT[0] + OUT[1]].T[None],
        table[17][None],
        jnp.concatenate([gates[:, :FFM], gates[:, 2 * FFM : 2 * FFM + 64]], axis=1)[None],
        jnp.concatenate([gates[:, FFM : 2 * FFM], gates[:, 2 * FFM + 64 :]], axis=1)[None],
        og[:, DOWN[0] : DOWN[0] + FFD].T[None],
    )


def solution(mesh):
    count = mesh.shape["dp"]
    side = {16: 4, 4: 2}[count]
    in_specs = (
        P("section", None, "dp", None),
        P("dp", None),
        P("section", ("dp", "tensor")),
        P("section", "dp", "tensor"),
        P("section", "dp", "tensor"),
        P("section", "dp", "tensor"),
        P("section", "dp", "tensor"),
        P("section", ("dp", "tensor"), None),
        P("section", "dp", "tensor"),
        P("section", ("dp", "tensor")),
        P("section", ("dp", "tensor")),
        P("section", "tensor", "dp"),
        P("section", ("dp", "tensor")),
        P("section", "dp", "tensor"),
        P("section", "dp", "tensor"),
        P("section", "tensor", "dp"),
    )
    out_specs = (
        P("section", None, "dp", None),
        P("section", ("dp", "tensor")),
        P("section", "dp", "tensor"),
        P("section", "dp", "tensor"),
        P("section", "dp", "tensor"),
        P("section", "dp", "tensor"),
        P("section", ("dp", "tensor"), None),
        P("section", "dp", "tensor"),
        P("section", ("dp", "tensor")),
        P("section", ("dp", "tensor")),
        P("section", "tensor", "dp"),
        P("section", ("dp", "tensor")),
        P("section", "dp", "tensor"),
        P("section", "dp", "tensor"),
        P("section", "tensor", "dp"),
    )
    return jax.shard_map(
        functools.partial(on_device, side, count // side),
        mesh=mesh,
        in_specs=in_specs,
        out_specs=out_specs,
        check_vma=False,
    )
```

```python
import functools

import jax
import jax.numpy as jnp
from jax import lax
from jax.experimental import pallas as pl
from jax.experimental.pallas import tpu as pltpu
from jax.sharding import PartitionSpec as P

CH = 64
HK = 128
HV = 256
TOK = 256
BLOCKS = TOK // CH
FFD = 704
FFM = 640
QKVG = (0, 768)
OUT = (768, 256)
GU = (1024, 1408)
DOWN = (2432, 768)
SMALL = (3200, 128)
WIDE = 3328
AT_IN, AT_MID, AT_GAIN, AT_BIAS = 16, 17, 18, 19
epsilon = 1e-06
head_floor = 1.0
MESH = pl.DeviceIdType.MESH
f32 = jnp.float32
bf16 = jnp.bfloat16

GATHER = (
    (0, 384, 0),
    (384, 384, 1),
    (768, 768, 0),
    (1536, 896, 1),
    (2432, 384, 0),
    (2816, 384, 1),
    (3200, 128, 0),
)
SCATTER = (
    (1024, 1408, 0),
    (2432, 768, 1),
    (768, 256, 0),
    (0, 384, 0),
    (384, 384, 1),
)


def dot(a, b):
    return lax.dot_general(a, b, (((1,), (0,)), ((), ())), preferred_element_type=f32)


def dot_back(a, b):
    return lax.dot_general(a, b, (((1,), (1,)), ((), ())), preferred_element_type=f32)


def dot_grad(a, b):
    return lax.dot_general(a, b, (((0,), (0,)), ((), ())), preferred_element_type=f32)


def low(a):
    return a.astype(bf16)


def wide(a):
    return a.astype(f32)


def rms_scale(v):
    return lax.rsqrt(jnp.mean(v * v, axis=-1, keepdims=True) + epsilon)


def kernel(
    X,
    Z,
    T,
    pipe_in,
    doc_lengths,
    norm_in,
    w_query,
    w_key,
    w_value,
    w_out_gate,
    w_rank_down,
    w_rank_up,
    rank_bias,
    head_gain,
    w_out,
    norm_mid,
    w_gate,
    w_up,
    w_down,
    ends,
    g_norm_in,
    g_query,
    g_key,
    g_value,
    g_out_gate,
    g_rank_down,
    g_rank_up,
    g_rank_bias,
    g_head_gain,
    g_out,
    g_norm_mid,
    g_gate,
    g_up,
    g_down,
    W,
    shard,
    tiles,
    line,
    pick_gain,
    pick_bias,
    pick_up,
    rows_of,
    gain,
    bias,
    rank_up,
    allowed,
    aux,
    xbuf,
    x1,
    normed,
    nm,
    qkvg,
    cum,
    slope,
    amat,
    states,
    attn,
    mixed,
    hid,
    gu,
    inner,
    rank,
    dh,
    dy0,
    res,
    res_in,
    pbuf,
    rbuf,
    G,
    GA,
    GB,
    GC,
    Q,
    RF,
    og,
    dqkvg,
    dmix,
    small_rows,
    EG,
    EY,
    EB,
    ES,
    EO,
    EX,
    EZ,
    a_sem,
    gs,
    gr,
    ys,
    yr,
    ss,
    sr,
    e_sem,
    t_sem,
    u_sem,
    v_sem,
):
    c = lax.axis_index("section")
    d = lax.axis_index("dp")
    t = lax.axis_index("tensor")
    x, z = d // Z, d % Z
    o = 1 - c
    own = pipe_in.at[0]
    D = pipe_in.shape[-1]
    R = w_query.shape[1]
    B = R // T
    N = X * Z
    G_RANK = w_rank_down.shape[2]
    n_gain, n_bias = head_gain.shape[1], rank_bias.shape[1]
    H = R // 2
    TL = TOK // T
    size = (X, Z)
    here = (x, z)

    def dp_peer(axis, k):
        if axis == 0:
            return ((x + k) % X) * Z + z
        return x * Z + (z + k) % Z

    def remote(src, dst, s, r, **device):
        return pltpu.make_async_remote_copy(
            src_ref=src, dst_ref=dst, send_sem=s, recv_sem=r, device_id=device, device_id_type=MESH
        )

    barrier = pltpu.get_barrier_semaphore()
    for k in range(1, X):
        pl.semaphore_signal(barrier, inc=1, device_id={"dp": dp_peer(0, k)}, device_id_type=MESH)
    for k in range(1, Z):
        pl.semaphore_signal(barrier, inc=1, device_id={"dp": dp_peer(1, k)}, device_id_type=MESH)
    for k in range(1, T):
        pl.semaphore_signal(barrier, inc=1, device_id={"tensor": (t + k) % T}, device_id_type=MESH)
    pl.semaphore_signal(barrier, inc=1, device_id={"section": o}, device_id_type=MESH)
    pl.semaphore_wait(barrier, X + Z + T - 2)

    def lanes(shape):
        return lax.broadcasted_iota(jnp.int32, shape, len(shape) - 1)

    def downs(shape):
        return lax.broadcasted_iota(jnp.int32, shape, len(shape) - 2)

    def column(ref, n):
        line[...] = jnp.zeros_like(line)
        line[0:1, 0:n] = wide(ref[...])
        spread = jnp.broadcast_to(line[0:1, :], (B, 128))
        return jnp.sum(jnp.where(lanes((B, 128)) == downs((B, 128)), spread, 0.0), axis=1, keepdims=True)

    line[...] = jnp.zeros_like(line)
    line[0:B, 0:G_RANK] = wide(w_rank_down[0])
    tile = line[0:B, :]
    lane, down = lanes((B, 128)), downs((B, 128))
    for at, ref, n in (
        (AT_IN, norm_in, B),
        (AT_MID, norm_mid, B),
        (AT_GAIN, head_gain, n_gain),
        (AT_BIAS, rank_bias, n_bias),
    ):
        tile = jnp.where(lane == at, column(ref, n), tile)
    second = wide(w_rank_up[0])
    turned = pltpu.roll(jnp.broadcast_to(second, (8, 128)), 64, 1)[0:1]
    tile = jnp.where(jnp.logical_and(down == 0, lane >= 64), turned, tile)
    tile = jnp.where(jnp.logical_and(down == 1, lane >= 64), second, tile)
    tiles[t] = low(tile)

    def tile_copy(k):
        s, r = t_sem.at[0, k - 1], t_sem.at[1, k - 1]
        peer, source = (t + k) % T, (t - k) % T
        return remote(tiles.at[t], tiles.at[t], s, r, tensor=peer), remote(
            tiles.at[source], tiles.at[source], s, r, tensor=peer
        )

    for k in range(1, T):
        tile_copy(k)[0].start()

    MAIN = SMALL[0]
    shard[:, 0:128] = w_query[0]
    shard[:, 128:256] = w_key[0]
    shard[:, 256:512] = w_value[0]
    shard[:, 512:768] = w_out_gate[0]
    shard[:, 768:1024] = low(wide(w_out[0]).T)
    shard[:, GU[0] : GU[0] + FFM] = w_gate[0, :, :FFM]
    shard[:, GU[0] + FFM : GU[0] + 2 * FFM] = w_up[0, :, :FFM]
    shard[:, GU[0] + 2 * FFM : GU[0] + GU[1]] = jnp.concatenate(
        [w_gate[0, :, FFM:], w_up[0, :, FFM:]], axis=1
    )
    shard[:, MAIN - 128 : MAIN] = jnp.zeros((R, 128), bf16)
    shard[:, DOWN[0] : DOWN[0] + FFD] = low(wide(w_down[0]).T)

    half = lambda h: pl.ds(pl.multiple_of(h * H, H), H)
    main = pl.ds(0, MAIN)
    extra = pl.ds(MAIN, SMALL[1])
    swap_w = remote(
        shard.at[half(o), main], W.at[c, x, z, o, :, main], a_sem.at[0], a_sem.at[1], section=o
    )
    swap_x = remote(own.at[o], xbuf.at[c], a_sem.at[2], a_sem.at[3], section=o)
    keep_w = pltpu.make_async_copy(shard.at[half(c), main], W.at[c, x, z, c, :, main], a_sem.at[4])
    keep_x = pltpu.make_async_copy(own.at[c], xbuf.at[c], a_sem.at[5])
    swap_w.start()
    swap_x.start()
    keep_w.start()
    keep_x.start()
    got_w = remote(
        shard.at[half(o), main], W.at[o, x, z, c, :, main], a_sem.at[0], a_sem.at[1], section=o
    )
    got_x = remote(own.at[o], xbuf.at[o], a_sem.at[2], a_sem.at[3], section=o)
    swap_e = remote(
        shard.at[half(o), extra], W.at[c, x, z, o, :, extra], a_sem.at[6], a_sem.at[7], section=o
    )
    got_e = remote(
        shard.at[half(o), extra], W.at[o, x, z, c, :, extra], a_sem.at[6], a_sem.at[7], section=o
    )
    keep_e = pltpu.make_async_copy(shard.at[half(c), extra], W.at[c, x, z, c, :, extra], a_sem.at[8])

    def small_swap():
        for k in range(1, T):
            tile_copy(k)[1].wait_recv()
        shard[:, MAIN:WIDE] = tiles[...].reshape(R, 128)
        swap_e.start()
        keep_e.start()

    def w_first(l, j, k):
        c0, n, axis = GATHER[j]
        at = W.at[l, x, z, c, :, pl.ds(c0, n)]
        if axis == 0:
            into = W.at[l, (x - k) % X, z, c, :, pl.ds(c0, n)]
        else:
            into = W.at[l, x, (z - k) % Z, c, :, pl.ds(c0, n)]
        s, r = gs.at[l, j, k - 1], gr.at[l, j, k - 1]
        return remote(at, at, s, r, dp=dp_peer(axis, k)), remote(into, into, s, r, dp=dp_peer(axis, k))

    def w_second(l, j, k):
        c0, n, axis = GATHER[j]
        cols = pl.ds(c0, n)
        if axis == 0:
            at, into = W.at[l, :, z, c, :, cols], W.at[l, :, (z - k) % Z, c, :, cols]
        else:
            at, into = W.at[l, x, :, c, :, cols], W.at[l, (x - k) % X, :, c, :, cols]
        s, r = gs.at[l, j, 2 + k], gr.at[l, j, 2 + k]
        return remote(at, at, s, r, dp=dp_peer(1 - axis, k)), remote(
            into, into, s, r, dp=dp_peer(1 - axis, k)
        )

    def w_third(l, j):
        c0, n, _ = GATHER[j]
        cols = pl.ds(c0, n)
        at, into = W.at[l, :, :, c, :, cols], W.at[l, :, :, o, :, cols]
        s, r = gs.at[l, j, 6], gr.at[l, j, 6]
        return remote(at, at, s, r, section=o), remote(into, into, s, r, section=o)

    def gather_first(l, j):
        for k in range(1, size[GATHER[j][2]]):
            w_first(l, j, k)[0].start()

    def gather_second(l, j):
        axis = GATHER[j][2]
        for k in range(1, size[axis]):
            w_first(l, j, k)[1].wait_recv()
        for k in range(1, size[1 - axis]):
            w_second(l, j, k)[0].start()

    def gather_third(l, j):
        axis = GATHER[j][2]
        for k in range(1, size[1 - axis]):
            w_second(l, j, k)[1].wait_recv()
        w_third(l, j)[0].start()

    arrived = set()

    def weight(l, part):
        c0, n = part
        for j, (g0, gn, _) in enumerate(GATHER):
            if g0 < c0 + n and c0 < g0 + gn and (l, j) not in arrived:
                arrived.add((l, j))
                w_third(l, j)[1].wait_recv()
        return W[l, :, :, :, :, c0 : c0 + n].reshape(D, n)

    def prepare():
        r, g = downs((D, HV)), lanes((D, HV))
        pick_gain[...] = low(
            jnp.where(jnp.logical_and(r % B < n_gain, r // B * n_gain + r % B == g), 1.0, 0.0)
        )
        r, g = downs((D, HK)), lanes((D, HK)) + t * HK
        pick_bias[...] = low(
            jnp.where(jnp.logical_and(r % B < n_bias, r // B * n_bias + r % B == g), 1.0, 0.0)
        )
        r, g = downs((128, D)), lanes((128, D))
        for i in range(2):
            pick_up[i] = low(jnp.where(g == r * R + t * B + i, 1.0, 0.0))
        bounds, total = [], 0
        for j in range(doc_lengths.shape[1]):
            total = total + doc_lengths[c, j]
            bounds.append(total)

        def segment(at):
            seg = jnp.zeros(at.shape, jnp.int32)
            for bound in bounds:
                seg = seg + jnp.where(bound <= at, 1, 0)
            return seg

        i, j = downs((TOK, TOK)), lanes((TOK, TOK))
        same = jnp.logical_and(i // CH == j // CH, segment(i) == segment(j))
        allowed[...] = jnp.where(jnp.logical_and(i >= j, same), 1.0, 0.0)
        i, lane = downs((TOK, 128)), lanes((TOK, 128))
        first = i // CH * CH
        seg, before, last = segment(i), segment(first - 1), segment(first + CH - 1)
        one = lambda v: jnp.where(v, 1.0, 0.0)
        aux[...] = jnp.where(
            lane == 0, one(seg == before), jnp.where(lane == 1, one(seg == last), one(last == before))
        )

    def small_whole(l):
        every = weight(l, SMALL)
        pick = low(jnp.where(lanes((16, 128)) == downs((16, 128)) + AT_IN, 1.0, 0.0))
        found = dot_back(pick, every)
        rows_of[l] = found
        gain[l] = dot(low(found), pick_gain[...])[2:3]
        bias[l] = dot(low(found), pick_bias[...])[3:4]
        first, second = dot(pick_up[0], every), dot(pick_up[1], every)
        rank_up[l] = low(jnp.where(lanes((128, 128)) < 64, pltpu.roll(first, 64, 1), second))

    def rows(p):
        return pl.ds(pl.multiple_of(p * TL, TL), TL)

    def sum_copy(i, k):
        peer = (t + k) % T
        return remote(
            pbuf.at[i // 2 % 2, rows(peer)], rbuf.at[i // 2 % 2, k - 1], ys.at[i, k - 1], yr.at[i, k - 1], tensor=peer
        )

    def sum_start(i, part):
        pbuf[i // 2 % 2] = low(part)
        for k in range(1, T):
            sum_copy(i, k).start()

    def sum_wait(i):
        total = wide(pbuf[i // 2 % 2, rows(t)])
        for k in range(1, T):
            sum_copy(i, k).wait_recv()
            total = total + wide(rbuf[i // 2 % 2, k - 1])
        for k in range(1, T):
            sum_copy(i, k).wait_send()
        return total

    def share_copy(i, ref, k):
        peer = (t + k) % T
        s, r = ys.at[i, k - 1], yr.at[i, k - 1]
        mine, into = ref.at[rows(t)], ref.at[rows((t - k) % T)]
        return remote(mine, mine, s, r, tensor=peer), remote(into, into, s, r, tensor=peer)

    def share_start(i, ref, value):
        ref[rows(t)] = low(value)
        for k in range(1, T):
            share_copy(i, ref, k)[0].start()

    def share_wait(i, ref):
        for k in range(1, T):
            share_copy(i, ref, k)[1].wait_recv()
        for k in range(1, T):
            share_copy(i, ref, k)[0].wait_send()

    def s_swap(l, j):
        c0, n, _ = SCATTER[j]
        cols = pl.ds(c0, n)
        return remote(
            G.at[:, :, o, :, cols], GA.at[l, :, :, :, cols], ss.at[l, j, 0], sr.at[l, j, 0], section=o
        )

    def s_first(l, j, k):
        c0, n, axis = SCATTER[j]
        cols = pl.ds(c0, n)
        src = G.at[(x + k) % X, :, c, :, cols] if axis == 0 else G.at[:, (z + k) % Z, c, :, cols]
        return remote(
            src, GB.at[l, k - 1, :, :, cols], ss.at[l, j, k], sr.at[l, j, k], dp=dp_peer(axis, k)
        )

    def s_second(l, j, k):
        c0, n, axis = SCATTER[j]
        cols = pl.ds(c0, n)
        place = (here[1 - axis] + k) % size[1 - axis]
        return remote(
            Q.at[l, place, :, cols],
            GC.at[l, k - 1, :, cols],
            ss.at[l, j, 3 + k],
            sr.at[l, j, 3 + k],
            dp=dp_peer(1 - axis, k),
        )

    def scatter_swap(l, j):
        s_swap(l, j).start()

    def scatter_first(l, j):
        c0, n, axis = SCATTER[j]
        s_swap(l, j).wait()
        for a in range(X):
            G[a, :, c, :, c0 : c0 + n] = low(
                wide(G[a, :, c, :, c0 : c0 + n]) + wide(GA[l, a, :, :, c0 : c0 + n])
            )
        for k in range(1, size[axis]):
            s_first(l, j, k).start()

    def scatter_second(l, j):
        c0, n, axis = SCATTER[j]
        cols = slice(c0, c0 + n)
        total = wide(G[x, :, c, :, cols] if axis == 0 else G[:, z, c, :, cols])
        for k in range(1, size[axis]):
            s_first(l, j, k).wait()
            total = total + wide(GB[l, k - 1, :, :, cols])
        Q[l, :, :, cols] = low(total)
        for k in range(1, size[1 - axis]):
            s_second(l, j, k).start()

    def scatter_third(l, j):
        c0, n, axis = SCATTER[j]
        cols = slice(c0, c0 + n)
        total = wide(Q[l, here[1 - axis], :, cols])
        for k in range(1, size[1 - axis]):
            s_second(l, j, k).wait()
            total = total + wide(GC[l, k - 1, :, cols])
        RF[l, :, cols] = total

    scale = HK**-0.5
    sub = lambda v, n: v[n * CH : (n + 1) * CH]

    def mixer_forward(l):
        qk = qkvg[l]
        b = cum[l]
        qd = low(qk[:, 0:128] * scale * jnp.exp(b))
        kd = low(qk[:, 128:256] * jnp.exp(-b))
        v = low(qk[:, 256:512])
        scores = low(jnp.where(allowed[...] > 0.0, dot_back(qd, kd), 0.0))
        amat[l] = scores
        within = dot(scores, v)
        out = [sub(within, 0)]
        state = None
        for n in range(BLOCKS - 1):
            bn = sub(b, n)
            last = bn[CH - 1 : CH]
            tail = sub(aux[...], n)[:, 1:2]
            kt = low(sub(qk, n)[:, 128:256] * jnp.exp(last - bn) * tail)
            fresh = dot_grad(sub(v, n), kt)
            if state is None:
                state = fresh
            else:
                state = aux[n * CH : n * CH + 1, 2:3] * jnp.exp(last) * state + fresh
            states[l, n] = state
            carried = sub(aux[...], n + 1)[:, 0:1]
            out.append(sub(within, n + 1) + carried * dot_back(sub(qd, n + 1), low(state)))
        attn[l] = jnp.concatenate(out, axis=0)

    def running(v, upper):
        row = lax.broadcasted_iota(jnp.int32, (TOK, TOK), 0)
        col = lax.broadcasted_iota(jnp.int32, (TOK, TOK), 1)
        order = (row <= col) if upper else (row >= col)
        tri = jnp.where(jnp.logical_and(order, row // CH == col // CH), 1.0, 0.0).astype(bf16)
        first = low(v)
        rest = v - wide(first)
        second = low(rest)
        third = low(rest - wide(second))
        return dot(tri, first) + (dot(tri, second) + dot(tri, third))

    def forward(l, i, x_ref, out_ref, hooks):
        hooks[0]()
        small_whole(l)
        xin = wide(x_ref[...])
        normed[l] = low(xin * rms_scale(xin) * rows_of[l, 0:1])
        nrm = normed[l]
        qkvg[l] = dot(nrm, weight(l, QKVG))
        rank[l] = low(dot(nrm, weight(l, SMALL)))
        pre = dot(rank[l], rank_up[l]) + bias[l]
        soft = jnp.log1p(jnp.exp(-jnp.abs(pre)))
        slope[l] = jax.nn.sigmoid(-pre) / 16.0
        cum[l] = running((jnp.minimum(pre, 0.0) - soft) / 16.0, False)
        mixer_forward(l)
        at = attn[l]
        g = qkvg[l, :, 512:768]
        head = lax.rsqrt(jnp.mean(at * at, axis=-1, keepdims=True) + head_floor)
        mixed[l] = low(at * head * gain[l] * g * jax.nn.sigmoid(g))
        hooks[1]()
        sum_start(i, dot_back(mixed[l], weight(l, OUT)))
        hidden = wide(x_ref[rows(t)]) + sum_wait(i)
        hid[l] = hidden
        share_start(i + 1, nm.at[l], hidden * rms_scale(hidden) * rows_of[l, 1:2])
        hooks[2]()
        w_gu = weight(l, GU)
        share_wait(i + 1, nm.at[l])
        acts = dot(nm[l], w_gu)
        gu[l] = acts
        first = jax.nn.silu(acts[:, :FFM]) * acts[:, FFM : 2 * FFM]
        both = acts[:, 2 * FFM :]
        lane = lax.broadcasted_iota(jnp.int32, (TOK, 128), 1)
        last = jnp.where(lane < 64, jax.nn.silu(both) * pltpu.roll(both, 64, 1), 0.0)
        inner[l, :, :FFM] = low(first)
        inner[l, :, FFM:] = low(last)
        sum_start(i + 2, dot_back(inner[l], weight(l, DOWN)))
        hooks[3]()
        y = hid[l] + sum_wait(i + 2)
        share_start(i + 3, out_ref, y)

    def silu_parts(v):
        sig = jax.nn.sigmoid(v)
        return v * sig, sig * (1.0 + v * (1.0 - sig))

    def put(part, left, right):
        c0, n = part
        step = D // X
        for a in range(X):
            G[a, :, :, :, c0 : c0 + n] = low(
                dot_grad(left[:, a * step : (a + 1) * step], right)
            ).reshape(Z, 2, H, n)

    def mixer_backward(l):
        at = attn[l]
        g = qkvg[l, :, 512:768]
        head = lax.rsqrt(jnp.mean(at * at, axis=-1, keepdims=True) + head_floor)
        unit = at * head
        act, act_slope = silu_parts(g)
        dm = dmix[...]
        dqkvg[:, 512:768] = low(dm * unit * gain[l] * act_slope)
        du = dm * act
        d_gain = jnp.sum(du * unit, axis=0, keepdims=True)
        w = du * gain[l]
        do = low(head * (w - unit * jnp.mean(w * unit, axis=-1, keepdims=True)))
        q, k = qkvg[l, :, 0:128], qkvg[l, :, 128:256]
        b = cum[l]
        grow, shrink = jnp.exp(b), jnp.exp(-b)
        qd = low(q * scale * grow)
        kd = low(k * shrink)
        v = low(qkvg[l, :, 256:512])
        d_scores = low(jnp.where(allowed[...] > 0.0, dot_back(do, v), 0.0))
        d_qd = dot(d_scores, kd)
        d_kd = dot_grad(d_scores, qd)
        d_v = dot_grad(amat[l], do)
        d_b = wide(qd) * d_qd - wide(kd) * d_kd
        d_k = d_kd * shrink
        out_q, out_k, out_v, out_b = [None] * BLOCKS, [None] * BLOCKS, [None] * BLOCKS, [None] * BLOCKS
        d_state = None
        for n in reversed(range(BLOCKS)):
            dq_n, dk_n, dv_n, db_n = sub(d_qd, n), sub(d_k, n), sub(d_v, n), sub(d_b, n)
            if n < BLOCKS - 1:
                bn = sub(b, n)
                last = bn[CH - 1 : CH]
                fade = jnp.exp(last - bn) * sub(aux[...], n)[:, 1:2]
                kt = low(sub(k, n) * fade)
                d_low = low(d_state)
                d_kt = dot(sub(v, n), d_low)
                dv_n = dv_n + dot_back(kt, d_low)
                dk_n = dk_n + d_kt * fade
                moved = wide(kt) * d_kt
                db_n = db_n - moved
                d_last = jnp.sum(moved, axis=0, keepdims=True)
                if n > 0:
                    keep = aux[n * CH : n * CH + 1, 2:3] * jnp.exp(last)
                    d_last = d_last + keep * jnp.sum(
                        states[l, n - 1] * d_state, axis=0, keepdims=True
                    )
                place = lax.broadcasted_iota(jnp.int32, (CH, HK), 0)
                db_n = db_n + jnp.where(place == CH - 1, d_last, 0.0)
            if n > 0:
                do_n = low(wide(sub(do, n)) * sub(aux[...], n)[:, 0:1])
                d_across = dot(do_n, low(states[l, n - 1]))
                dq_n = dq_n + d_across
                db_n = db_n + wide(sub(qd, n)) * d_across
                fresh = dot_grad(do_n, sub(qd, n))
                d_state = fresh if n == BLOCKS - 1 else keep * d_state + fresh
            out_q[n], out_k[n], out_v[n], out_b[n] = dq_n, dk_n, dv_n, db_n
        dqkvg[:, 0:128] = low(jnp.concatenate(out_q, axis=0) * scale * grow)
        dqkvg[:, 128:256] = low(jnp.concatenate(out_k, axis=0))
        dqkvg[:, 256:512] = low(jnp.concatenate(out_v, axis=0))
        d_decay = running(jnp.concatenate(out_b, axis=0), True)
        return low(d_decay * slope[l]), d_gain

    def small_copy(l, k):
        peer = (t + k) % T
        return remote(
            EG.at[l, :, :, peer], EB.at[l, k - 1], u_sem.at[l, 0, k - 1], u_sem.at[l, 1, k - 1], tensor=peer
        )

    def small_gradients(l, d_rank, d_pre, d_gain):
        rank_rows = downs((16, HV))
        at_gain = low(jnp.where(rank_rows == 2, d_gain, 0.0))
        d_bias = jnp.sum(wide(d_pre), axis=0, keepdims=True)
        at_bias = low(jnp.where(downs((16, HK)) == 3, d_bias, 0.0))
        found = small_rows[l] + dot_back(at_gain, pick_gain[...]) + dot_back(at_bias, pick_bias[...])
        pick = low(jnp.where(lanes((16, 128)) == downs((16, 128)) + AT_IN, 1.0, 0.0))
        ups = dot_grad(rank[l], d_pre)
        right = lanes((128, 128)) >= 64
        every = (
            dot_grad(normed[l], d_rank)
            + dot_grad(low(found), pick)
            + dot_grad(pick_up[0], low(jnp.where(right, pltpu.roll(ups, 64, 1), 0.0)))
            + dot_grad(pick_up[1], low(jnp.where(right, ups, 0.0)))
        )
        EG[l] = low(every).reshape(X, Z, T, B, 128)
        for k in range(1, T):
            small_copy(l, k).start()

    def small_sum(l):
        total = wide(EG[l, :, :, t])
        for k in range(1, T):
            small_copy(l, k).wait()
            total = total + wide(EB[l, k - 1])
        EY[l] = low(total)

    small_swap_out = remote(EY.at[o], EO, v_sem.at[0, 0], v_sem.at[0, 1], section=o)

    def small_x(k):
        return remote(
            ES.at[(x + k) % X], EX.at[k - 1], v_sem.at[k, 0], v_sem.at[k, 1], dp=dp_peer(0, k)
        )

    def small_z(k):
        return remote(
            ES.at[x, (z + k) % Z], EZ.at[k - 1], v_sem.at[3 + k, 0], v_sem.at[3 + k, 1], dp=dp_peer(1, k)
        )

    def small_first():
        small_swap_out.wait()
        ES[...] = low(wide(EY[c]) + wide(EO[...]))
        for k in range(1, X):
            small_x(k).start()

    def small_second():
        total = wide(ES[x])
        for k in range(1, X):
            small_x(k).wait()
            total = total + wide(EX[k - 1])
        ES[x] = low(total)
        for k in range(1, Z):
            small_z(k).start()

    def small_third():
        total = wide(ES[x, z])
        for k in range(1, Z):
            small_z(k).wait()
            total = total + wide(EZ[k - 1])
        g_rank_down[0] = total[:, 0:G_RANK]
        turn = lanes((B, 128)) == downs((B, 128))
        for at, ref, n in (
            (AT_IN, g_norm_in, B),
            (AT_MID, g_norm_mid, B),
            (AT_GAIN, g_head_gain, n_gain),
            (AT_BIAS, g_rank_bias, n_bias),
        ):
            row = jnp.sum(jnp.where(turn, total[:, at : at + 1], 0.0), axis=0, keepdims=True)
            ref[...] = row[:, 0:n]
        turned = pltpu.roll(total[0:8], 64, 1)[0:1]
        g_rank_up[0] = jnp.where(lanes((1, 128)) < 64, turned, total[1:2])

    def backward(l, i, x_ref, dy_ref, out_ref, hooks):
        dy = dy_ref[...]
        d_inner = dot(dy, weight(l, DOWN))
        gate, up, both = gu[l, :, :FFM], gu[l, :, FFM : 2 * FFM], gu[l, :, 2 * FFM :]
        act, act_slope = silu_parts(gate)
        act_b, slope_b = silu_parts(both)
        rest = d_inner[:, FFM:]
        mix_b = rest * pltpu.roll(both, 64, 1) * slope_b + pltpu.roll(rest * act_b, 64, 1)
        d_gu = jnp.concatenate(
            [low(d_inner[:, :FFM] * up * act_slope), low(d_inner[:, :FFM] * act), low(mix_b)], axis=1
        )
        sum_start(i, dot_back(d_gu, weight(l, GU)))
        put(DOWN, dy, inner[l])
        scatter_swap(l, 1)
        put(GU, nm[l], d_gu)
        scatter_swap(l, 0)
        hooks[0]()
        d_mid = sum_wait(i)
        hidden = hid[l]
        scale_mid = rms_scale(hidden)
        unit = hidden * scale_mid
        small_rows[l] = jnp.zeros((16, D), f32)
        small_rows[l, 1:2] = jnp.sum(d_mid * unit, axis=0, keepdims=True)
        scaled = d_mid * rows_of[l, 1:2]
        d_hidden = wide(dy_ref[rows(t)]) + scale_mid * (
            scaled - unit * jnp.mean(scaled * unit, axis=-1, keepdims=True)
        )
        hid[l] = d_hidden
        share_start(i + 1, dh, d_hidden)
        hooks[1]()
        share_wait(i + 1, dh)
        dmix[...] = dot(dh[...], weight(l, OUT))
        d_pre, d_gain = mixer_backward(l)
        d_rank = low(dot_back(d_pre, rank_up[l]))
        partial = dot_back(dqkvg[...], weight(l, QKVG)) + dot_back(d_rank, weight(l, SMALL))
        sum_start(i + 2, partial)
        xin = wide(x_ref[...])
        small_rows[l, 0:1] = jnp.sum(partial * (xin * rms_scale(xin)), axis=0, keepdims=True)
        hooks[2]()
        put(OUT, dh[...], mixed[l])
        scatter_swap(l, 2)
        put(QKVG, normed[l], dqkvg[...])
        scatter_swap(l, 3)
        scatter_swap(l, 4)
        small_gradients(l, d_rank, d_pre, d_gain)
        hooks[3]()
        d_normed = sum_wait(i + 2)
        xin = wide(x_ref[rows(t)])
        scale_in = rms_scale(xin)
        unit = xin * scale_in
        scaled = d_normed * rows_of[l, 0:1]
        dx = hid[l] + scale_in * (scaled - unit * jnp.mean(scaled * unit, axis=-1, keepdims=True))
        share_start(i + 3, out_ref, dx)

    def nothing():
        pass

    early, late = (6, 0, 1), (2, 3, 4, 5)

    def first_weights():
        prepare()
        small_swap()
        got_w.wait_recv()
        keep_w.wait()
        for j in early[1:]:
            gather_first(0, j)
        got_e.wait_recv()
        keep_e.wait()
        gather_first(0, early[0])
        for j in early:
            gather_second(0, j)
        for j in late:
            gather_first(0, j)
        for j in early:
            gather_third(0, j)
        for j in late:
            gather_second(0, j)

    def each(step, l, which):
        def run():
            for j in which:
                step(l, j)

        return run

    got_x.wait_recv()
    keep_x.wait()
    everything = early + late
    forward(
        0,
        0,
        xbuf.at[0],
        x1,
        (
            first_weights,
            each(gather_third, 0, late),
            each(gather_first, 1, everything),
            each(gather_second, 1, everything),
        ),
    )
    each(gather_third, 1, everything)()
    share_wait(3, x1)
    forward(1, 4, x1, res.at[1], (nothing, nothing, nothing, nothing))

    def send_y():
        share_wait(7, res.at[1])

    ff, mix = (0, 1), (2, 3, 4)
    backward(
        1,
        8,
        x1,
        xbuf.at[1],
        dy0,
        (
            send_y,
            each(scatter_first, 1, ff),
            each(scatter_second, 1, ff),
            each(scatter_third, 1, ff),
        ),
    )
    each(scatter_first, 1, mix)()
    share_wait(11, dy0)

    def in_second():
        each(scatter_first, 0, ff)()
        each(scatter_third, 1, mix)()
        small_sum(1)

    backward(
        0,
        12,
        xbuf.at[0],
        dy0,
        res.at[0],
        (each(scatter_second, 1, mix), in_second, each(scatter_second, 0, ff), each(scatter_third, 0, ff)),
    )
    each(scatter_first, 0, mix)()
    small_sum(0)
    small_swap_out.start()
    share_wait(15, res.at[0])
    give_end = remote(res.at[o], res_in, e_sem.at[0], e_sem.at[1], section=o)
    give_end.start()
    small_first()
    each(scatter_second, 0, mix)()
    small_second()
    ends[0, c] = wide(res[c])
    each(scatter_third, 0, mix)()
    give_grad = remote(RF.at[o], og.at[c], e_sem.at[2], e_sem.at[3], section=o)
    got_grad = remote(RF.at[o], og.at[o], e_sem.at[2], e_sem.at[3], section=o)
    give_grad.start()
    og[c] = RF[c]
    give_end.wait_recv()
    ends[0, o] = wide(res_in[...])
    small_third()
    got_grad.wait_recv()
    whole = lambda c0, n: og[:, :, c0 : c0 + n].reshape(R, n)
    g_query[0] = whole(0, 128)
    g_key[0] = whole(128, 128)
    g_value[0] = whole(256, 256)
    g_out_gate[0] = whole(512, 256)
    g_out[0] = whole(*OUT).T
    g_gate[0, :, :FFM] = whole(GU[0], FFM)
    g_up[0, :, :FFM] = whole(GU[0] + FFM, FFM)
    both = whole(GU[0] + 2 * FFM, 128)
    g_gate[0, :, FFM:] = both[:, 0:64]
    g_up[0, :, FFM:] = pltpu.roll(both, 64, 1)[:, 0:64]
    g_down[0] = whole(*DOWN).T[0:FFD]
    give_end.wait_send()
    give_grad.wait_send()
    swap_w.wait_send()
    swap_x.wait_send()
    swap_e.wait_send()
    for k in range(1, T):
        tile_copy(k)[0].wait_send()
    for l in range(2):
        for j, (_, _, axis) in enumerate(GATHER):
            for k in range(1, size[axis]):
                w_first(l, j, k)[0].wait_send()
            for k in range(1, size[1 - axis]):
                w_second(l, j, k)[0].wait_send()
            w_third(l, j)[0].wait_send()


def on_device(X, Z, *operands):
    T = lax.axis_size("tensor")
    D = operands[0].shape[-1]
    R = operands[3].shape[1]
    H, TL, B, N = R // 2, TOK // T, R // T, X * Z
    top = max(X, Z)
    scratch = [
        pltpu.VMEM((2, X, Z, 2, H, WIDE), bf16),
        pltpu.VMEM((R, WIDE), bf16),
        pltpu.VMEM((T, B, 128), bf16),
        pltpu.VMEM((max(B, 8), 128), f32),
        pltpu.VMEM((D, HV), bf16),
        pltpu.VMEM((D, HK), bf16),
        pltpu.VMEM((2, 128, D), bf16),
        pltpu.VMEM((2, 16, D), f32),
        pltpu.VMEM((2, 1, HV), f32),
        pltpu.VMEM((2, 1, HK), f32),
        pltpu.VMEM((2, 128, HK), bf16),
        pltpu.VMEM((TOK, TOK), f32),
        pltpu.VMEM((TOK, 128), f32),
        pltpu.VMEM((2, TOK, D), bf16),
        pltpu.VMEM((TOK, D), bf16),
        pltpu.VMEM((2, TOK, D), bf16),
        pltpu.VMEM((2, TOK, D), bf16),
        pltpu.VMEM((2, TOK, 768), f32),
        pltpu.VMEM((2, TOK, HK), f32),
        pltpu.VMEM((2, TOK, HK), f32),
        pltpu.VMEM((2, TOK, TOK), bf16),
        pltpu.VMEM((2, BLOCKS - 1, HV, HK), f32),
        pltpu.VMEM((2, TOK, HV), f32),
        pltpu.VMEM((2, TOK, HV), bf16),
        pltpu.VMEM((2, TL, D), f32),
        pltpu.VMEM((2, TOK, GU[1]), f32),
        pltpu.VMEM((2, TOK, DOWN[1]), bf16),
        pltpu.VMEM((2, TOK, 128), bf16),
        pltpu.VMEM((TOK, D), bf16),
        pltpu.VMEM((TOK, D), bf16),
        pltpu.VMEM((2, TOK, D), bf16),
        pltpu.VMEM((TOK, D), bf16),
        pltpu.VMEM((2, TOK, D), bf16),
        pltpu.VMEM((2, T - 1, TL, D), bf16),
        pltpu.VMEM((X, Z, 2, H, SMALL[0]), bf16),
        pltpu.VMEM((2, X, Z, H, SMALL[0]), bf16),
        pltpu.VMEM((2, top - 1, top, H, SMALL[0]), bf16),
        pltpu.VMEM((2, top - 1, H, SMALL[0]), bf16),
        pltpu.VMEM((2, top, H, SMALL[0]), bf16),
        pltpu.VMEM((2, H, SMALL[0]), f32),
        pltpu.VMEM((2, H, SMALL[0]), f32),
        pltpu.VMEM((TOK, 768), bf16),
        pltpu.VMEM((TOK, HV), f32),
        pltpu.VMEM((2, 16, D), f32),
        pltpu.VMEM((2, X, Z, T, B, 128), bf16),
        pltpu.VMEM((2, X, Z, B, 128), bf16),
        pltpu.VMEM((2, T - 1, X, Z, B, 128), bf16),
        pltpu.VMEM((X, Z, B, 128), bf16),
        pltpu.VMEM((X, Z, B, 128), bf16),
        pltpu.VMEM((X - 1, Z, B, 128), bf16),
        pltpu.VMEM((Z - 1, B, 128), bf16),
        pltpu.SemaphoreType.DMA((9,)),
        pltpu.SemaphoreType.DMA((2, len(GATHER), 7)),
        pltpu.SemaphoreType.DMA((2, len(GATHER), 7)),
        pltpu.SemaphoreType.DMA((16, T - 1)),
        pltpu.SemaphoreType.DMA((16, T - 1)),
        pltpu.SemaphoreType.DMA((2, len(SCATTER), 7)),
        pltpu.SemaphoreType.DMA((2, len(SCATTER), 7)),
        pltpu.SemaphoreType.DMA((4,)),
        pltpu.SemaphoreType.DMA((2, T - 1)),
        pltpu.SemaphoreType.DMA((2, 2, T - 1)),
        pltpu.SemaphoreType.DMA((7, 2)),
    ]
    order = (2, 3, 4, 5, 6, 7, 8, 9, 10, 11, 12, 13, 14, 15)
    outs = (jax.ShapeDtypeStruct((1, 2, TOK, D), f32),) + tuple(
        jax.ShapeDtypeStruct(operands[k].shape, f32) for k in order
    )
    vmem = pl.BlockSpec(memory_space=pltpu.VMEM)
    smem = pl.BlockSpec(memory_space=pltpu.SMEM)
    return pl.pallas_call(
        functools.partial(kernel, X, Z, T),
        out_shape=outs,
        in_specs=[vmem, smem] + [vmem] * (len(operands) - 2),
        out_specs=(vmem,) * len(outs),
        scratch_shapes=scratch,
        compiler_params=pltpu.CompilerParams(
            collective_id=0, has_side_effects=True, vmem_limit_bytes=64 * 1024 * 1024 - 65536
        ),
    )(*operands)


def solution(mesh):
    count = mesh.shape["dp"]
    side = {16: 4, 4: 2}[count]
    in_specs = (
        P("section", None, "dp", None),
        P("dp", None),
        P("section", ("dp", "tensor")),
        P("section", "dp", "tensor"),
        P("section", "dp", "tensor"),
        P("section", "dp", "tensor"),
        P("section", "dp", "tensor"),
        P("section", ("dp", "tensor"), None),
        P("section", "dp", "tensor"),
        P("section", ("dp", "tensor")),
        P("section", ("dp", "tensor")),
        P("section", "tensor", "dp"),
        P("section", ("dp", "tensor")),
        P("section", "dp", "tensor"),
        P("section", "dp", "tensor"),
        P("section", "tensor", "dp"),
    )
    out_specs = (
        P("section", None, "dp", None),
        P("section", ("dp", "tensor")),
        P("section", "dp", "tensor"),
        P("section", "dp", "tensor"),
        P("section", "dp", "tensor"),
        P("section", "dp", "tensor"),
        P("section", ("dp", "tensor"), None),
        P("section", "dp", "tensor"),
        P("section", ("dp", "tensor")),
        P("section", ("dp", "tensor")),
        P("section", "tensor", "dp"),
        P("section", ("dp", "tensor")),
        P("section", "dp", "tensor"),
        P("section", "dp", "tensor"),
        P("section", "tensor", "dp"),
    )
    return jax.shard_map(
        functools.partial(on_device, side, count // side),
        mesh=mesh,
        in_specs=in_specs,
        out_specs=out_specs,
        check_vma=False,
    )
```

```python
import functools

import jax
import jax.numpy as jnp
from jax import lax
from jax.experimental import pallas as pl
from jax.experimental.pallas import tpu as pltpu
from jax.sharding import PartitionSpec as P

CH = 64
HK = 128
HV = 256
TOK = 256
BLOCKS = TOK // CH
FFD = 704
FFM = 640
QKVG = (0, 768)
OUT = (768, 256)
GU = (1024, 1408)
DOWN = (2432, 768)
SMALL = (3200, 128)
WIDE = 3328
AT_IN, AT_MID, AT_GAIN, AT_BIAS = 16, 17, 18, 19
epsilon = 1e-06
head_floor = 1.0
MESH = pl.DeviceIdType.MESH
f32 = jnp.float32
bf16 = jnp.bfloat16

GATHER = (
    (0, 384, 0),
    (384, 384, 1),
    (768, 256, 0),
    (1024, 640, 1),
    (1664, 768, 0),
    (2432, 384, 1),
    (2816, 384, 0),
    (3200, 128, 1),
)
SCATTER = (
    (1024, 1408, 0),
    (2432, 768, 1),
    (768, 256, 0),
    (0, 384, 0),
    (384, 384, 1),
)


def dot(a, b):
    return lax.dot_general(a, b, (((1,), (0,)), ((), ())), preferred_element_type=f32)


def dot_back(a, b):
    return lax.dot_general(a, b, (((1,), (1,)), ((), ())), preferred_element_type=f32)


def dot_grad(a, b):
    return lax.dot_general(a, b, (((0,), (0,)), ((), ())), preferred_element_type=f32)


def low(a):
    return a.astype(bf16)


def wide(a):
    return a.astype(f32)


def rms_scale(v):
    return lax.rsqrt(jnp.mean(v * v, axis=-1, keepdims=True) + epsilon)


def kernel(
    X,
    Z,
    T,
    pipe_in,
    doc_lengths,
    norm_in,
    w_query,
    w_key,
    w_value,
    w_out_gate,
    w_rank_down,
    w_rank_up,
    rank_bias,
    head_gain,
    w_out,
    norm_mid,
    w_gate,
    w_up,
    w_down,
    ends,
    g_norm_in,
    g_query,
    g_key,
    g_value,
    g_out_gate,
    g_rank_down,
    g_rank_up,
    g_rank_bias,
    g_head_gain,
    g_out,
    g_norm_mid,
    g_gate,
    g_up,
    g_down,
    W,
    shard,
    tiles,
    line,
    pick_gain,
    pick_bias,
    pick_up,
    rows_of,
    gain,
    bias,
    rank_up,
    allowed,
    aux,
    xbuf,
    x1,
    normed,
    nm,
    qkvg,
    cum,
    slope,
    amat,
    states,
    attn,
    mixed,
    hid,
    d_hid,
    gu,
    inner,
    rank,
    dh,
    dy0,
    res,
    pbuf,
    rbuf,
    G,
    GA,
    GB,
    GC,
    Q,
    RF,
    og,
    dqkvg,
    d_gu,
    d_pre,
    d_rank,
    d_states,
    small_rows,
    EG,
    EY,
    EB,
    ES,
    EO,
    EX,
    EZ,
    a_sem,
    gs,
    gr,
    ys,
    yr,
    ss,
    sr,
    e_sem,
    t_sem,
    u_sem,
    v_sem,
):
    c = lax.axis_index("section")
    d = lax.axis_index("dp")
    t = lax.axis_index("tensor")
    x, z = d // Z, d % Z
    o = 1 - c
    own = pipe_in.at[0]
    D = pipe_in.shape[-1]
    R = w_query.shape[1]
    B = R // T
    N = X * Z
    G_RANK = w_rank_down.shape[2]
    n_gain, n_bias = head_gain.shape[1], rank_bias.shape[1]
    H = R // 2
    HALF = TOK // 2
    S = HALF // T
    size = (X, Z)
    here = (x, z)

    def dp_peer(axis, k):
        if axis == 0:
            return ((x + k) % X) * Z + z
        return x * Z + (z + k) % Z

    def remote(src, dst, s, r, **device):
        return pltpu.make_async_remote_copy(
            src_ref=src, dst_ref=dst, send_sem=s, recv_sem=r, device_id=device, device_id_type=MESH
        )

    barrier = pltpu.get_barrier_semaphore()
    for k in range(1, X):
        pl.semaphore_signal(barrier, inc=1, device_id={"dp": dp_peer(0, k)}, device_id_type=MESH)
    for k in range(1, Z):
        pl.semaphore_signal(barrier, inc=1, device_id={"dp": dp_peer(1, k)}, device_id_type=MESH)
    for k in range(1, T):
        pl.semaphore_signal(barrier, inc=1, device_id={"tensor": (t + k) % T}, device_id_type=MESH)
    pl.semaphore_signal(barrier, inc=1, device_id={"section": o}, device_id_type=MESH)
    pl.semaphore_wait(barrier, X + Z + T - 2)

    def lanes(shape):
        return lax.broadcasted_iota(jnp.int32, shape, len(shape) - 1)

    def downs(shape):
        return lax.broadcasted_iota(jnp.int32, shape, len(shape) - 2)

    def column(ref, n):
        line[...] = jnp.zeros_like(line)
        line[0:1, 0:n] = wide(ref[...])
        spread = jnp.broadcast_to(line[0:1, :], (B, 128))
        return jnp.sum(jnp.where(lanes((B, 128)) == downs((B, 128)), spread, 0.0), axis=1, keepdims=True)

    line[...] = jnp.zeros_like(line)
    line[0:B, 0:G_RANK] = wide(w_rank_down[0])
    tile = line[0:B, :]
    lane, down = lanes((B, 128)), downs((B, 128))
    for at, ref, n in (
        (AT_IN, norm_in, B),
        (AT_MID, norm_mid, B),
        (AT_GAIN, head_gain, n_gain),
        (AT_BIAS, rank_bias, n_bias),
    ):
        tile = jnp.where(lane == at, column(ref, n), tile)
    second = wide(w_rank_up[0])
    turned = pltpu.roll(jnp.broadcast_to(second, (8, 128)), 64, 1)[0:1]
    tile = jnp.where(jnp.logical_and(down == 0, lane >= 64), turned, tile)
    tile = jnp.where(jnp.logical_and(down == 1, lane >= 64), second, tile)
    tiles[t] = low(tile)

    def tile_copy(k):
        s, r = t_sem.at[0, k - 1], t_sem.at[1, k - 1]
        peer, source = (t + k) % T, (t - k) % T
        return remote(tiles.at[t], tiles.at[t], s, r, tensor=peer), remote(
            tiles.at[source], tiles.at[source], s, r, tensor=peer
        )

    for k in range(1, T):
        tile_copy(k)[0].start()

    MAIN = SMALL[0]
    shard[:, 0:128] = w_query[0]
    shard[:, 128:256] = w_key[0]
    shard[:, 256:512] = w_value[0]
    shard[:, 512:768] = w_out_gate[0]
    shard[:, 768:1024] = w_out[0]
    shard[:, GU[0] : GU[0] + FFM] = w_gate[0, :, :FFM]
    shard[:, GU[0] + FFM : GU[0] + 2 * FFM] = w_up[0, :, :FFM]
    shard[:, GU[0] + 2 * FFM : GU[0] + GU[1]] = jnp.concatenate(
        [w_gate[0, :, FFM:], w_up[0, :, FFM:]], axis=1
    )
    shard[:, MAIN - 128 : MAIN] = jnp.zeros((R, 128), bf16)
    shard[:, DOWN[0] : DOWN[0] + FFD] = w_down[0]

    half = lambda h: pl.ds(pl.multiple_of(h * H, H), H)
    main = pl.ds(0, MAIN)
    extra = pl.ds(MAIN, SMALL[1])
    swap_w = remote(
        shard.at[half(o), main], W.at[c, x, z, o, :, main], a_sem.at[0], a_sem.at[1], section=o
    )
    swap_x = remote(own.at[o], xbuf.at[c], a_sem.at[2], a_sem.at[3], section=o)
    keep_w = pltpu.make_async_copy(shard.at[half(c), main], W.at[c, x, z, c, :, main], a_sem.at[4])
    keep_x = pltpu.make_async_copy(own.at[c], xbuf.at[c], a_sem.at[5])
    swap_w.start()
    swap_x.start()
    keep_w.start()
    keep_x.start()
    got_w = remote(
        shard.at[half(o), main], W.at[o, x, z, c, :, main], a_sem.at[0], a_sem.at[1], section=o
    )
    got_x = remote(own.at[o], xbuf.at[o], a_sem.at[2], a_sem.at[3], section=o)
    swap_e = remote(
        shard.at[half(o), extra], W.at[c, x, z, o, :, extra], a_sem.at[6], a_sem.at[7], section=o
    )
    got_e = remote(
        shard.at[half(o), extra], W.at[o, x, z, c, :, extra], a_sem.at[6], a_sem.at[7], section=o
    )
    keep_e = pltpu.make_async_copy(shard.at[half(c), extra], W.at[c, x, z, c, :, extra], a_sem.at[8])

    def small_swap():
        for k in range(1, T):
            tile_copy(k)[1].wait_recv()
        shard[:, MAIN:WIDE] = tiles[...].reshape(R, 128)
        swap_e.start()
        keep_e.start()

    def w_first(l, j, k):
        c0, n, axis = GATHER[j]
        at = W.at[l, x, z, c, :, pl.ds(c0, n)]
        if axis == 0:
            into = W.at[l, (x - k) % X, z, c, :, pl.ds(c0, n)]
        else:
            into = W.at[l, x, (z - k) % Z, c, :, pl.ds(c0, n)]
        s, r = gs.at[l, j, k - 1], gr.at[l, j, k - 1]
        return remote(at, at, s, r, dp=dp_peer(axis, k)), remote(into, into, s, r, dp=dp_peer(axis, k))

    def w_second(l, j, k):
        c0, n, axis = GATHER[j]
        cols = pl.ds(c0, n)
        if axis == 0:
            at, into = W.at[l, :, z, c, :, cols], W.at[l, :, (z - k) % Z, c, :, cols]
        else:
            at, into = W.at[l, x, :, c, :, cols], W.at[l, (x - k) % X, :, c, :, cols]
        s, r = gs.at[l, j, 2 + k], gr.at[l, j, 2 + k]
        return remote(at, at, s, r, dp=dp_peer(1 - axis, k)), remote(
            into, into, s, r, dp=dp_peer(1 - axis, k)
        )

    def w_third(l, j):
        c0, n, _ = GATHER[j]
        cols = pl.ds(c0, n)
        at, into = W.at[l, :, :, c, :, cols], W.at[l, :, :, o, :, cols]
        s, r = gs.at[l, j, 6], gr.at[l, j, 6]
        return remote(at, at, s, r, section=o), remote(into, into, s, r, section=o)

    def gather_first(l, j):
        for k in range(1, size[GATHER[j][2]]):
            w_first(l, j, k)[0].start()

    def gather_second(l, j):
        axis = GATHER[j][2]
        for k in range(1, size[axis]):
            w_first(l, j, k)[1].wait_recv()
        for k in range(1, size[1 - axis]):
            w_second(l, j, k)[0].start()

    def gather_third(l, j):
        axis = GATHER[j][2]
        for k in range(1, size[1 - axis]):
            w_second(l, j, k)[1].wait_recv()
        w_third(l, j)[0].start()

    arrived = set()

    def weight(l, part):
        c0, n = part
        for j, (g0, gn, _) in enumerate(GATHER):
            if g0 < c0 + n and c0 < g0 + gn and (l, j) not in arrived:
                arrived.add((l, j))
                w_third(l, j)[1].wait_recv()
        return W[l, :, :, :, :, c0 : c0 + n].reshape(D, n)

    def prepare():
        r, g = downs((D, HV)), lanes((D, HV))
        pick_gain[...] = low(
            jnp.where(jnp.logical_and(r % B < n_gain, r // B * n_gain + r % B == g), 1.0, 0.0)
        )
        r, g = downs((D, HK)), lanes((D, HK)) + t * HK
        pick_bias[...] = low(
            jnp.where(jnp.logical_and(r % B < n_bias, r // B * n_bias + r % B == g), 1.0, 0.0)
        )
        r, g = downs((128, D)), lanes((128, D))
        for i in range(2):
            pick_up[i] = low(jnp.where(g == r * R + t * B + i, 1.0, 0.0))
        bounds, total = [], 0
        for j in range(doc_lengths.shape[1]):
            total = total + doc_lengths[c, j]
            bounds.append(total)

        def segment(at):
            seg = jnp.zeros(at.shape, jnp.int32)
            for bound in bounds:
                seg = seg + jnp.where(bound <= at, 1, 0)
            return seg

        i, j = downs((TOK, TOK)), lanes((TOK, TOK))
        same = jnp.logical_and(i // CH == j // CH, segment(i) == segment(j))
        allowed[...] = jnp.where(jnp.logical_and(i >= j, same), 1.0, 0.0)
        i, lane = downs((TOK, 128)), lanes((TOK, 128))
        first = i // CH * CH
        seg, before, last = segment(i), segment(first - 1), segment(first + CH - 1)
        one = lambda v: jnp.where(v, 1.0, 0.0)
        aux[...] = jnp.where(
            lane == 0, one(seg == before), jnp.where(lane == 1, one(seg == last), one(last == before))
        )

    def small_whole(l):
        every = weight(l, SMALL)
        pick = low(jnp.where(lanes((16, 128)) == downs((16, 128)) + AT_IN, 1.0, 0.0))
        found = dot_back(pick, every)
        rows_of[l] = found
        gain[l] = dot(low(found), pick_gain[...])[2:3]
        bias[l] = dot(low(found), pick_bias[...])[3:4]
        first, second = dot(pick_up[0], every), dot(pick_up[1], every)
        rank_up[l] = low(jnp.where(lanes((128, 128)) < 64, pltpu.roll(first, 64, 1), second))

    def rows(p, h):
        return pl.ds(pl.multiple_of(h * HALF + p * S, S), S)

    def of(h):
        return slice(h * HALF, (h + 1) * HALF)

    def sum_copy(i, h, k):
        peer = (t + k) % T
        into = rbuf.at[2 if i == 6 else i // 2 % 2, h, k - 1]
        return remote(
            pbuf.at[i // 2 % 2, rows(peer, h)], into, ys.at[i, h, k - 1], yr.at[i, h, k - 1], tensor=peer
        )

    def sum_start(i, h, part):
        pbuf[i // 2 % 2, of(h)] = low(part)
        for k in range(1, T):
            sum_copy(i, h, k).start()

    def sum_wait(i, h):
        total = wide(pbuf[i // 2 % 2, rows(t, h)])
        for k in range(1, T):
            sum_copy(i, h, k).wait_recv()
            total = total + wide(rbuf[2 if i == 6 else i // 2 % 2, h, k - 1])
        for k in range(1, T):
            sum_copy(i, h, k).wait_send()
        return total

    def share_copy(i, h, ref, k):
        peer = (t + k) % T
        s, r = ys.at[i, h, k - 1], yr.at[i, h, k - 1]
        mine, into = ref.at[rows(t, h)], ref.at[rows((t - k) % T, h)]
        return remote(mine, mine, s, r, tensor=peer), remote(into, into, s, r, tensor=peer)

    def share_start(i, h, ref, value):
        ref[rows(t, h)] = low(value)
        for k in range(1, T):
            share_copy(i, h, ref, k)[0].start()

    def share_wait(i, h, ref):
        for k in range(1, T):
            share_copy(i, h, ref, k)[1].wait_recv()
        for k in range(1, T):
            share_copy(i, h, ref, k)[0].wait_send()

    def s_swap(l, j):
        c0, n, _ = SCATTER[j]
        cols = pl.ds(c0, n)
        return remote(
            G.at[:, :, o, :, cols], GA.at[l, :, :, :, cols], ss.at[l, j, 0], sr.at[l, j, 0], section=o
        )

    def s_first(l, j, k):
        c0, n, axis = SCATTER[j]
        cols = pl.ds(c0, n)
        src = G.at[(x + k) % X, :, c, :, cols] if axis == 0 else G.at[:, (z + k) % Z, c, :, cols]
        return remote(
            src, GB.at[l, k - 1, :, :, cols], ss.at[l, j, k], sr.at[l, j, k], dp=dp_peer(axis, k)
        )

    def s_second(l, j, k):
        c0, n, axis = SCATTER[j]
        cols = pl.ds(c0, n)
        place = (here[1 - axis] + k) % size[1 - axis]
        return remote(
            Q.at[l, place, :, cols],
            GC.at[l, k - 1, :, cols],
            ss.at[l, j, 3 + k],
            sr.at[l, j, 3 + k],
            dp=dp_peer(1 - axis, k),
        )

    def scatter_swap(l, j):
        s_swap(l, j).start()

    def scatter_first(l, j):
        c0, n, axis = SCATTER[j]
        s_swap(l, j).wait()
        for a in range(X):
            G[a, :, c, :, c0 : c0 + n] = low(
                wide(G[a, :, c, :, c0 : c0 + n]) + wide(GA[l, a, :, :, c0 : c0 + n])
            )
        for k in range(1, size[axis]):
            s_first(l, j, k).start()

    def scatter_second(l, j):
        c0, n, axis = SCATTER[j]
        cols = slice(c0, c0 + n)
        total = wide(G[x, :, c, :, cols] if axis == 0 else G[:, z, c, :, cols])
        for k in range(1, size[axis]):
            s_first(l, j, k).wait()
            total = total + wide(GB[l, k - 1, :, :, cols])
        Q[l, :, :, cols] = low(total)
        for k in range(1, size[1 - axis]):
            s_second(l, j, k).start()

    def scatter_third(l, j):
        c0, n, axis = SCATTER[j]
        cols = slice(c0, c0 + n)
        total = wide(Q[l, here[1 - axis], :, cols])
        for k in range(1, size[1 - axis]):
            s_second(l, j, k).wait()
            total = total + wide(GC[l, k - 1, :, cols])
        RF[l, :, cols] = total

    scale = HK**-0.5
    sub = lambda v, n: v[n * CH : (n + 1) * CH]

    def mixer_forward(l, h):
        r = of(h)
        qk = qkvg[l, r]
        b = cum[l, r]
        qd = low(qk[:, 0:128] * scale * jnp.exp(b))
        kd = low(qk[:, 128:256] * jnp.exp(-b))
        v = low(qk[:, 256:512])
        scores = low(jnp.where(allowed[r, r] > 0.0, dot_back(qd, kd), 0.0))
        amat[l, h] = scores
        within = dot(scores, v)
        ax = aux[r]
        out = []
        for e in range(HALF // CH):
            n = h * (HALF // CH) + e
            here_out = sub(within, e)
            if n > 0:
                here_out = here_out + sub(ax, e)[:, 0:1] * dot_back(sub(qd, e), low(states[l, n - 1]))
            out.append(here_out)
            if n < BLOCKS - 1:
                bn = sub(b, e)
                last = bn[CH - 1 : CH]
                kt = low(sub(qk, e)[:, 128:256] * jnp.exp(last - bn) * sub(ax, e)[:, 1:2])
                state = dot_grad(sub(v, e), kt)
                if n > 0:
                    state = state + sub(ax, e)[0:1, 2:3] * jnp.exp(last) * states[l, n - 1]
                states[l, n] = state
        attn[l, r] = jnp.concatenate(out, axis=0)

    def running(v, upper):
        row = lax.broadcasted_iota(jnp.int32, (HALF, HALF), 0)
        col = lax.broadcasted_iota(jnp.int32, (HALF, HALF), 1)
        order = (row <= col) if upper else (row >= col)
        tri = jnp.where(jnp.logical_and(order, row // CH == col // CH), 1.0, 0.0).astype(bf16)
        first = low(v)
        rest = v - wide(first)
        second = low(rest)
        third = low(rest - wide(second))
        return dot(tri, first) + (dot(tri, second) + dot(tri, third))

    def attention(l, h, i, x_ref):
        r = of(h)
        xin = wide(x_ref[r])
        nrm = low(xin * rms_scale(xin) * rows_of[l, 0:1])
        normed[l, r] = nrm
        qkvg[l, r] = dot(nrm, weight(l, QKVG))
        ranked = low(dot(nrm, weight(l, SMALL)))
        rank[l, r] = ranked
        pre = dot(ranked, rank_up[l]) + bias[l]
        soft = jnp.log1p(jnp.exp(-jnp.abs(pre)))
        slope[l, r] = jax.nn.sigmoid(-pre) / 16.0
        cum[l, r] = running((jnp.minimum(pre, 0.0) - soft) / 16.0, False)
        mixer_forward(l, h)
        at = attn[l, r]
        g = qkvg[l, r, 512:768]
        head = lax.rsqrt(jnp.mean(at * at, axis=-1, keepdims=True) + head_floor)
        both = low(at * head * gain[l] * g * jax.nn.sigmoid(g))
        mixed[l, r] = both
        sum_start(i, h, dot_back(both, weight(l, OUT)))

    def middle(l, h, i, x_ref):
        hidden = wide(x_ref[rows(t, h)]) + sum_wait(i, h)
        hid[l, h] = hidden
        share_start(i + 1, h, nm.at[l], hidden * rms_scale(hidden) * rows_of[l, 1:2])

    def feed(l, h, i):
        share_wait(i + 1, h, nm.at[l])
        r = of(h)
        acts = dot(nm[l, r], weight(l, GU))
        gu[l, r] = acts
        first = jax.nn.silu(acts[:, :FFM]) * acts[:, FFM : 2 * FFM]
        both = acts[:, 2 * FFM :]
        lane = lax.broadcasted_iota(jnp.int32, (HALF, 128), 1)
        last = jnp.where(lane < 64, jax.nn.silu(both) * pltpu.roll(both, 64, 1), 0.0)
        inner[l, r, :FFM] = low(first)
        inner[l, r, FFM:] = low(last)

    def forward_down(l, h, i):
        sum_start(i + 2, h, dot_back(inner[l, of(h)], weight(l, DOWN)))

    def forward_end(l, h, i, out_ref):
        share_start(i + 3, h, out_ref, hid[l, h] + sum_wait(i + 2, h))

    def silu_parts(v):
        sig = jax.nn.sigmoid(v)
        return v * sig, sig * (1.0 + v * (1.0 - sig))

    def put(part, left, right):
        c0, n = part
        step = D // X
        for a in range(X):
            G[a, :, :, :, c0 : c0 + n] = low(
                dot_grad(left[:, a * step : (a + 1) * step], right)
            ).reshape(Z, 2, H, n)

    def mixer_backward(l, h, dm):
        r = of(h)
        at = attn[l, r]
        g = qkvg[l, r, 512:768]
        head = lax.rsqrt(jnp.mean(at * at, axis=-1, keepdims=True) + head_floor)
        unit = at * head
        act, act_slope = silu_parts(g)
        dqkvg[r, 512:768] = low(dm * unit * gain[l] * act_slope)
        du = dm * act
        d_gain = jnp.sum(du * unit, axis=0, keepdims=True)
        w = du * gain[l]
        do = low(head * (w - unit * jnp.mean(w * unit, axis=-1, keepdims=True)))
        q, k = qkvg[l, r, 0:128], qkvg[l, r, 128:256]
        b = cum[l, r]
        grow, shrink = jnp.exp(b), jnp.exp(-b)
        qd = low(q * scale * grow)
        kd = low(k * shrink)
        v = low(qkvg[l, r, 256:512])
        d_scores = low(jnp.where(allowed[r, r] > 0.0, dot_back(do, v), 0.0))
        d_qd = dot(d_scores, kd)
        d_kd = dot_grad(d_scores, qd)
        d_v = dot_grad(amat[l, h], do)
        d_b = wide(qd) * d_qd - wide(kd) * d_kd
        d_k = d_kd * shrink
        ax = aux[r]
        per = HALF // CH
        out_q, out_k, out_v, out_b = [None] * per, [None] * per, [None] * per, [None] * per
        for e in reversed(range(per)):
            n = h * per + e
            dq_n, dk_n, dv_n, db_n = sub(d_qd, e), sub(d_k, e), sub(d_v, e), sub(d_b, e)
            if n < BLOCKS - 1:
                d_state = d_states[...]
                bn = sub(b, e)
                last = bn[CH - 1 : CH]
                fade = jnp.exp(last - bn) * sub(ax, e)[:, 1:2]
                kt = low(sub(k, e) * fade)
                d_low = low(d_state)
                d_kt = dot(sub(v, e), d_low)
                dv_n = dv_n + dot_back(kt, d_low)
                dk_n = dk_n + d_kt * fade
                moved = wide(kt) * d_kt
                db_n = db_n - moved
                d_last = jnp.sum(moved, axis=0, keepdims=True)
                if n > 0:
                    keep = sub(ax, e)[0:1, 2:3] * jnp.exp(last)
                    d_last = d_last + keep * jnp.sum(states[l, n - 1] * d_state, axis=0, keepdims=True)
                place = lax.broadcasted_iota(jnp.int32, (CH, HK), 0)
                db_n = db_n + jnp.where(place == CH - 1, d_last, 0.0)
            if n > 0:
                do_n = low(wide(sub(do, e)) * sub(ax, e)[:, 0:1])
                d_across = dot(do_n, low(states[l, n - 1]))
                dq_n = dq_n + d_across
                db_n = db_n + wide(sub(qd, e)) * d_across
                fresh = dot_grad(do_n, sub(qd, e))
                d_states[...] = fresh if n == BLOCKS - 1 else keep * d_state + fresh
            out_q[e], out_k[e], out_v[e], out_b[e] = dq_n, dk_n, dv_n, db_n
        dqkvg[r, 0:128] = low(jnp.concatenate(out_q, axis=0) * scale * grow)
        dqkvg[r, 128:256] = low(jnp.concatenate(out_k, axis=0))
        dqkvg[r, 256:512] = low(jnp.concatenate(out_v, axis=0))
        d_decay = running(jnp.concatenate(out_b, axis=0), True)
        d_pre[r] = low(d_decay * slope[l, r])
        return d_gain

    def feed_back(l, h, i, dy_ref):
        r = of(h)
        d_inner = dot(dy_ref[r], weight(l, DOWN))
        gate, up, both = gu[l, r, :FFM], gu[l, r, FFM : 2 * FFM], gu[l, r, 2 * FFM :]
        act, act_slope = silu_parts(gate)
        act_b, slope_b = silu_parts(both)
        rest = d_inner[:, FFM:]
        mix_b = rest * pltpu.roll(both, 64, 1) * slope_b + pltpu.roll(rest * act_b, 64, 1)
        part = jnp.concatenate(
            [low(d_inner[:, :FFM] * up * act_slope), low(d_inner[:, :FFM] * act), low(mix_b)], axis=1
        )
        d_gu[r] = part
        sum_start(i, h, dot_back(part, weight(l, GU)))

    def middle_back(l, h, i, dy_ref):
        d_mid = sum_wait(i, h)
        hidden = hid[l, h]
        scale_mid = rms_scale(hidden)
        unit = hidden * scale_mid
        small_rows[l, 1:2] += jnp.sum(d_mid * unit, axis=0, keepdims=True)
        scaled = d_mid * rows_of[l, 1:2]
        d_hidden = wide(dy_ref[rows(t, h)]) + scale_mid * (
            scaled - unit * jnp.mean(scaled * unit, axis=-1, keepdims=True)
        )
        d_hid[h] = d_hidden
        share_start(i + 1, h, dh, d_hidden)

    def attention_back(l, h, i, x_ref):
        r = of(h)
        share_wait(i + 1, h, dh)
        d_gain = mixer_backward(l, h, dot(dh[r], weight(l, OUT)))
        ranked = low(dot_back(d_pre[r], rank_up[l]))
        d_rank[r] = ranked
        partial = dot_back(dqkvg[r], weight(l, QKVG)) + dot_back(ranked, weight(l, SMALL))
        sum_start(i + 2, h, partial)
        xin = wide(x_ref[r])
        small_rows[l, 0:1] += jnp.sum(partial * (xin * rms_scale(xin)), axis=0, keepdims=True)
        return d_gain

    def backward_end(l, h, i, x_ref, out_ref):
        d_normed = sum_wait(i + 2, h)
        xin = wide(x_ref[rows(t, h)])
        scale_in = rms_scale(xin)
        unit = xin * scale_in
        scaled = d_normed * rows_of[l, 0:1]
        dx = d_hid[h] + scale_in * (scaled - unit * jnp.mean(scaled * unit, axis=-1, keepdims=True))
        share_start(i + 3, h, out_ref, dx)

    def small_copy(l, k):
        peer = (t + k) % T
        return remote(
            EG.at[l, :, :, peer], EB.at[l, k - 1], u_sem.at[l, 0, k - 1], u_sem.at[l, 1, k - 1], tensor=peer
        )

    def small_gradients(l, d_gain):
        rank_rows = downs((16, HV))
        at_gain = low(jnp.where(rank_rows == 2, d_gain, 0.0))
        d_bias = jnp.sum(wide(d_pre[...]), axis=0, keepdims=True)
        at_bias = low(jnp.where(downs((16, HK)) == 3, d_bias, 0.0))
        found = small_rows[l] + dot_back(at_gain, pick_gain[...]) + dot_back(at_bias, pick_bias[...])
        pick = low(jnp.where(lanes((16, 128)) == downs((16, 128)) + AT_IN, 1.0, 0.0))
        ups = dot_grad(rank[l], d_pre[...])
        right = lanes((128, 128)) >= 64
        every = (
            dot_grad(normed[l], d_rank[...])
            + dot_grad(low(found), pick)
            + dot_grad(pick_up[0], low(jnp.where(right, pltpu.roll(ups, 64, 1), 0.0)))
            + dot_grad(pick_up[1], low(jnp.where(right, ups, 0.0)))
        )
        EG[l] = low(every).reshape(X, Z, T, B, 128)
        for k in range(1, T):
            small_copy(l, k).start()

    def small_sum(l):
        total = wide(EG[l, :, :, t])
        for k in range(1, T):
            small_copy(l, k).wait()
            total = total + wide(EB[l, k - 1])
        EY[l] = low(total)

    small_swap_out = remote(EY.at[o], EO, v_sem.at[0, 0], v_sem.at[0, 1], section=o)

    def small_x(k):
        return remote(
            ES.at[(x + k) % X], EX.at[k - 1], v_sem.at[k, 0], v_sem.at[k, 1], dp=dp_peer(0, k)
        )

    def small_z(k):
        return remote(
            ES.at[x, (z + k) % Z], EZ.at[k - 1], v_sem.at[3 + k, 0], v_sem.at[3 + k, 1], dp=dp_peer(1, k)
        )

    def small_first():
        small_swap_out.wait()
        ES[...] = low(wide(EY[c]) + wide(EO[...]))
        for k in range(1, X):
            small_x(k).start()

    def small_second():
        total = wide(ES[x])
        for k in range(1, X):
            small_x(k).wait()
            total = total + wide(EX[k - 1])
        ES[x] = low(total)
        for k in range(1, Z):
            small_z(k).start()

    def small_third():
        total = wide(ES[x, z])
        for k in range(1, Z):
            small_z(k).wait()
            total = total + wide(EZ[k - 1])
        g_rank_down[0] = total[:, 0:G_RANK]
        turn = lanes((B, 128)) == downs((B, 128))
        for at, ref, n in (
            (AT_IN, g_norm_in, B),
            (AT_MID, g_norm_mid, B),
            (AT_GAIN, g_head_gain, n_gain),
            (AT_BIAS, g_rank_bias, n_bias),
        ):
            row = jnp.sum(jnp.where(turn, total[:, at : at + 1], 0.0), axis=0, keepdims=True)
            ref[...] = row[:, 0:n]
        turned = pltpu.roll(total[0:8], 64, 1)[0:1]
        g_rank_up[0] = jnp.where(lanes((1, 128)) < 64, turned, total[1:2])

    def backward(l, i, x_ref, dy_ref, out_ref, hooks):
        dy = dy_ref[...]
        d_inner = dot(dy, weight(l, DOWN))
        gate, up, both = gu[l, :, :FFM], gu[l, :, FFM : 2 * FFM], gu[l, :, 2 * FFM :]
        act, act_slope = silu_parts(gate)
        act_b, slope_b = silu_parts(both)
        rest = d_inner[:, FFM:]
        mix_b = rest * pltpu.roll(both, 64, 1) * slope_b + pltpu.roll(rest * act_b, 64, 1)
        d_gu = jnp.concatenate(
            [low(d_inner[:, :FFM] * up * act_slope), low(d_inner[:, :FFM] * act), low(mix_b)], axis=1
        )
        sum_start(i, dot_back(d_gu, weight(l, GU)))
        hooks[4]()
        put(DOWN, dy, inner[l])
        scatter_swap(l, 1)
        put(GU, nm[l], d_gu)
        scatter_swap(l, 0)
        hooks[0]()
        d_mid = sum_wait(i)
        hidden = hid[l]
        scale_mid = rms_scale(hidden)
        unit = hidden * scale_mid
        small_rows[l] = jnp.zeros((16, D), f32)
        small_rows[l, 1:2] = jnp.sum(d_mid * unit, axis=0, keepdims=True)
        scaled = d_mid * rows_of[l, 1:2]
        d_hidden = wide(dy_ref[rows(t)]) + scale_mid * (
            scaled - unit * jnp.mean(scaled * unit, axis=-1, keepdims=True)
        )
        d_hid[...] = d_hidden
        share_start(i + 1, dh, d_hidden)
        hooks[1]()
        share_wait(i + 1, dh)
        dmix[...] = dot(dh[...], weight(l, OUT))
        hooks[5]()
        d_pre, d_gain = mixer_backward(l)
        d_rank = low(dot_back(d_pre, rank_up[l]))
        partial = dot_back(dqkvg[...], weight(l, QKVG)) + dot_back(d_rank, weight(l, SMALL))
        hooks[6]()
        sum_start(i + 2, partial)
        xin = wide(x_ref[...])
        small_rows[l, 0:1] = jnp.sum(partial * (xin * rms_scale(xin)), axis=0, keepdims=True)
        hooks[2]()
        put(OUT, dh[...], mixed[l])
        scatter_swap(l, 2)
        put(QKVG, normed[l], dqkvg[...])
        scatter_swap(l, 3)
        scatter_swap(l, 4)
        small_gradients(l, d_rank, d_pre, d_gain)
        hooks[3]()
        d_normed = sum_wait(i + 2)
        xin = wide(x_ref[rows(t)])
        scale_in = rms_scale(xin)
        unit = xin * scale_in
        scaled = d_normed * rows_of[l, 0:1]
        dx = d_hid[...] + scale_in * (scaled - unit * jnp.mean(scaled * unit, axis=-1, keepdims=True))
        share_start(i + 3, out_ref, dx)

    early, late = (0, 1, 7, 2), (3, 4, 5, 6)

    def first_weights():
        prepare()
        got_w.wait_recv()
        keep_w.wait()
        for j in (0, 1, 2):
            gather_first(0, j)
        small_swap()
        got_e.wait_recv()
        keep_e.wait()
        gather_first(0, 7)
        for j in early:
            gather_second(0, j)
        for j in late:
            gather_first(0, j)
        for j in early:
            gather_third(0, j)
        for j in late:
            gather_second(0, j)

    def each(step, l, which):
        def run():
            for j in which:
                step(l, j)

        return run

    small_rows[...] = jnp.zeros_like(small_rows)
    got_x.wait_recv()
    keep_x.wait()
    everything = early + late
    ahead, back = (0, 1), (1, 0)
    x0, cot = xbuf.at[0], xbuf.at[1]

    first_weights()
    small_whole(0)
    for h in ahead:
        attention(0, h, 0, x0)
    each(gather_third, 0, late[:2])()
    for h in ahead:
        middle(0, h, 0, x0)
    each(gather_third, 0, late[2:])()
    each(gather_first, 1, everything)()
    for h in ahead:
        feed(0, h, 0)
        forward_down(0, h, 0)
    each(gather_second, 1, everything)()
    for h in ahead:
        forward_end(0, h, 0, x1)
    each(gather_third, 1, early)()
    small_whole(1)
    for h in ahead:
        share_wait(3, h, x1)
        attention(1, h, 4, x1)
    each(gather_third, 1, late)()
    for h in ahead:
        middle(1, h, 4, x1)
    for h in ahead:
        feed(1, h, 4)

    ff, mix = (0, 1), (2, 3, 4)
    for h in back:
        feed_back(1, h, 8, cot)
    for h in back:
        forward_down(1, h, 4)
    put(DOWN, cot[...], inner[1])
    scatter_swap(1, 1)
    for h in back:
        middle_back(1, h, 8, cot)
    put(GU, nm[1], d_gu[...])
    scatter_swap(1, 0)
    for h in back:
        forward_end(1, h, 4, res.at[1])
    d_gain = [attention_back(1, h, 8, x1) for h in back]
    each(scatter_first, 1, ff)()
    put(OUT, dh[...], mixed[1])
    scatter_swap(1, 2)
    put(QKVG, normed[1], dqkvg[...])
    scatter_swap(1, 3)
    scatter_swap(1, 4)
    for h in back:
        backward_end(1, h, 8, x1, dy0)
    small_gradients(1, d_gain[0] + d_gain[1])
    each(scatter_second, 1, ff)()
    for h in back:
        share_wait(11, h, dy0)
        feed_back(0, h, 12, dy0)
    each(scatter_first, 1, mix)()
    each(scatter_third, 1, ff)()
    put(DOWN, dy0[...], inner[0])
    scatter_swap(0, 1)
    for h in back:
        middle_back(0, h, 12, dy0)
    put(GU, nm[0], d_gu[...])
    scatter_swap(0, 0)
    each(scatter_second, 1, mix)()
    d_gain = [attention_back(0, h, 12, x0) for h in back]
    each(scatter_first, 0, ff)()
    put(OUT, dh[...], mixed[0])
    scatter_swap(0, 2)
    put(QKVG, normed[0], dqkvg[...])
    scatter_swap(0, 3)
    scatter_swap(0, 4)
    for h in back:
        backward_end(0, h, 12, x0, res.at[0])
    small_gradients(0, d_gain[0] + d_gain[1])
    small_sum(1)
    for h in back:
        share_wait(7, h, res.at[1])
    each(scatter_third, 1, mix)()
    each(scatter_second, 0, ff)()
    each(scatter_first, 0, mix)()
    small_sum(0)
    small_swap_out.start()
    for h in back:
        share_wait(15, h, res.at[0])
    each(scatter_third, 0, ff)()
    give_end = remote(res.at[o], ends.at[0, c], e_sem.at[0], e_sem.at[1], section=o)
    got_end = remote(res.at[o], ends.at[0, o], e_sem.at[0], e_sem.at[1], section=o)
    give_end.start()
    small_first()
    each(scatter_second, 0, mix)()
    small_second()
    ends[0, c] = res[c]
    each(scatter_third, 0, mix)()
    give_grad = remote(RF.at[o], og.at[c], e_sem.at[2], e_sem.at[3], section=o)
    got_grad = remote(RF.at[o], og.at[o], e_sem.at[2], e_sem.at[3], section=o)
    give_grad.start()
    og[c] = RF[c]
    got_end.wait_recv()
    small_third()
    got_grad.wait_recv()
    whole = lambda c0, n: og[:, :, c0 : c0 + n].reshape(R, n)
    g_query[0] = whole(0, 128)
    g_key[0] = whole(128, 128)
    g_value[0] = whole(256, 256)
    g_out_gate[0] = whole(512, 256)
    g_out[0] = whole(*OUT)
    g_gate[0, :, :FFM] = whole(GU[0], FFM)
    g_up[0, :, :FFM] = whole(GU[0] + FFM, FFM)
    both = whole(GU[0] + 2 * FFM, 128)
    g_gate[0, :, FFM:] = both[:, 0:64]
    g_up[0, :, FFM:] = pltpu.roll(both, 64, 1)[:, 0:64]
    g_down[0] = whole(*DOWN)[:, 0:FFD]
    give_end.wait_send()
    give_grad.wait_send()
    swap_w.wait_send()
    swap_x.wait_send()
    swap_e.wait_send()
    for k in range(1, T):
        tile_copy(k)[0].wait_send()
    for l in range(2):
        for j, (_, _, axis) in enumerate(GATHER):
            for k in range(1, size[axis]):
                w_first(l, j, k)[0].wait_send()
            for k in range(1, size[1 - axis]):
                w_second(l, j, k)[0].wait_send()
            w_third(l, j)[0].wait_send()


def on_device(X, Z, *operands):
    T = lax.axis_size("tensor")
    D = operands[0].shape[-1]
    R = operands[3].shape[1]
    H, TL, B, N = R // 2, TOK // T, R // T, X * Z
    top = max(X, Z)
    scratch = [
        pltpu.VMEM((2, X, Z, 2, H, WIDE), bf16),
        pltpu.VMEM((R, WIDE), bf16),
        pltpu.VMEM((T, B, 128), bf16),
        pltpu.VMEM((max(B, 8), 128), f32),
        pltpu.VMEM((D, HV), bf16),
        pltpu.VMEM((D, HK), bf16),
        pltpu.VMEM((2, 128, D), bf16),
        pltpu.VMEM((2, 16, D), f32),
        pltpu.VMEM((2, 1, HV), f32),
        pltpu.VMEM((2, 1, HK), f32),
        pltpu.VMEM((2, 128, HK), bf16),
        pltpu.VMEM((TOK, TOK), f32),
        pltpu.VMEM((TOK, 128), f32),
        pltpu.VMEM((2, TOK, D), bf16),
        pltpu.VMEM((TOK, D), bf16),
        pltpu.VMEM((2, TOK, D), bf16),
        pltpu.VMEM((2, TOK, D), bf16),
        pltpu.VMEM((2, TOK, 768), f32),
        pltpu.VMEM((2, TOK, HK), f32),
        pltpu.VMEM((2, TOK, HK), f32),
        pltpu.VMEM((2, 2, TOK // 2, TOK // 2), bf16),
        pltpu.VMEM((2, BLOCKS - 1, HV, HK), f32),
        pltpu.VMEM((2, TOK, HV), f32),
        pltpu.VMEM((2, TOK, HV), bf16),
        pltpu.VMEM((2, 2, TL // 2, D), f32),
        pltpu.VMEM((2, TL // 2, D), f32),
        pltpu.VMEM((2, TOK, GU[1]), f32),
        pltpu.VMEM((2, TOK, DOWN[1]), bf16),
        pltpu.VMEM((2, TOK, 128), bf16),
        pltpu.VMEM((TOK, D), bf16),
        pltpu.VMEM((TOK, D), bf16),
        pltpu.VMEM((2, TOK, D), bf16),
        pltpu.VMEM((2, TOK, D), bf16),
        pltpu.VMEM((3, 2, T - 1, TL // 2, D), bf16),
        pltpu.VMEM((X, Z, 2, H, SMALL[0]), bf16),
        pltpu.VMEM((2, X, Z, H, SMALL[0]), bf16),
        pltpu.VMEM((2, top - 1, top, H, SMALL[0]), bf16),
        pltpu.VMEM((2, top - 1, H, SMALL[0]), bf16),
        pltpu.VMEM((2, top, H, SMALL[0]), bf16),
        pltpu.VMEM((2, H, SMALL[0]), f32),
        pltpu.VMEM((2, H, SMALL[0]), f32),
        pltpu.VMEM((TOK, 768), bf16),
        pltpu.VMEM((TOK, GU[1]), bf16),
        pltpu.VMEM((TOK, 128), bf16),
        pltpu.VMEM((TOK, 128), bf16),
        pltpu.VMEM((HV, HK), f32),
        pltpu.VMEM((2, 16, D), f32),
        pltpu.VMEM((2, X, Z, T, B, 128), bf16),
        pltpu.VMEM((2, X, Z, B, 128), bf16),
        pltpu.VMEM((2, T - 1, X, Z, B, 128), bf16),
        pltpu.VMEM((X, Z, B, 128), bf16),
        pltpu.VMEM((X, Z, B, 128), bf16),
        pltpu.VMEM((X - 1, Z, B, 128), bf16),
        pltpu.VMEM((Z - 1, B, 128), bf16),
        pltpu.SemaphoreType.DMA((9,)),
        pltpu.SemaphoreType.DMA((2, len(GATHER), 7)),
        pltpu.SemaphoreType.DMA((2, len(GATHER), 7)),
        pltpu.SemaphoreType.DMA((16, 2, T - 1)),
        pltpu.SemaphoreType.DMA((16, 2, T - 1)),
        pltpu.SemaphoreType.DMA((2, len(SCATTER), 7)),
        pltpu.SemaphoreType.DMA((2, len(SCATTER), 7)),
        pltpu.SemaphoreType.DMA((4,)),
        pltpu.SemaphoreType.DMA((2, T - 1)),
        pltpu.SemaphoreType.DMA((2, 2, T - 1)),
        pltpu.SemaphoreType.DMA((7, 2)),
    ]
    flipped = lambda a: a.transpose(0, 2, 1)
    operands = list(operands)
    operands[11], operands[15] = flipped(operands[11]), flipped(operands[15])
    order = (2, 3, 4, 5, 6, 7, 8, 9, 10, 11, 12, 13, 14, 15)
    outs = (jax.ShapeDtypeStruct((1, 2, TOK, D), bf16),) + tuple(
        jax.ShapeDtypeStruct(operands[k].shape, f32) for k in order
    )
    vmem = pl.BlockSpec(memory_space=pltpu.VMEM)
    smem = pl.BlockSpec(memory_space=pltpu.SMEM)
    results = pl.pallas_call(
        functools.partial(kernel, X, Z, T),
        out_shape=outs,
        in_specs=[vmem, smem] + [vmem] * (len(operands) - 2),
        out_specs=(vmem,) * len(outs),
        scratch_shapes=scratch,
        compiler_params=pltpu.CompilerParams(
            collective_id=0, has_side_effects=True, vmem_limit_bytes=64 * 1024 * 1024 - 65536
        ),
    )(*operands)
    results = list(results)
    results[0] = results[0].astype(f32)
    results[10], results[14] = flipped(results[10]), flipped(results[14])
    return tuple(results)


def solution(mesh):
    count = mesh.shape["dp"]
    side = {16: 4, 4: 2}[count]
    in_specs = (
        P("section", None, "dp", None),
        P("dp", None),
        P("section", ("dp", "tensor")),
        P("section", "dp", "tensor"),
        P("section", "dp", "tensor"),
        P("section", "dp", "tensor"),
        P("section", "dp", "tensor"),
        P("section", ("dp", "tensor"), None),
        P("section", "dp", "tensor"),
        P("section", ("dp", "tensor")),
        P("section", ("dp", "tensor")),
        P("section", "tensor", "dp"),
        P("section", ("dp", "tensor")),
        P("section", "dp", "tensor"),
        P("section", "dp", "tensor"),
        P("section", "tensor", "dp"),
    )
    out_specs = (
        P("section", None, "dp", None),
        P("section", ("dp", "tensor")),
        P("section", "dp", "tensor"),
        P("section", "dp", "tensor"),
        P("section", "dp", "tensor"),
        P("section", "dp", "tensor"),
        P("section", ("dp", "tensor"), None),
        P("section", "dp", "tensor"),
        P("section", ("dp", "tensor")),
        P("section", ("dp", "tensor")),
        P("section", "tensor", "dp"),
        P("section", ("dp", "tensor")),
        P("section", "dp", "tensor"),
        P("section", "dp", "tensor"),
        P("section", "tensor", "dp"),
    )
    return jax.shard_map(
        functools.partial(on_device, side, count // side),
        mesh=mesh,
        in_specs=in_specs,
        out_specs=out_specs,
        check_vma=False,
    )
```

```python
import functools

import jax
import jax.numpy as jnp
from jax import lax
from jax.experimental import pallas as pl
from jax.experimental.pallas import tpu as pltpu
from jax.sharding import PartitionSpec as P

CH = 64
HK = 128
HV = 256
TOK = 256
BLOCKS = TOK // CH
FFD = 704
FFM = 640
QKVG = (0, 768)
QKV, GATES = (0, 512), (512, 256)
OUT = (768, 256)
GU = (1024, 1408)
DOWN = (2432, 768)
SMALL = (3200, 128)
WIDE = 3328
AT_IN, AT_MID, AT_GAIN, AT_BIAS = 16, 17, 18, 19
epsilon = 1e-06
head_floor = 1.0
MESH = pl.DeviceIdType.MESH
f32 = jnp.float32
bf16 = jnp.bfloat16

GATHER = (
    (0, 256, 0),
    (256, 256, 1),
    (3200, 128, 0),
    (512, 256, 0),
    (768, 256, 1),
    (1024, 640, 1),
    (1664, 768, 0),
    (2432, 384, 1),
    (2816, 384, 0),
)
SCATTER = (
    (1024, 640, 0),
    (1664, 768, 1),
    (2432, 384, 0),
    (2816, 384, 1),
    (768, 128, 0),
    (896, 128, 1),
    (0, 384, 0),
    (384, 384, 1),
)

def dot(a, b):
    return lax.dot_general(a, b, (((1,), (0,)), ((), ())), preferred_element_type=f32)


def dot_back(a, b):
    return lax.dot_general(a, b, (((1,), (1,)), ((), ())), preferred_element_type=f32)


def dot_grad(a, b):
    return lax.dot_general(a, b, (((0,), (0,)), ((), ())), preferred_element_type=f32)


def low(a):
    return a.astype(bf16)


def wide(a):
    return a.astype(f32)


def rms_scale(v):
    return lax.rsqrt(jnp.mean(v * v, axis=-1, keepdims=True) + epsilon)


def kernel(
    X,
    Z,
    T,
    pipe_in,
    doc_lengths,
    norm_in,
    w_query,
    w_key,
    w_value,
    w_out_gate,
    w_rank_down,
    w_rank_up,
    rank_bias,
    head_gain,
    w_out,
    norm_mid,
    w_gate,
    w_up,
    w_down,
    ends,
    og,
    small,
    W,
    shard,
    tiles,
    line,
    pick_gain,
    pick_bias,
    pick_up,
    rows_of,
    gain,
    bias,
    rank_up,
    allowed,
    aux,
    xbuf,
    x1,
    normed,
    nm,
    qkvg,
    cum,
    slope,
    amat,
    states,
    attn,
    mixed,
    hid,
    d_hid,
    gu,
    inner,
    rank,
    dh,
    dy0,
    res,
    pbuf,
    rbuf,
    G,
    GA,
    GB,
    GC,
    Q,
    RF,
    dqkvg,
    d_gu,
    d_pre,
    d_rank,
    d_states,
    small_rows,
    EG,
    EY,
    EB,
    ES,
    EO,
    EX,
    EZ,
    a_sem,
    gs,
    gr,
    ys,
    yr,
    ss,
    sr,
    e_sem,
    t_sem,
    u_sem,
    v_sem,
):
    c = lax.axis_index("section")
    d = lax.axis_index("dp")
    t = lax.axis_index("tensor")
    x, z = d // Z, d % Z
    o = 1 - c
    own = pipe_in.at[0]
    D = pipe_in.shape[-1]
    R = w_query.shape[1]
    B = R // T
    N = X * Z
    G_RANK = w_rank_down.shape[2]
    n_gain, n_bias = head_gain.shape[1], rank_bias.shape[1]
    H = R // 2
    HALF = TOK // 2
    S = HALF // T
    size = (X, Z)
    here = (x, z)

    def dp_peer(axis, k):
        if axis == 0:
            return ((x + k) % X) * Z + z
        return x * Z + (z + k) % Z

    def remote(src, dst, s, r, **device):
        return pltpu.make_async_remote_copy(
            src_ref=src, dst_ref=dst, send_sem=s, recv_sem=r, device_id=device, device_id_type=MESH
        )

    barrier = pltpu.get_barrier_semaphore()
    for k in range(1, X):
        pl.semaphore_signal(barrier, inc=1, device_id={"dp": dp_peer(0, k)}, device_id_type=MESH)
    for k in range(1, Z):
        pl.semaphore_signal(barrier, inc=1, device_id={"dp": dp_peer(1, k)}, device_id_type=MESH)
    for k in range(1, T):
        pl.semaphore_signal(barrier, inc=1, device_id={"tensor": (t + k) % T}, device_id_type=MESH)
    pl.semaphore_signal(barrier, inc=1, device_id={"section": o}, device_id_type=MESH)

    def lanes(shape):
        return lax.broadcasted_iota(jnp.int32, shape, len(shape) - 1)

    def downs(shape):
        return lax.broadcasted_iota(jnp.int32, shape, len(shape) - 2)

    def column(ref, n):
        line[...] = jnp.zeros_like(line)
        line[0:1, 0:n] = wide(ref[...])
        spread = jnp.broadcast_to(line[0:1, :], (B, 128))
        return jnp.sum(jnp.where(lanes((B, 128)) == downs((B, 128)), spread, 0.0), axis=1, keepdims=True)

    line[...] = jnp.zeros_like(line)
    line[0:B, 0:G_RANK] = wide(w_rank_down[0])
    tile = line[0:B, :]
    lane, down = lanes((B, 128)), downs((B, 128))
    for at, ref, n in (
        (AT_IN, norm_in, B),
        (AT_MID, norm_mid, B),
        (AT_GAIN, head_gain, n_gain),
        (AT_BIAS, rank_bias, n_bias),
    ):
        tile = jnp.where(lane == at, column(ref, n), tile)
    second = wide(w_rank_up[0])
    turned = pltpu.roll(jnp.broadcast_to(second, (8, 128)), 64, 1)[0:1]
    tile = jnp.where(jnp.logical_and(down == 0, lane >= 64), turned, tile)
    tile = jnp.where(jnp.logical_and(down == 1, lane >= 64), second, tile)
    tiles[t] = low(tile)

    def tile_copy(k):
        s, r = t_sem.at[0, k - 1], t_sem.at[1, k - 1]
        peer, source = (t + k) % T, (t - k) % T
        return remote(tiles.at[t], tiles.at[t], s, r, tensor=peer), remote(
            tiles.at[source], tiles.at[source], s, r, tensor=peer
        )

    MAIN = SMALL[0]
    shard[:, 0:128] = w_query[0]
    shard[:, 128:256] = w_key[0]
    shard[:, 256:512] = w_value[0]
    shard[:, 512:768] = w_out_gate[0]
    shard[:, 768:1024] = w_out[0]
    half = lambda h: pl.ds(pl.multiple_of(h * H, H), H)
    near, far = pl.ds(0, GU[0]), pl.ds(GU[0], MAIN - GU[0])
    extra = pl.ds(MAIN, SMALL[1])

    def swap(cols, at):
        s, r = a_sem.at[at], a_sem.at[at + 1]
        give = remote(shard.at[half(o), cols], W.at[c, x, z, o, :, cols], s, r, section=o)
        got = remote(shard.at[half(o), cols], W.at[o, x, z, c, :, cols], s, r, section=o)
        keep = pltpu.make_async_copy(shard.at[half(c), cols], W.at[c, x, z, c, :, cols], a_sem.at[at + 2])
        return give, got, keep

    swap_x = remote(own.at[o], xbuf.at[c], a_sem.at[9], a_sem.at[10], section=o)
    got_x = remote(own.at[o], xbuf.at[o], a_sem.at[9], a_sem.at[10], section=o)
    keep_x = pltpu.make_async_copy(own.at[c], xbuf.at[c], a_sem.at[11])
    swap_near, got_near, keep_near = swap(near, 0)
    swap_far, got_far, keep_far = swap(far, 3)
    swap_e, got_e, keep_e = swap(extra, 6)

    pl.semaphore_wait(barrier, X + Z + T - 2)
    for k in range(1, T):
        tile_copy(k)[0].start()
    swap_near.start()
    keep_near.start()
    shard[:, GU[0] : GU[0] + FFM] = w_gate[0, :, :FFM]
    shard[:, GU[0] + FFM : GU[0] + 2 * FFM] = w_up[0, :, :FFM]
    shard[:, GU[0] + 2 * FFM : GU[0] + GU[1]] = jnp.concatenate(
        [w_gate[0, :, FFM:], w_up[0, :, FFM:]], axis=1
    )
    shard[:, MAIN - 128 : MAIN] = jnp.zeros((R, 128), bf16)
    shard[:, DOWN[0] : DOWN[0] + FFD] = w_down[0]
    swap_far.start()
    keep_far.start()
    swap_x.start()
    keep_x.start()

    def small_swap():
        for k in range(1, T):
            tile_copy(k)[1].wait_recv()
        shard[:, MAIN:WIDE] = tiles[...].reshape(R, 128)
        swap_e.start()
        keep_e.start()

    def w_first(l, j, k):
        c0, n, axis = GATHER[j]
        at = W.at[l, x, z, c, :, pl.ds(c0, n)]
        if axis == 0:
            into = W.at[l, (x - k) % X, z, c, :, pl.ds(c0, n)]
        else:
            into = W.at[l, x, (z - k) % Z, c, :, pl.ds(c0, n)]
        s, r = gs.at[l, j, k - 1], gr.at[l, j, k - 1]
        return remote(at, at, s, r, dp=dp_peer(axis, k)), remote(into, into, s, r, dp=dp_peer(axis, k))

    def w_second(l, j, k):
        c0, n, axis = GATHER[j]
        cols = pl.ds(c0, n)
        if axis == 0:
            at, into = W.at[l, :, z, c, :, cols], W.at[l, :, (z - k) % Z, c, :, cols]
        else:
            at, into = W.at[l, x, :, c, :, cols], W.at[l, (x - k) % X, :, c, :, cols]
        s, r = gs.at[l, j, 2 + k], gr.at[l, j, 2 + k]
        return remote(at, at, s, r, dp=dp_peer(1 - axis, k)), remote(
            into, into, s, r, dp=dp_peer(1 - axis, k)
        )

    def w_third(l, j):
        c0, n, _ = GATHER[j]
        cols = pl.ds(c0, n)
        at, into = W.at[l, :, :, c, :, cols], W.at[l, :, :, o, :, cols]
        s, r = gs.at[l, j, 6], gr.at[l, j, 6]
        return remote(at, at, s, r, section=o), remote(into, into, s, r, section=o)

    def gather_first(l, j):
        for k in range(1, size[GATHER[j][2]]):
            w_first(l, j, k)[0].start()

    def gather_second(l, j):
        axis = GATHER[j][2]
        for k in range(1, size[axis]):
            w_first(l, j, k)[1].wait_recv()
        for k in range(1, size[1 - axis]):
            w_second(l, j, k)[0].start()

    def gather_third(l, j):
        axis = GATHER[j][2]
        for k in range(1, size[1 - axis]):
            w_second(l, j, k)[1].wait_recv()
        w_third(l, j)[0].start()

    arrived = set()

    def weight(l, part):
        c0, n = part
        for j, (g0, gn, _) in enumerate(GATHER):
            if g0 < c0 + n and c0 < g0 + gn and (l, j) not in arrived:
                arrived.add((l, j))
                w_third(l, j)[1].wait_recv()
        return W[l, :, :, :, :, c0 : c0 + n].reshape(D, n)

    def prepare():
        r, g = downs((D, HV)), lanes((D, HV))
        pick_gain[...] = low(
            jnp.where(jnp.logical_and(r % B < n_gain, r // B * n_gain + r % B == g), 1.0, 0.0)
        )
        r, g = downs((D, HK)), lanes((D, HK)) + t * HK
        pick_bias[...] = low(
            jnp.where(jnp.logical_and(r % B < n_bias, r // B * n_bias + r % B == g), 1.0, 0.0)
        )
        r, g = downs((128, D)), lanes((128, D))
        for i in range(2):
            pick_up[i] = low(jnp.where(g == r * R + t * B + i, 1.0, 0.0))
        bounds, total = [], 0
        for j in range(doc_lengths.shape[1]):
            total = total + doc_lengths[c, j]
            bounds.append(total)

        def segment(at):
            seg = jnp.zeros(at.shape, jnp.int32)
            for bound in bounds:
                seg = seg + jnp.where(bound <= at, 1, 0)
            return seg

        i, j = downs((TOK, TOK)), lanes((TOK, TOK))
        same = jnp.logical_and(i // CH == j // CH, segment(i) == segment(j))
        allowed[...] = jnp.where(jnp.logical_and(i >= j, same), 1.0, 0.0)
        i, lane = downs((TOK, 128)), lanes((TOK, 128))
        first = i // CH * CH
        seg, before, last = segment(i), segment(first - 1), segment(first + CH - 1)
        one = lambda v: jnp.where(v, 1.0, 0.0)
        aux[...] = jnp.where(
            lane == 0, one(seg == before), jnp.where(lane == 1, one(seg == last), one(last == before))
        )

    def small_whole(l):
        every = weight(l, SMALL)
        pick = low(jnp.where(lanes((16, 128)) == downs((16, 128)) + AT_IN, 1.0, 0.0))
        found = dot_back(pick, every)
        rows_of[l] = found
        gain[l] = dot(low(found), pick_gain[...])[2:3]
        bias[l] = dot(low(found), pick_bias[...])[3:4]
        first, second = dot(pick_up[0], every), dot(pick_up[1], every)
        rank_up[l] = low(jnp.where(lanes((128, 128)) < 64, pltpu.roll(first, 64, 1), second))

    def rows(p, h):
        return pl.ds(pl.multiple_of(h * HALF + p * S, S), S)

    def of(h):
        return slice(h * HALF, (h + 1) * HALF)

    def sum_copy(i, h, k):
        peer = (t + k) % T
        into = rbuf.at[2 if i == 6 else i // 2 % 2, h, k - 1]
        return remote(
            pbuf.at[i // 2 % 2, rows(peer, h)], into, ys.at[i, h, k - 1], yr.at[i, h, k - 1], tensor=peer
        )

    def sum_start(i, h, part):
        pbuf[i // 2 % 2, of(h)] = low(part)
        for k in range(1, T):
            sum_copy(i, h, k).start()

    def sum_wait(i, h):
        total = wide(pbuf[i // 2 % 2, rows(t, h)])
        for k in range(1, T):
            sum_copy(i, h, k).wait_recv()
            total = total + wide(rbuf[2 if i == 6 else i // 2 % 2, h, k - 1])
        for k in range(1, T):
            sum_copy(i, h, k).wait_send()
        return total

    def share_copy(i, h, ref, k):
        peer = (t + k) % T
        s, r = ys.at[i, h, k - 1], yr.at[i, h, k - 1]
        mine, into = ref.at[rows(t, h)], ref.at[rows((t - k) % T, h)]
        return remote(mine, mine, s, r, tensor=peer), remote(into, into, s, r, tensor=peer)

    def share_start(i, h, ref, value):
        ref[rows(t, h)] = low(value)
        for k in range(1, T):
            share_copy(i, h, ref, k)[0].start()

    def share_wait(i, h, ref):
        for k in range(1, T):
            share_copy(i, h, ref, k)[1].wait_recv()
        for k in range(1, T):
            share_copy(i, h, ref, k)[0].wait_send()

    def s_swap(l, j):
        c0, n, _ = SCATTER[j]
        cols = pl.ds(c0, n)
        return remote(
            G.at[:, :, o, :, cols], GA.at[l, :, :, :, cols], ss.at[l, j, 0], sr.at[l, j, 0], section=o
        )

    def s_first(l, j, k):
        c0, n, axis = SCATTER[j]
        cols = pl.ds(c0, n)
        src = G.at[(x + k) % X, :, c, :, cols] if axis == 0 else G.at[:, (z + k) % Z, c, :, cols]
        return remote(
            src, GB.at[l, k - 1, :, :, cols], ss.at[l, j, k], sr.at[l, j, k], dp=dp_peer(axis, k)
        )

    def s_second(l, j, k):
        c0, n, axis = SCATTER[j]
        cols = pl.ds(c0, n)
        place = (here[1 - axis] + k) % size[1 - axis]
        return remote(
            Q.at[l, place, :, cols],
            GC.at[l, k - 1, :, cols],
            ss.at[l, j, 3 + k],
            sr.at[l, j, 3 + k],
            dp=dp_peer(1 - axis, k),
        )

    def scatter_swap(l, j):
        s_swap(l, j).start()

    def scatter_first(l, j):
        c0, n, axis = SCATTER[j]
        s_swap(l, j).wait()
        for a in range(X):
            G[a, :, c, :, c0 : c0 + n] = G[a, :, c, :, c0 : c0 + n] + GA[l, a, :, :, c0 : c0 + n]
        for k in range(1, size[axis]):
            s_first(l, j, k).start()

    def scatter_second(l, j):
        c0, n, axis = SCATTER[j]
        cols = slice(c0, c0 + n)
        total = wide(G[x, :, c, :, cols] if axis == 0 else G[:, z, c, :, cols])
        for k in range(1, size[axis]):
            s_first(l, j, k).wait()
            total = total + wide(GB[l, k - 1, :, :, cols])
        Q[l, :, :, cols] = low(total)
        for k in range(1, size[1 - axis]):
            s_second(l, j, k).start()

    def scatter_third(l, j):
        c0, n, axis = SCATTER[j]
        cols = slice(c0, c0 + n)
        total = wide(Q[l, here[1 - axis], :, cols])
        for k in range(1, size[1 - axis]):
            s_second(l, j, k).wait()
            total = total + wide(GC[l, k - 1, :, cols])
        RF[l, :, cols] = total

    scale = HK**-0.5
    sub = lambda v, n: v[n * CH : (n + 1) * CH]

    def mixer_forward(l, h):
        r = of(h)
        qk = qkvg[l, r]
        b = cum[l, r]
        qd = low(qk[:, 0:128] * scale * jnp.exp(b))
        kd = low(qk[:, 128:256] * jnp.exp(-b))
        v = low(qk[:, 256:512])
        scores = low(jnp.where(allowed[r, r] > 0.0, dot_back(qd, kd), 0.0))
        amat[l, h] = scores
        within = dot(scores, v)
        ax = aux[r]
        out = []
        for e in range(HALF // CH):
            n = h * (HALF // CH) + e
            here_out = sub(within, e)
            if n > 0:
                here_out = here_out + sub(ax, e)[:, 0:1] * dot_back(sub(qd, e), low(states[l, n - 1]))
            out.append(here_out)
            if n < BLOCKS - 1:
                bn = sub(b, e)
                last = bn[CH - 1 : CH]
                kt = low(sub(qk, e)[:, 128:256] * jnp.exp(last - bn) * sub(ax, e)[:, 1:2])
                state = dot_grad(sub(v, e), kt)
                if n > 0:
                    state = state + sub(ax, e)[0:1, 2:3] * jnp.exp(last) * states[l, n - 1]
                states[l, n] = state
        attn[l, r] = jnp.concatenate(out, axis=0)

    def running(v, upper):
        row = lax.broadcasted_iota(jnp.int32, (HALF, HALF), 0)
        col = lax.broadcasted_iota(jnp.int32, (HALF, HALF), 1)
        order = (row <= col) if upper else (row >= col)
        tri = jnp.where(jnp.logical_and(order, row // CH == col // CH), 1.0, 0.0).astype(bf16)
        first = low(v)
        rest = v - wide(first)
        second = low(rest)
        third = low(rest - wide(second))
        return dot(tri, first) + (dot(tri, second) + dot(tri, third))

    def attention(l, h, i, x_ref, between=()):
        r = of(h)
        xin = wide(x_ref[r])
        nrm = low(xin * rms_scale(xin) * rows_of[l, 0:1])
        normed[l, r] = nrm
        qkvg[l, r, 0:512] = dot(nrm, weight(l, QKV))
        ranked = low(dot(nrm, weight(l, SMALL)))
        rank[l, r] = ranked
        pre = dot(ranked, rank_up[l]) + bias[l]
        soft = jnp.log1p(jnp.exp(-jnp.abs(pre)))
        slope[l, r] = jax.nn.sigmoid(-pre) / 16.0
        cum[l, r] = running((jnp.minimum(pre, 0.0) - soft) / 16.0, False)
        each(gather_third, l, between)()
        mixer_forward(l, h)
        at = attn[l, r]
        g = dot(nrm, weight(l, GATES))
        qkvg[l, r, 512:768] = g
        head = lax.rsqrt(jnp.mean(at * at, axis=-1, keepdims=True) + head_floor)
        both = low(at * head * gain[l] * g * jax.nn.sigmoid(g))
        mixed[l, r] = both
        sum_start(i, h, dot_back(both, weight(l, OUT)))

    def middle(l, h, i, x_ref):
        hidden = wide(x_ref[rows(t, h)]) + sum_wait(i, h)
        hid[l, h] = hidden
        share_start(i + 1, h, nm.at[l], hidden * rms_scale(hidden) * rows_of[l, 1:2])

    def feed(l, h, i):
        share_wait(i + 1, h, nm.at[l])
        r = of(h)
        acts = dot(nm[l, r], weight(l, GU))
        gu[l, r] = acts
        first = jax.nn.silu(acts[:, :FFM]) * acts[:, FFM : 2 * FFM]
        both = acts[:, 2 * FFM :]
        lane = lax.broadcasted_iota(jnp.int32, (HALF, 128), 1)
        last = jnp.where(lane < 64, jax.nn.silu(both) * pltpu.roll(both, 64, 1), 0.0)
        inner[l, r, :FFM] = low(first)
        inner[l, r, FFM:] = low(last)

    def forward_down(l, h, i):
        sum_start(i + 2, h, dot_back(inner[l, of(h)], weight(l, DOWN)))

    def forward_end(l, h, i, out_ref):
        share_start(i + 3, h, out_ref, hid[l, h] + sum_wait(i + 2, h))

    def silu_parts(v):
        sig = jax.nn.sigmoid(v)
        return v * sig, sig * (1.0 + v * (1.0 - sig))

    def put(part, left, right):
        c0, n = part
        step = D // X
        for a in range(X):
            G[a, :, :, :, c0 : c0 + n] = low(
                dot_grad(left[:, a * step : (a + 1) * step], right)
            ).reshape(Z, 2, H, n)

    def mixer_backward(l, h, dm):
        r = of(h)
        at = attn[l, r]
        g = qkvg[l, r, 512:768]
        head = lax.rsqrt(jnp.mean(at * at, axis=-1, keepdims=True) + head_floor)
        unit = at * head
        act, act_slope = silu_parts(g)
        dqkvg[r, 512:768] = low(dm * unit * gain[l] * act_slope)
        du = dm * act
        d_gain = jnp.sum(du * unit, axis=0, keepdims=True)
        w = du * gain[l]
        do = low(head * (w - unit * jnp.mean(w * unit, axis=-1, keepdims=True)))
        q, k = qkvg[l, r, 0:128], qkvg[l, r, 128:256]
        b = cum[l, r]
        grow, shrink = jnp.exp(b), jnp.exp(-b)
        qd = low(q * scale * grow)
        kd = low(k * shrink)
        v = low(qkvg[l, r, 256:512])
        d_scores = low(jnp.where(allowed[r, r] > 0.0, dot_back(do, v), 0.0))
        d_qd = dot(d_scores, kd)
        d_kd = dot_grad(d_scores, qd)
        d_v = dot_grad(amat[l, h], do)
        d_b = wide(qd) * d_qd - wide(kd) * d_kd
        d_k = d_kd * shrink
        ax = aux[r]
        per = HALF // CH
        out_q, out_k, out_v, out_b = [None] * per, [None] * per, [None] * per, [None] * per
        for e in reversed(range(per)):
            n = h * per + e
            dq_n, dk_n, dv_n, db_n = sub(d_qd, e), sub(d_k, e), sub(d_v, e), sub(d_b, e)
            if n < BLOCKS - 1:
                d_state = d_states[...]
                bn = sub(b, e)
                last = bn[CH - 1 : CH]
                fade = jnp.exp(last - bn) * sub(ax, e)[:, 1:2]
                kt = low(sub(k, e) * fade)
                d_low = low(d_state)
                d_kt = dot(sub(v, e), d_low)
                dv_n = dv_n + dot_back(kt, d_low)
                dk_n = dk_n + d_kt * fade
                moved = wide(kt) * d_kt
                db_n = db_n - moved
                d_last = jnp.sum(moved, axis=0, keepdims=True)
                if n > 0:
                    keep = sub(ax, e)[0:1, 2:3] * jnp.exp(last)
                    d_last = d_last + keep * jnp.sum(states[l, n - 1] * d_state, axis=0, keepdims=True)
                place = lax.broadcasted_iota(jnp.int32, (CH, HK), 0)
                db_n = db_n + jnp.where(place == CH - 1, d_last, 0.0)
            if n > 0:
                do_n = low(wide(sub(do, e)) * sub(ax, e)[:, 0:1])
                d_across = dot(do_n, low(states[l, n - 1]))
                dq_n = dq_n + d_across
                db_n = db_n + wide(sub(qd, e)) * d_across
                fresh = dot_grad(do_n, sub(qd, e))
                d_states[...] = fresh if n == BLOCKS - 1 else keep * d_state + fresh
            out_q[e], out_k[e], out_v[e], out_b[e] = dq_n, dk_n, dv_n, db_n
        dqkvg[r, 0:128] = low(jnp.concatenate(out_q, axis=0) * scale * grow)
        dqkvg[r, 128:256] = low(jnp.concatenate(out_k, axis=0))
        dqkvg[r, 256:512] = low(jnp.concatenate(out_v, axis=0))
        d_decay = running(jnp.concatenate(out_b, axis=0), True)
        d_pre[r] = low(d_decay * slope[l, r])
        return d_gain

    def feed_back(l, h, i, dy_ref):
        r = of(h)
        d_inner = dot(dy_ref[r], weight(l, DOWN))
        gate, up, both = gu[l, r, :FFM], gu[l, r, FFM : 2 * FFM], gu[l, r, 2 * FFM :]
        act, act_slope = silu_parts(gate)
        act_b, slope_b = silu_parts(both)
        rest = d_inner[:, FFM:]
        mix_b = rest * pltpu.roll(both, 64, 1) * slope_b + pltpu.roll(rest * act_b, 64, 1)
        part = jnp.concatenate(
            [low(d_inner[:, :FFM] * up * act_slope), low(d_inner[:, :FFM] * act), low(mix_b)], axis=1
        )
        d_gu[r] = part
        sum_start(i, h, dot_back(part, weight(l, GU)))

    def middle_back(l, h, i, dy_ref):
        d_mid = sum_wait(i, h)
        hidden = hid[l, h]
        scale_mid = rms_scale(hidden)
        unit = hidden * scale_mid
        small_rows[l, 1:2] += jnp.sum(d_mid * unit, axis=0, keepdims=True)
        scaled = d_mid * rows_of[l, 1:2]
        d_hidden = wide(dy_ref[rows(t, h)]) + scale_mid * (
            scaled - unit * jnp.mean(scaled * unit, axis=-1, keepdims=True)
        )
        d_hid[h] = d_hidden
        share_start(i + 1, h, dh, d_hidden)

    def attention_back(l, h, i, x_ref):
        r = of(h)
        share_wait(i + 1, h, dh)
        d_gain = mixer_backward(l, h, dot(dh[r], weight(l, OUT)))
        ranked = low(dot_back(d_pre[r], rank_up[l]))
        d_rank[r] = ranked
        partial = dot_back(dqkvg[r], weight(l, QKVG)) + dot_back(ranked, weight(l, SMALL))
        sum_start(i + 2, h, partial)
        xin = wide(x_ref[r])
        small_rows[l, 0:1] += jnp.sum(partial * (xin * rms_scale(xin)), axis=0, keepdims=True)
        return d_gain

    def backward_end(l, h, i, x_ref, out_ref):
        d_normed = sum_wait(i + 2, h)
        xin = wide(x_ref[rows(t, h)])
        scale_in = rms_scale(xin)
        unit = xin * scale_in
        scaled = d_normed * rows_of[l, 0:1]
        dx = d_hid[h] + scale_in * (scaled - unit * jnp.mean(scaled * unit, axis=-1, keepdims=True))
        share_start(i + 3, h, out_ref, dx)

    def small_copy(l, k):
        peer = (t + k) % T
        return remote(
            EG.at[l, :, :, peer], EB.at[l, k - 1], u_sem.at[l, 0, k - 1], u_sem.at[l, 1, k - 1], tensor=peer
        )

    def small_gradients(l, d_gain):
        rank_rows = downs((16, HV))
        at_gain = low(jnp.where(rank_rows == 2, d_gain, 0.0))
        d_bias = jnp.sum(wide(d_pre[...]), axis=0, keepdims=True)
        at_bias = low(jnp.where(downs((16, HK)) == 3, d_bias, 0.0))
        found = small_rows[l] + dot_back(at_gain, pick_gain[...]) + dot_back(at_bias, pick_bias[...])
        pick = low(jnp.where(lanes((16, 128)) == downs((16, 128)) + AT_IN, 1.0, 0.0))
        ups = dot_grad(rank[l], d_pre[...])
        right = lanes((128, 128)) >= 64
        every = (
            dot_grad(normed[l], d_rank[...])
            + dot_grad(low(found), pick)
            + dot_grad(pick_up[0], low(jnp.where(right, pltpu.roll(ups, 64, 1), 0.0)))
            + dot_grad(pick_up[1], low(jnp.where(right, ups, 0.0)))
        )
        EG[l] = low(every).reshape(X, Z, T, B, 128)
        for k in range(1, T):
            small_copy(l, k).start()

    def small_sum(l):
        total = wide(EG[l, :, :, t])
        for k in range(1, T):
            small_copy(l, k).wait()
            total = total + wide(EB[l, k - 1])
        EY[l] = low(total)

    small_swap_out = remote(EY.at[o], EO, v_sem.at[0, 0], v_sem.at[0, 1], section=o)

    def small_x(k):
        return remote(
            ES.at[(x + k) % X], EX.at[k - 1], v_sem.at[k, 0], v_sem.at[k, 1], dp=dp_peer(0, k)
        )

    def small_z(k):
        return remote(
            ES.at[x, (z + k) % Z], EZ.at[k - 1], v_sem.at[3 + k, 0], v_sem.at[3 + k, 1], dp=dp_peer(1, k)
        )

    def small_first():
        small_swap_out.wait()
        ES[...] = EY[c] + EO[...]
        for k in range(1, X):
            small_x(k).start()

    def small_second():
        total = wide(ES[x])
        for k in range(1, X):
            small_x(k).wait()
            total = total + wide(EX[k - 1])
        ES[x] = low(total)
        for k in range(1, Z):
            small_z(k).start()

    def small_third():
        total = wide(ES[x, z])
        for k in range(1, Z):
            small_z(k).wait()
            total = total + wide(EZ[k - 1])
        small[...] = total

    def backward(l, i, x_ref, dy_ref, out_ref, hooks):
        dy = dy_ref[...]
        d_inner = dot(dy, weight(l, DOWN))
        gate, up, both = gu[l, :, :FFM], gu[l, :, FFM : 2 * FFM], gu[l, :, 2 * FFM :]
        act, act_slope = silu_parts(gate)
        act_b, slope_b = silu_parts(both)
        rest = d_inner[:, FFM:]
        mix_b = rest * pltpu.roll(both, 64, 1) * slope_b + pltpu.roll(rest * act_b, 64, 1)
        d_gu = jnp.concatenate(
            [low(d_inner[:, :FFM] * up * act_slope), low(d_inner[:, :FFM] * act), low(mix_b)], axis=1
        )
        sum_start(i, dot_back(d_gu, weight(l, GU)))
        hooks[4]()
        put(DOWN, dy, inner[l])
        scatter_swap(l, 1)
        put(GU, nm[l], d_gu)
        scatter_swap(l, 0)
        hooks[0]()
        d_mid = sum_wait(i)
        hidden = hid[l]
        scale_mid = rms_scale(hidden)
        unit = hidden * scale_mid
        small_rows[l] = jnp.zeros((16, D), f32)
        small_rows[l, 1:2] = jnp.sum(d_mid * unit, axis=0, keepdims=True)
        scaled = d_mid * rows_of[l, 1:2]
        d_hidden = wide(dy_ref[rows(t)]) + scale_mid * (
            scaled - unit * jnp.mean(scaled * unit, axis=-1, keepdims=True)
        )
        d_hid[...] = d_hidden
        share_start(i + 1, dh, d_hidden)
        hooks[1]()
        share_wait(i + 1, dh)
        dmix[...] = dot(dh[...], weight(l, OUT))
        hooks[5]()
        d_pre, d_gain = mixer_backward(l)
        d_rank = low(dot_back(d_pre, rank_up[l]))
        partial = dot_back(dqkvg[...], weight(l, QKVG)) + dot_back(d_rank, weight(l, SMALL))
        hooks[6]()
        sum_start(i + 2, partial)
        xin = wide(x_ref[...])
        small_rows[l, 0:1] = jnp.sum(partial * (xin * rms_scale(xin)), axis=0, keepdims=True)
        hooks[2]()
        put(OUT, dh[...], mixed[l])
        scatter_swap(l, 2)
        put(QKVG, normed[l], dqkvg[...])
        scatter_swap(l, 3)
        scatter_swap(l, 4)
        small_gradients(l, d_rank, d_pre, d_gain)
        hooks[3]()
        d_normed = sum_wait(i + 2)
        xin = wide(x_ref[rows(t)])
        scale_in = rms_scale(xin)
        unit = xin * scale_in
        scaled = d_normed * rows_of[l, 0:1]
        dx = d_hid[...] + scale_in * (scaled - unit * jnp.mean(scaled * unit, axis=-1, keepdims=True))
        share_start(i + 3, out_ref, dx)

    first_in, mid, late = (0, 1, 2), (3, 4), (5, 6, 7, 8)
    early = first_in + mid

    def first_weights():
        got_near.wait_recv()
        keep_near.wait()
        for j in (0, 1):
            gather_first(0, j)
        small_swap()
        got_e.wait_recv()
        keep_e.wait()
        gather_first(0, 2)
        for j in mid:
            gather_first(0, j)
        prepare()
        for j in early:
            gather_second(0, j)
        got_far.wait_recv()
        keep_far.wait()
        for j in late:
            gather_first(0, j)
        for j in first_in:
            gather_third(0, j)
        for j in late:
            gather_second(0, j)
        for j in early:
            gather_first(1, j)

    def each(step, l, which):
        def run():
            for j in which:
                step(l, j)

        return run

    small_rows[...] = jnp.zeros_like(small_rows)
    everything = early + late
    ahead, back = (0, 1), (1, 0)
    x0, cot = xbuf.at[0], xbuf.at[1]

    first_weights()
    small_whole(0)
    got_x.wait_recv()
    keep_x.wait()
    attention(0, 0, 0, x0, mid)
    attention(0, 1, 0, x0)
    middle(0, 0, 0, x0)
    each(gather_third, 0, late[:2])()
    middle(0, 1, 0, x0)
    each(gather_third, 0, late[2:])()
    each(gather_second, 1, early)()
    each(gather_first, 1, late)()
    for h in ahead:
        feed(0, h, 0)
        forward_down(0, h, 0)
    each(gather_third, 1, early)()
    each(gather_second, 1, late)()
    for h in ahead:
        forward_end(0, h, 0, x1)
    small_whole(1)
    for h in ahead:
        share_wait(3, h, x1)
        attention(1, h, 4, x1)
    each(gather_third, 1, late)()
    for h in ahead:
        middle(1, h, 4, x1)
    for h in ahead:
        feed(1, h, 4)

    of_gu, of_down, of_out, of_qkvg = (0, 1), (2, 3), (4, 5), (6, 7)
    ff, mix = of_down + of_gu, of_out + of_qkvg
    for h in back:
        feed_back(1, h, 8, cot)
    for h in back:
        forward_down(1, h, 4)
    put(DOWN, cot[...], inner[1])
    each(scatter_swap, 1, of_down)()
    for h in back:
        middle_back(1, h, 8, cot)
    put(GU, nm[1], d_gu[...])
    each(scatter_swap, 1, of_gu)()
    for h in back:
        forward_end(1, h, 4, res.at[1])
    d_gain = [attention_back(1, h, 8, x1) for h in back]
    each(scatter_first, 1, ff)()
    put(OUT, dh[...], mixed[1])
    each(scatter_swap, 1, of_out)()
    put(QKVG, normed[1], dqkvg[...])
    each(scatter_swap, 1, of_qkvg)()
    for h in back:
        backward_end(1, h, 8, x1, dy0)
    small_gradients(1, d_gain[0] + d_gain[1])
    each(scatter_second, 1, ff)()
    for h in back:
        share_wait(11, h, dy0)
        feed_back(0, h, 12, dy0)
    each(scatter_first, 1, mix)()
    each(scatter_third, 1, ff)()
    put(DOWN, dy0[...], inner[0])
    each(scatter_swap, 0, of_down)()
    put(GU, nm[0], d_gu[...])
    each(scatter_swap, 0, of_gu)()
    for h in back:
        middle_back(0, h, 12, dy0)
    each(scatter_second, 1, mix)()
    each(scatter_first, 0, ff)()
    d_gain = [attention_back(0, 1, 12, x0)]
    d_gain.append(attention_back(0, 0, 12, x0))
    put(QKVG, normed[0], dqkvg[...])
    each(scatter_swap, 0, of_qkvg)()
    put(OUT, dh[...], mixed[0])
    each(scatter_swap, 0, of_out)()
    small_gradients(0, d_gain[0] + d_gain[1])
    each(scatter_first, 0, of_qkvg + of_out)()
    for h in back:
        backward_end(0, h, 12, x0, res.at[0])
    each(scatter_second, 0, ff)()
    small_sum(1)
    small_sum(0)
    small_swap_out.start()
    for h in back:
        share_wait(7, h, res.at[1])
    each(scatter_third, 1, mix)()
    for h in back:
        share_wait(15, h, res.at[0])
    give_end = remote(res.at[o], ends.at[0, c], e_sem.at[0], e_sem.at[1], section=o)
    got_end = remote(res.at[o], ends.at[0, o], e_sem.at[0], e_sem.at[1], section=o)
    give_end.start()
    each(scatter_second, 0, mix)()
    small_first()
    ends[0, c] = res[c]
    each(scatter_third, 0, ff)()
    small_second()
    each(scatter_third, 0, mix)()
    give_grad = remote(RF.at[o], og.at[c], e_sem.at[2], e_sem.at[3], section=o)
    got_grad = remote(RF.at[o], og.at[o], e_sem.at[2], e_sem.at[3], section=o)
    give_grad.start()
    og[c] = RF[c]
    got_end.wait_recv()
    small_third()
    got_grad.wait_recv()
    give_end.wait_send()
    give_grad.wait_send()
    swap_near.wait_send()
    swap_far.wait_send()
    swap_x.wait_send()
    swap_e.wait_send()
    for k in range(1, T):
        tile_copy(k)[0].wait_send()
    for l in range(2):
        for j, (_, _, axis) in enumerate(GATHER):
            for k in range(1, size[axis]):
                w_first(l, j, k)[0].wait_send()
            for k in range(1, size[1 - axis]):
                w_second(l, j, k)[0].wait_send()
            w_third(l, j)[0].wait_send()


def unpack(
    packed_ends,
    og,
    small,
    ends,
    g_norm_in,
    g_query,
    g_key,
    g_value,
    g_out_gate,
    g_rank_down,
    g_rank_up,
    g_rank_bias,
    g_head_gain,
    g_out,
    g_norm_mid,
    g_gate,
    g_up,
    g_down,
):
    R, B = 2 * og.shape[1], small.shape[0]
    ends[...] = wide(packed_ends[...])
    whole = lambda c0, n: og[:, :, c0 : c0 + n].reshape(R, n)
    g_query[0] = whole(0, 128)
    g_key[0] = whole(128, 128)
    g_value[0] = whole(256, 256)
    g_out_gate[0] = whole(512, 256)
    g_out[0] = whole(*OUT)
    g_gate[0, :, :FFM] = whole(GU[0], FFM)
    g_up[0, :, :FFM] = whole(GU[0] + FFM, FFM)
    both = whole(GU[0] + 2 * FFM, 128)
    g_gate[0, :, FFM:] = both[:, 0:64]
    g_up[0, :, FFM:] = pltpu.roll(both, 64, 1)[:, 0:64]
    g_down[0] = whole(*DOWN)[:, 0:FFD]
    total = small[...]
    g_rank_down[0] = total[:, 0 : g_rank_down.shape[2]]
    lane = lax.broadcasted_iota(jnp.int32, (B, 128), 1)
    turn = lane == lax.broadcasted_iota(jnp.int32, (B, 128), 0)
    for at, ref in (
        (AT_IN, g_norm_in),
        (AT_MID, g_norm_mid),
        (AT_GAIN, g_head_gain),
        (AT_BIAS, g_rank_bias),
    ):
        row = jnp.sum(jnp.where(turn, total[:, at : at + 1], 0.0), axis=0, keepdims=True)
        ref[...] = row[:, 0 : ref.shape[1]]
    turned = pltpu.roll(total[0:8], 64, 1)[0:1]
    g_rank_up[0] = jnp.where(lane[0:1] < 64, turned, total[1:2])


def on_device(X, Z, *operands):
    T = lax.axis_size("tensor")
    D = operands[0].shape[-1]
    R = operands[3].shape[1]
    H, TL, B, N = R // 2, TOK // T, R // T, X * Z
    top = max(X, Z)
    scratch = [
        pltpu.VMEM((2, X, Z, 2, H, WIDE), bf16),
        pltpu.VMEM((R, WIDE), bf16),
        pltpu.VMEM((T, B, 128), bf16),
        pltpu.VMEM((max(B, 8), 128), f32),
        pltpu.VMEM((D, HV), bf16),
        pltpu.VMEM((D, HK), bf16),
        pltpu.VMEM((2, 128, D), bf16),
        pltpu.VMEM((2, 16, D), f32),
        pltpu.VMEM((2, 1, HV), f32),
        pltpu.VMEM((2, 1, HK), f32),
        pltpu.VMEM((2, 128, HK), bf16),
        pltpu.VMEM((TOK, TOK), f32),
        pltpu.VMEM((TOK, 128), f32),
        pltpu.VMEM((2, TOK, D), bf16),
        pltpu.VMEM((TOK, D), bf16),
        pltpu.VMEM((2, TOK, D), bf16),
        pltpu.VMEM((2, TOK, D), bf16),
        pltpu.VMEM((2, TOK, 768), f32),
        pltpu.VMEM((2, TOK, HK), f32),
        pltpu.VMEM((2, TOK, HK), f32),
        pltpu.VMEM((2, 2, TOK // 2, TOK // 2), bf16),
        pltpu.VMEM((2, BLOCKS - 1, HV, HK), f32),
        pltpu.VMEM((2, TOK, HV), f32),
        pltpu.VMEM((2, TOK, HV), bf16),
        pltpu.VMEM((2, 2, TL // 2, D), f32),
        pltpu.VMEM((2, TL // 2, D), f32),
        pltpu.VMEM((2, TOK, GU[1]), f32),
        pltpu.VMEM((2, TOK, DOWN[1]), bf16),
        pltpu.VMEM((2, TOK, 128), bf16),
        pltpu.VMEM((TOK, D), bf16),
        pltpu.VMEM((TOK, D), bf16),
        pltpu.VMEM((2, TOK, D), bf16),
        pltpu.VMEM((2, TOK, D), bf16),
        pltpu.VMEM((3, 2, T - 1, TL // 2, D), bf16),
        pltpu.VMEM((X, Z, 2, H, SMALL[0]), bf16),
        pltpu.VMEM((2, X, Z, H, SMALL[0]), bf16),
        pltpu.VMEM((2, top - 1, top, H, SMALL[0]), bf16),
        pltpu.VMEM((2, top - 1, H, SMALL[0]), bf16),
        pltpu.VMEM((2, top, H, SMALL[0]), bf16),
        pltpu.VMEM((2, H, SMALL[0]), f32),
        pltpu.VMEM((TOK, 768), bf16),
        pltpu.VMEM((TOK, GU[1]), bf16),
        pltpu.VMEM((TOK, 128), bf16),
        pltpu.VMEM((TOK, 128), bf16),
        pltpu.VMEM((HV, HK), f32),
        pltpu.VMEM((2, 16, D), f32),
        pltpu.VMEM((2, X, Z, T, B, 128), bf16),
        pltpu.VMEM((2, X, Z, B, 128), bf16),
        pltpu.VMEM((2, T - 1, X, Z, B, 128), bf16),
        pltpu.VMEM((X, Z, B, 128), bf16),
        pltpu.VMEM((X, Z, B, 128), bf16),
        pltpu.VMEM((X - 1, Z, B, 128), bf16),
        pltpu.VMEM((Z - 1, B, 128), bf16),
        pltpu.SemaphoreType.DMA((12,)),
        pltpu.SemaphoreType.DMA((2, len(GATHER), 7)),
        pltpu.SemaphoreType.DMA((2, len(GATHER), 7)),
        pltpu.SemaphoreType.DMA((16, 2, T - 1)),
        pltpu.SemaphoreType.DMA((16, 2, T - 1)),
        pltpu.SemaphoreType.DMA((2, len(SCATTER), 7)),
        pltpu.SemaphoreType.DMA((2, len(SCATTER), 7)),
        pltpu.SemaphoreType.DMA((4,)),
        pltpu.SemaphoreType.DMA((2, T - 1)),
        pltpu.SemaphoreType.DMA((2, 2, T - 1)),
        pltpu.SemaphoreType.DMA((7, 2)),
    ]
    flipped = lambda a: a.transpose(0, 2, 1)
    operands = list(operands)
    operands[11], operands[15] = flipped(operands[11]), flipped(operands[15])
    vmem = pl.BlockSpec(memory_space=pltpu.VMEM)
    smem = pl.BlockSpec(memory_space=pltpu.SMEM)
    packed = pl.pallas_call(
        functools.partial(kernel, X, Z, T),
        out_shape=(
            jax.ShapeDtypeStruct((1, 2, TOK, D), bf16),
            jax.ShapeDtypeStruct((2, H, SMALL[0]), f32),
            jax.ShapeDtypeStruct((B, 128), f32),
        ),
        in_specs=[vmem, smem] + [vmem] * (len(operands) - 2),
        out_specs=(vmem,) * 3,
        scratch_shapes=scratch,
        compiler_params=pltpu.CompilerParams(
            collective_id=0, has_side_effects=True, vmem_limit_bytes=64 * 1024 * 1024 - 65536
        ),
    )(*operands)
    outs = (jax.ShapeDtypeStruct((1, 2, TOK, D), f32),) + tuple(
        jax.ShapeDtypeStruct(operands[k].shape, f32) for k in range(2, 16)
    )
    results = list(
        pl.pallas_call(
            unpack,
            out_shape=outs,
            in_specs=[vmem] * 3,
            out_specs=(vmem,) * len(outs),
            compiler_params=pltpu.CompilerParams(vmem_limit_bytes=32 * 1024 * 1024),
        )(*packed)
    )
    results[10], results[14] = flipped(results[10]), flipped(results[14])
    return tuple(results)


def solution(mesh):
    count = mesh.shape["dp"]
    side = {16: 4, 4: 2}[count]
    in_specs = (
        P("section", None, "dp", None),
        P("dp", None),
        P("section", ("dp", "tensor")),
        P("section", "dp", "tensor"),
        P("section", "dp", "tensor"),
        P("section", "dp", "tensor"),
        P("section", "dp", "tensor"),
        P("section", ("dp", "tensor"), None),
        P("section", "dp", "tensor"),
        P("section", ("dp", "tensor")),
        P("section", ("dp", "tensor")),
        P("section", "tensor", "dp"),
        P("section", ("dp", "tensor")),
        P("section", "dp", "tensor"),
        P("section", "dp", "tensor"),
        P("section", "tensor", "dp"),
    )
    out_specs = (
        P("section", None, "dp", None),
        P("section", ("dp", "tensor")),
        P("section", "dp", "tensor"),
        P("section", "dp", "tensor"),
        P("section", "dp", "tensor"),
        P("section", "dp", "tensor"),
        P("section", ("dp", "tensor"), None),
        P("section", "dp", "tensor"),
        P("section", ("dp", "tensor")),
        P("section", ("dp", "tensor")),
        P("section", "tensor", "dp"),
        P("section", ("dp", "tensor")),
        P("section", "dp", "tensor"),
        P("section", "dp", "tensor"),
        P("section", "tensor", "dp"),
    )
    return jax.shard_map(
        functools.partial(on_device, side, count // side),
        mesh=mesh,
        in_specs=in_specs,
        out_specs=out_specs,
        check_vma=False,
    )
```

```python
import functools

import jax
import jax.numpy as jnp
from jax import lax
from jax.experimental import pallas as pl
from jax.experimental.pallas import tpu as pltpu
from jax.sharding import PartitionSpec as P

CH = 64
HK = 128
HV = 256
TOK = 256
BLOCKS = TOK // CH
FFD = 704
FFM = 640
QKVG = (0, 768)
QKV, GATES = (0, 512), (512, 256)
OUT = (768, 256)
GU = (1024, 1408)
DOWN = (2432, 768)
SMALL = (3200, 128)
WIDE = 3328
AT_IN, AT_MID, AT_GAIN, AT_BIAS = 16, 17, 18, 19
epsilon = 1e-06
head_floor = 1.0
MESH = pl.DeviceIdType.MESH
f32 = jnp.float32
bf16 = jnp.bfloat16

GATHER = (
    (0, 256, 0),
    (256, 256, 1),
    (3200, 128, 0),
    (512, 256, 0),
    (768, 256, 1),
    (1024, 640, 1),
    (1664, 768, 0),
    (2432, 384, 1),
    (2816, 384, 0),
)
SCATTER = (
    (1024, 640, 0),
    (1664, 768, 1),
    (2432, 384, 0),
    (2816, 384, 1),
    (768, 128, 0),
    (896, 128, 1),
    (0, 384, 0),
    (384, 384, 1),
)

def dot(a, b):
    return lax.dot_general(a, b, (((1,), (0,)), ((), ())), preferred_element_type=f32)


def dot_back(a, b):
    return lax.dot_general(a, b, (((1,), (1,)), ((), ())), preferred_element_type=f32)


def dot_grad(a, b):
    return lax.dot_general(a, b, (((0,), (0,)), ((), ())), preferred_element_type=f32)


def low(a):
    return a.astype(bf16)


def wide(a):
    return a.astype(f32)


def rms_scale(v):
    return lax.rsqrt(jnp.mean(v * v, axis=-1, keepdims=True) + epsilon)


def kernel(
    X,
    Z,
    T,
    pipe_in,
    doc_lengths,
    norm_in,
    w_query,
    w_key,
    w_value,
    w_out_gate,
    w_rank_down,
    w_rank_up,
    rank_bias,
    head_gain,
    w_out,
    norm_mid,
    w_gate,
    w_up,
    w_down,
    ends,
    og,
    small,
    W,
    shard,
    tiles,
    line,
    pick_gain,
    pick_bias,
    pick_up,
    rows_of,
    gain,
    bias,
    rank_up,
    allowed,
    aux,
    xbuf,
    x1,
    normed,
    nm,
    qkvg,
    cum,
    slope,
    amat,
    states,
    attn,
    mixed,
    hid,
    d_hid,
    gu,
    inner,
    rank,
    dh,
    dy0,
    res,
    pbuf,
    rbuf,
    G,
    GA,
    GB,
    GC,
    Q,
    RF,
    dqkvg,
    d_gu,
    d_pre,
    d_rank,
    d_states,
    small_rows,
    EG,
    EY,
    EB,
    ES,
    EO,
    EX,
    EZ,
    a_sem,
    gs,
    gr,
    ys,
    yr,
    ss,
    sr,
    e_sem,
    t_sem,
    u_sem,
    v_sem,
):
    c = lax.axis_index("section")
    d = lax.axis_index("dp")
    t = lax.axis_index("tensor")
    x, z = d // Z, d % Z
    o = 1 - c
    own = pipe_in.at[0]
    D = pipe_in.shape[-1]
    R = w_query.shape[1]
    B = R // T
    N = X * Z
    G_RANK = w_rank_down.shape[2]
    n_gain, n_bias = head_gain.shape[1], rank_bias.shape[1]
    H = R // 2
    HALF = TOK // 2
    S = HALF // T
    size = (X, Z)
    here = (x, z)

    def dp_peer(axis, k):
        if axis == 0:
            return ((x + k) % X) * Z + z
        return x * Z + (z + k) % Z

    def remote(src, dst, s, r, **device):
        return pltpu.make_async_remote_copy(
            src_ref=src, dst_ref=dst, send_sem=s, recv_sem=r, device_id=device, device_id_type=MESH
        )

    barrier = pltpu.get_barrier_semaphore()
    for k in range(1, X):
        pl.semaphore_signal(barrier, inc=1, device_id={"dp": dp_peer(0, k)}, device_id_type=MESH)
    for k in range(1, Z):
        pl.semaphore_signal(barrier, inc=1, device_id={"dp": dp_peer(1, k)}, device_id_type=MESH)
    for k in range(1, T):
        pl.semaphore_signal(barrier, inc=1, device_id={"tensor": (t + k) % T}, device_id_type=MESH)
    pl.semaphore_signal(barrier, inc=1, device_id={"section": o}, device_id_type=MESH)

    def lanes(shape):
        return lax.broadcasted_iota(jnp.int32, shape, len(shape) - 1)

    def downs(shape):
        return lax.broadcasted_iota(jnp.int32, shape, len(shape) - 2)

    def column(ref, n):
        line[...] = jnp.zeros_like(line)
        line[0:1, 0:n] = wide(ref[...])
        spread = jnp.broadcast_to(line[0:1, :], (B, 128))
        return jnp.sum(jnp.where(lanes((B, 128)) == downs((B, 128)), spread, 0.0), axis=1, keepdims=True)

    line[...] = jnp.zeros_like(line)
    line[0:B, 0:G_RANK] = wide(w_rank_down[0])
    tile = line[0:B, :]
    lane, down = lanes((B, 128)), downs((B, 128))
    for at, ref, n in (
        (AT_IN, norm_in, B),
        (AT_MID, norm_mid, B),
        (AT_GAIN, head_gain, n_gain),
        (AT_BIAS, rank_bias, n_bias),
    ):
        tile = jnp.where(lane == at, column(ref, n), tile)
    second = wide(w_rank_up[0])
    turned = pltpu.roll(jnp.broadcast_to(second, (8, 128)), 64, 1)[0:1]
    tile = jnp.where(jnp.logical_and(down == 0, lane >= 64), turned, tile)
    tile = jnp.where(jnp.logical_and(down == 1, lane >= 64), second, tile)
    tiles[t] = low(tile)

    def tile_copy(k):
        s, r = t_sem.at[0, k - 1], t_sem.at[1, k - 1]
        peer, source = (t + k) % T, (t - k) % T
        return remote(tiles.at[t], tiles.at[t], s, r, tensor=peer), remote(
            tiles.at[source], tiles.at[source], s, r, tensor=peer
        )

    MAIN = SMALL[0]
    shard[:, 0:128] = w_query[0]
    shard[:, 128:256] = w_key[0]
    shard[:, 256:512] = w_value[0]
    shard[:, 512:768] = w_out_gate[0]
    shard[:, 768:1024] = w_out[0]
    half = lambda h: pl.ds(pl.multiple_of(h * H, H), H)
    near, far = pl.ds(0, GU[0]), pl.ds(GU[0], MAIN - GU[0])
    extra = pl.ds(MAIN, SMALL[1])

    def swap(cols, at):
        s, r = a_sem.at[at], a_sem.at[at + 1]
        give = remote(shard.at[half(o), cols], W.at[c, x, z, o, :, cols], s, r, section=o)
        got = remote(shard.at[half(o), cols], W.at[o, x, z, c, :, cols], s, r, section=o)
        keep = pltpu.make_async_copy(shard.at[half(c), cols], W.at[c, x, z, c, :, cols], a_sem.at[at + 2])
        return give, got, keep

    swap_x = remote(own.at[o], xbuf.at[c], a_sem.at[9], a_sem.at[10], section=o)
    got_x = remote(own.at[o], xbuf.at[o], a_sem.at[9], a_sem.at[10], section=o)
    keep_x = pltpu.make_async_copy(own.at[c], xbuf.at[c], a_sem.at[11])
    swap_near, got_near, keep_near = swap(near, 0)
    swap_far, got_far, keep_far = swap(far, 3)
    swap_e, got_e, keep_e = swap(extra, 6)

    pl.semaphore_wait(barrier, X + Z + T - 2)
    for k in range(1, T):
        tile_copy(k)[0].start()
    swap_near.start()
    keep_near.start()
    shard[:, GU[0] : GU[0] + FFM] = w_gate[0, :, :FFM]
    shard[:, GU[0] + FFM : GU[0] + 2 * FFM] = w_up[0, :, :FFM]
    shard[:, GU[0] + 2 * FFM : GU[0] + GU[1]] = jnp.concatenate(
        [w_gate[0, :, FFM:], w_up[0, :, FFM:]], axis=1
    )
    shard[:, MAIN - 128 : MAIN] = jnp.zeros((R, 128), bf16)
    shard[:, DOWN[0] : DOWN[0] + FFD] = w_down[0]
    swap_far.start()
    keep_far.start()
    swap_x.start()
    keep_x.start()

    def small_swap():
        for k in range(1, T):
            tile_copy(k)[1].wait_recv()
        shard[:, MAIN:WIDE] = tiles[...].reshape(R, 128)
        swap_e.start()
        keep_e.start()

    def w_first(l, j, k):
        c0, n, axis = GATHER[j]
        at = W.at[l, x, z, c, :, pl.ds(c0, n)]
        if axis == 0:
            into = W.at[l, (x - k) % X, z, c, :, pl.ds(c0, n)]
        else:
            into = W.at[l, x, (z - k) % Z, c, :, pl.ds(c0, n)]
        s, r = gs.at[l, j, k - 1], gr.at[l, j, k - 1]
        return remote(at, at, s, r, dp=dp_peer(axis, k)), remote(into, into, s, r, dp=dp_peer(axis, k))

    def w_second(l, j, k):
        c0, n, axis = GATHER[j]
        cols = pl.ds(c0, n)
        if axis == 0:
            at, into = W.at[l, :, z, c, :, cols], W.at[l, :, (z - k) % Z, c, :, cols]
        else:
            at, into = W.at[l, x, :, c, :, cols], W.at[l, (x - k) % X, :, c, :, cols]
        s, r = gs.at[l, j, 2 + k], gr.at[l, j, 2 + k]
        return remote(at, at, s, r, dp=dp_peer(1 - axis, k)), remote(
            into, into, s, r, dp=dp_peer(1 - axis, k)
        )

    def w_third(l, j):
        c0, n, _ = GATHER[j]
        cols = pl.ds(c0, n)
        at, into = W.at[l, :, :, c, :, cols], W.at[l, :, :, o, :, cols]
        s, r = gs.at[l, j, 6], gr.at[l, j, 6]
        return remote(at, at, s, r, section=o), remote(into, into, s, r, section=o)

    def gather_first(l, j):
        for k in range(1, size[GATHER[j][2]]):
            w_first(l, j, k)[0].start()

    def gather_second(l, j):
        axis = GATHER[j][2]
        for k in range(1, size[axis]):
            w_first(l, j, k)[1].wait_recv()
        for k in range(1, size[1 - axis]):
            w_second(l, j, k)[0].start()

    def gather_third(l, j):
        axis = GATHER[j][2]
        for k in range(1, size[1 - axis]):
            w_second(l, j, k)[1].wait_recv()
        w_third(l, j)[0].start()

    arrived = set()

    def weight(l, part):
        c0, n = part
        for j, (g0, gn, _) in enumerate(GATHER):
            if g0 < c0 + n and c0 < g0 + gn and (l, j) not in arrived:
                arrived.add((l, j))
                w_third(l, j)[1].wait_recv()
        return W[l, :, :, :, :, c0 : c0 + n].reshape(D, n)

    def prepare():
        r, g = downs((D, HV)), lanes((D, HV))
        pick_gain[...] = low(
            jnp.where(jnp.logical_and(r % B < n_gain, r // B * n_gain + r % B == g), 1.0, 0.0)
        )
        r, g = downs((D, HK)), lanes((D, HK)) + t * HK
        pick_bias[...] = low(
            jnp.where(jnp.logical_and(r % B < n_bias, r // B * n_bias + r % B == g), 1.0, 0.0)
        )
        r, g = downs((128, D)), lanes((128, D))
        for i in range(2):
            pick_up[i] = low(jnp.where(g == r * R + t * B + i, 1.0, 0.0))
        bounds, total = [], 0
        for j in range(doc_lengths.shape[1]):
            total = total + doc_lengths[c, j]
            bounds.append(total)

        def segment(at):
            seg = jnp.zeros(at.shape, jnp.int32)
            for bound in bounds:
                seg = seg + jnp.where(bound <= at, 1, 0)
            return seg

        i, j = downs((TOK, TOK)), lanes((TOK, TOK))
        same = jnp.logical_and(i // CH == j // CH, segment(i) == segment(j))
        allowed[...] = jnp.where(jnp.logical_and(i >= j, same), 1.0, 0.0)
        i, lane = downs((TOK, 128)), lanes((TOK, 128))
        first = i // CH * CH
        seg, before, last = segment(i), segment(first - 1), segment(first + CH - 1)
        one = lambda v: jnp.where(v, 1.0, 0.0)
        aux[...] = jnp.where(
            lane == 0, one(seg == before), jnp.where(lane == 1, one(seg == last), one(last == before))
        )

    def small_whole(l):
        every = weight(l, SMALL)
        pick = low(jnp.where(lanes((16, 128)) == downs((16, 128)) + AT_IN, 1.0, 0.0))
        found = dot_back(pick, every)
        rows_of[l] = found
        gain[l] = dot(low(found), pick_gain[...])[2:3]
        bias[l] = dot(low(found), pick_bias[...])[3:4]
        first, second = dot(pick_up[0], every), dot(pick_up[1], every)
        rank_up[l] = low(jnp.where(lanes((128, 128)) < 64, pltpu.roll(first, 64, 1), second))

    def rows(p, h):
        return pl.ds(pl.multiple_of(h * HALF + p * S, S), S)

    def of(h):
        return slice(h * HALF, (h + 1) * HALF)

    def slot(i):
        return 2 if i == 6 else i // 2 % 2

    def sum_copy(i, h, k):
        peer = (t + k) % T
        into = rbuf.at[slot(i), h, k - 1]
        return remote(
            pbuf.at[slot(i), rows(peer, h)], into, ys.at[i, h, k - 1], yr.at[i, h, k - 1], tensor=peer
        )

    far_first = sorted(range(1, T), key=lambda k: -min(k, T - k))

    def sum_start(i, h, part):
        pbuf[slot(i), of(h)] = low(part)
        for k in far_first:
            sum_copy(i, h, k).start()

    def sum_wait(i, h):
        total = wide(pbuf[slot(i), rows(t, h)])
        for k in range(1, T):
            sum_copy(i, h, k).wait_recv()
            total = total + wide(rbuf[slot(i), h, k - 1])
        for k in range(1, T):
            sum_copy(i, h, k).wait_send()
        return total

    def share_copy(i, h, ref, k):
        peer = (t + k) % T
        s, r = ys.at[i, h, k - 1], yr.at[i, h, k - 1]
        mine, into = ref.at[rows(t, h)], ref.at[rows((t - k) % T, h)]
        return remote(mine, mine, s, r, tensor=peer), remote(into, into, s, r, tensor=peer)

    def share_start(i, h, ref, value):
        ref[rows(t, h)] = low(value)
        for k in far_first:
            share_copy(i, h, ref, k)[0].start()

    def share_wait(i, h, ref):
        for k in range(1, T):
            share_copy(i, h, ref, k)[1].wait_recv()
        for k in range(1, T):
            share_copy(i, h, ref, k)[0].wait_send()

    def s_swap(l, j):
        c0, n, _ = SCATTER[j]
        cols = pl.ds(c0, n)
        return remote(
            G.at[:, :, o, :, cols], GA.at[l, :, :, :, cols], ss.at[l, j, 0], sr.at[l, j, 0], section=o
        )

    def s_first(l, j, k):
        c0, n, axis = SCATTER[j]
        cols = pl.ds(c0, n)
        src = G.at[(x + k) % X, :, c, :, cols] if axis == 0 else G.at[:, (z + k) % Z, c, :, cols]
        return remote(
            src, GB.at[l, k - 1, :, :, cols], ss.at[l, j, k], sr.at[l, j, k], dp=dp_peer(axis, k)
        )

    def s_second(l, j, k):
        c0, n, axis = SCATTER[j]
        cols = pl.ds(c0, n)
        place = (here[1 - axis] + k) % size[1 - axis]
        return remote(
            Q.at[l, place, :, cols],
            GC.at[l, k - 1, :, cols],
            ss.at[l, j, 3 + k],
            sr.at[l, j, 3 + k],
            dp=dp_peer(1 - axis, k),
        )

    def scatter_swap(l, j):
        s_swap(l, j).start()

    def scatter_first(l, j):
        c0, n, axis = SCATTER[j]
        s_swap(l, j).wait()
        for a in range(X):
            G[a, :, c, :, c0 : c0 + n] = G[a, :, c, :, c0 : c0 + n] + GA[l, a, :, :, c0 : c0 + n]
        for k in range(1, size[axis]):
            s_first(l, j, k).start()

    def scatter_second(l, j):
        c0, n, axis = SCATTER[j]
        cols = slice(c0, c0 + n)
        total = wide(G[x, :, c, :, cols] if axis == 0 else G[:, z, c, :, cols])
        for k in range(1, size[axis]):
            s_first(l, j, k).wait()
            total = total + wide(GB[l, k - 1, :, :, cols])
        Q[l, :, :, cols] = low(total)
        for k in range(1, size[1 - axis]):
            s_second(l, j, k).start()

    def scatter_third(l, j):
        c0, n, axis = SCATTER[j]
        cols = slice(c0, c0 + n)
        total = wide(Q[l, here[1 - axis], :, cols])
        for k in range(1, size[1 - axis]):
            s_second(l, j, k).wait()
            total = total + wide(GC[l, k - 1, :, cols])
        RF[l, :, cols] = total

    scale = HK**-0.5
    sub = lambda v, n: v[n * CH : (n + 1) * CH]

    def mixer_forward(l, h):
        r = of(h)
        qk = qkvg[l, r]
        b = cum[l, r]
        qd = low(qk[:, 0:128] * scale * jnp.exp(b))
        kd = low(qk[:, 128:256] * jnp.exp(-b))
        v = low(qk[:, 256:512])
        scores = low(jnp.where(allowed[r, r] > 0.0, dot_back(qd, kd), 0.0))
        amat[l, h] = scores
        within = dot(scores, v)
        ax = aux[r]
        out = []
        for e in range(HALF // CH):
            n = h * (HALF // CH) + e
            here_out = sub(within, e)
            if n > 0:
                here_out = here_out + sub(ax, e)[:, 0:1] * dot_back(sub(qd, e), low(states[l, n - 1]))
            out.append(here_out)
            if n < BLOCKS - 1:
                bn = sub(b, e)
                last = bn[CH - 1 : CH]
                kt = low(sub(qk, e)[:, 128:256] * jnp.exp(last - bn) * sub(ax, e)[:, 1:2])
                state = dot_grad(sub(v, e), kt)
                if n > 0:
                    state = state + sub(ax, e)[0:1, 2:3] * jnp.exp(last) * states[l, n - 1]
                states[l, n] = state
        attn[l, r] = jnp.concatenate(out, axis=0)

    def running(v, upper):
        row = lax.broadcasted_iota(jnp.int32, (HALF, HALF), 0)
        col = lax.broadcasted_iota(jnp.int32, (HALF, HALF), 1)
        order = (row <= col) if upper else (row >= col)
        tri = jnp.where(jnp.logical_and(order, row // CH == col // CH), 1.0, 0.0).astype(bf16)
        first = low(v)
        rest = v - wide(first)
        return dot(tri, first) + dot(tri, low(rest))

    def attention(l, h, i, x_ref, between=()):
        r = of(h)
        xin = wide(x_ref[r])
        nrm = low(xin * rms_scale(xin) * rows_of[l, 0:1])
        normed[l, r] = nrm
        qkvg[l, r, 0:512] = dot(nrm, weight(l, QKV))
        ranked = low(dot(nrm, weight(l, SMALL)))
        rank[l, r] = ranked
        pre = dot(ranked, rank_up[l]) + bias[l]
        soft = jnp.log1p(jnp.exp(-jnp.abs(pre)))
        slope[l, r] = jax.nn.sigmoid(-pre) / 16.0
        cum[l, r] = running((jnp.minimum(pre, 0.0) - soft) / 16.0, False)
        each(gather_third, l, between)()
        mixer_forward(l, h)
        at = attn[l, r]
        g = dot(nrm, weight(l, GATES))
        qkvg[l, r, 512:768] = g
        head = lax.rsqrt(jnp.mean(at * at, axis=-1, keepdims=True) + head_floor)
        both = low(at * head * gain[l] * g * jax.nn.sigmoid(g))
        mixed[l, r] = both
        sum_start(i, h, dot_back(both, weight(l, OUT)))

    def middle(l, h, i, x_ref):
        hidden = wide(x_ref[rows(t, h)]) + sum_wait(i, h)
        hid[l, h] = hidden
        share_start(i + 1, h, nm.at[l], hidden * rms_scale(hidden) * rows_of[l, 1:2])

    def feed(l, h, i):
        share_wait(i + 1, h, nm.at[l])
        r = of(h)
        acts = dot(nm[l, r], weight(l, GU))
        gu[l, r] = acts
        first = jax.nn.silu(acts[:, :FFM]) * acts[:, FFM : 2 * FFM]
        both = acts[:, 2 * FFM :]
        lane = lax.broadcasted_iota(jnp.int32, (HALF, 128), 1)
        last = jnp.where(lane < 64, jax.nn.silu(both) * pltpu.roll(both, 64, 1), 0.0)
        inner[l, r, :FFM] = low(first)
        inner[l, r, FFM:] = low(last)

    def forward_down(l, h, i):
        sum_start(i + 2, h, dot_back(inner[l, of(h)], weight(l, DOWN)))

    def forward_end(l, h, i, out_ref):
        share_start(i + 3, h, out_ref, hid[l, h] + sum_wait(i + 2, h))

    def silu_parts(v):
        sig = jax.nn.sigmoid(v)
        return v * sig, sig * (1.0 + v * (1.0 - sig))

    def put(part, left, right):
        c0, n = part
        step = D // X
        for a in range(X):
            G[a, :, :, :, c0 : c0 + n] = low(
                dot_grad(left[:, a * step : (a + 1) * step], right)
            ).reshape(Z, 2, H, n)

    def mixer_backward(l, h, dm):
        r = of(h)
        at = attn[l, r]
        g = qkvg[l, r, 512:768]
        head = lax.rsqrt(jnp.mean(at * at, axis=-1, keepdims=True) + head_floor)
        unit = at * head
        act, act_slope = silu_parts(g)
        dqkvg[r, 512:768] = low(dm * unit * gain[l] * act_slope)
        du = dm * act
        d_gain = jnp.sum(du * unit, axis=0, keepdims=True)
        w = du * gain[l]
        do = low(head * (w - unit * jnp.mean(w * unit, axis=-1, keepdims=True)))
        q, k = qkvg[l, r, 0:128], qkvg[l, r, 128:256]
        b = cum[l, r]
        grow, shrink = jnp.exp(b), jnp.exp(-b)
        qd = low(q * scale * grow)
        kd = low(k * shrink)
        v = low(qkvg[l, r, 256:512])
        d_scores = low(jnp.where(allowed[r, r] > 0.0, dot_back(do, v), 0.0))
        d_qd = dot(d_scores, kd)
        d_kd = dot_grad(d_scores, qd)
        d_v = dot_grad(amat[l, h], do)
        d_b = wide(qd) * d_qd - wide(kd) * d_kd
        d_k = d_kd * shrink
        ax = aux[r]
        per = HALF // CH
        out_q, out_k, out_v, out_b = [None] * per, [None] * per, [None] * per, [None] * per
        for e in reversed(range(per)):
            n = h * per + e
            dq_n, dk_n, dv_n, db_n = sub(d_qd, e), sub(d_k, e), sub(d_v, e), sub(d_b, e)
            if n < BLOCKS - 1:
                d_state = d_states[...]
                bn = sub(b, e)
                last = bn[CH - 1 : CH]
                fade = jnp.exp(last - bn) * sub(ax, e)[:, 1:2]
                kt = low(sub(k, e) * fade)
                d_low = low(d_state)
                d_kt = dot(sub(v, e), d_low)
                dv_n = dv_n + dot_back(kt, d_low)
                dk_n = dk_n + d_kt * fade
                moved = wide(kt) * d_kt
                db_n = db_n - moved
                d_last = jnp.sum(moved, axis=0, keepdims=True)
                if n > 0:
                    keep = sub(ax, e)[0:1, 2:3] * jnp.exp(last)
                    d_last = d_last + keep * jnp.sum(states[l, n - 1] * d_state, axis=0, keepdims=True)
                place = lax.broadcasted_iota(jnp.int32, (CH, HK), 0)
                db_n = db_n + jnp.where(place == CH - 1, d_last, 0.0)
            if n > 0:
                do_n = low(wide(sub(do, e)) * sub(ax, e)[:, 0:1])
                d_across = dot(do_n, low(states[l, n - 1]))
                dq_n = dq_n + d_across
                db_n = db_n + wide(sub(qd, e)) * d_across
                fresh = dot_grad(do_n, sub(qd, e))
                d_states[...] = fresh if n == BLOCKS - 1 else keep * d_state + fresh
            out_q[e], out_k[e], out_v[e], out_b[e] = dq_n, dk_n, dv_n, db_n
        dqkvg[r, 0:128] = low(jnp.concatenate(out_q, axis=0) * scale * grow)
        dqkvg[r, 128:256] = low(jnp.concatenate(out_k, axis=0))
        dqkvg[r, 256:512] = low(jnp.concatenate(out_v, axis=0))
        d_decay = running(jnp.concatenate(out_b, axis=0), True)
        d_pre[r] = low(d_decay * slope[l, r])
        return d_gain

    def feed_back(l, h, i, dy_ref):
        r = of(h)
        d_inner = dot(dy_ref[r], weight(l, DOWN))
        gate, up, both = gu[l, r, :FFM], gu[l, r, FFM : 2 * FFM], gu[l, r, 2 * FFM :]
        act, act_slope = silu_parts(gate)
        act_b, slope_b = silu_parts(both)
        rest = d_inner[:, FFM:]
        mix_b = rest * pltpu.roll(both, 64, 1) * slope_b + pltpu.roll(rest * act_b, 64, 1)
        part = jnp.concatenate(
            [low(d_inner[:, :FFM] * up * act_slope), low(d_inner[:, :FFM] * act), low(mix_b)], axis=1
        )
        d_gu[r] = part
        sum_start(i, h, dot_back(part, weight(l, GU)))

    def middle_back(l, h, i, dy_ref):
        d_mid = sum_wait(i, h)
        hidden = hid[l, h]
        scale_mid = rms_scale(hidden)
        unit = hidden * scale_mid
        small_rows[l, 1:2] += jnp.sum(d_mid * unit, axis=0, keepdims=True)
        scaled = d_mid * rows_of[l, 1:2]
        d_hidden = wide(dy_ref[rows(t, h)]) + scale_mid * (
            scaled - unit * jnp.mean(scaled * unit, axis=-1, keepdims=True)
        )
        d_hid[h] = d_hidden
        share_start(i + 1, h, dh, d_hidden)

    def attention_back(l, h, i, x_ref):
        r = of(h)
        share_wait(i + 1, h, dh)
        d_gain = mixer_backward(l, h, dot(dh[r], weight(l, OUT)))
        ranked = low(dot_back(d_pre[r], rank_up[l]))
        d_rank[r] = ranked
        partial = dot_back(dqkvg[r], weight(l, QKVG)) + dot_back(ranked, weight(l, SMALL))
        sum_start(i + 2, h, partial)
        xin = wide(x_ref[r])
        small_rows[l, 0:1] += jnp.sum(partial * (xin * rms_scale(xin)), axis=0, keepdims=True)
        return d_gain

    def backward_end(l, h, i, x_ref, out_ref):
        d_normed = sum_wait(i + 2, h)
        xin = wide(x_ref[rows(t, h)])
        scale_in = rms_scale(xin)
        unit = xin * scale_in
        scaled = d_normed * rows_of[l, 0:1]
        dx = d_hid[h] + scale_in * (scaled - unit * jnp.mean(scaled * unit, axis=-1, keepdims=True))
        share_start(i + 3, h, out_ref, dx)

    def small_copy(l, k):
        peer = (t + k) % T
        return remote(
            EG.at[l, :, :, peer], EB.at[l, k - 1], u_sem.at[l, 0, k - 1], u_sem.at[l, 1, k - 1], tensor=peer
        )

    def small_gradients(l, d_gain):
        rank_rows = downs((16, HV))
        at_gain = low(jnp.where(rank_rows == 2, d_gain, 0.0))
        d_bias = jnp.sum(wide(d_pre[...]), axis=0, keepdims=True)
        at_bias = low(jnp.where(downs((16, HK)) == 3, d_bias, 0.0))
        found = small_rows[l] + dot_back(at_gain, pick_gain[...]) + dot_back(at_bias, pick_bias[...])
        pick = low(jnp.where(lanes((16, 128)) == downs((16, 128)) + AT_IN, 1.0, 0.0))
        ups = dot_grad(rank[l], d_pre[...])
        right = lanes((128, 128)) >= 64
        every = (
            dot_grad(normed[l], d_rank[...])
            + dot_grad(low(found), pick)
            + dot_grad(pick_up[0], low(jnp.where(right, pltpu.roll(ups, 64, 1), 0.0)))
            + dot_grad(pick_up[1], low(jnp.where(right, ups, 0.0)))
        )
        EG[l] = low(every).reshape(X, Z, T, B, 128)
        for k in range(1, T):
            small_copy(l, k).start()

    def small_sum(l):
        total = wide(EG[l, :, :, t])
        for k in range(1, T):
            small_copy(l, k).wait()
            total = total + wide(EB[l, k - 1])
        EY[l] = low(total)

    small_swap_out = remote(EY.at[o], EO, v_sem.at[0, 0], v_sem.at[0, 1], section=o)

    def small_x(k):
        return remote(
            ES.at[(x + k) % X], EX.at[k - 1], v_sem.at[k, 0], v_sem.at[k, 1], dp=dp_peer(0, k)
        )

    def small_z(k):
        return remote(
            ES.at[x, (z + k) % Z], EZ.at[k - 1], v_sem.at[3 + k, 0], v_sem.at[3 + k, 1], dp=dp_peer(1, k)
        )

    def small_first():
        small_swap_out.wait()
        ES[...] = EY[c] + EO[...]
        for k in range(1, X):
            small_x(k).start()

    def small_second():
        total = wide(ES[x])
        for k in range(1, X):
            small_x(k).wait()
            total = total + wide(EX[k - 1])
        ES[x] = low(total)
        for k in range(1, Z):
            small_z(k).start()

    def small_third():
        total = wide(ES[x, z])
        for k in range(1, Z):
            small_z(k).wait()
            total = total + wide(EZ[k - 1])
        small[...] = total

    def backward(l, i, x_ref, dy_ref, out_ref, hooks):
        dy = dy_ref[...]
        d_inner = dot(dy, weight(l, DOWN))
        gate, up, both = gu[l, :, :FFM], gu[l, :, FFM : 2 * FFM], gu[l, :, 2 * FFM :]
        act, act_slope = silu_parts(gate)
        act_b, slope_b = silu_parts(both)
        rest = d_inner[:, FFM:]
        mix_b = rest * pltpu.roll(both, 64, 1) * slope_b + pltpu.roll(rest * act_b, 64, 1)
        d_gu = jnp.concatenate(
            [low(d_inner[:, :FFM] * up * act_slope), low(d_inner[:, :FFM] * act), low(mix_b)], axis=1
        )
        sum_start(i, dot_back(d_gu, weight(l, GU)))
        hooks[4]()
        put(DOWN, dy, inner[l])
        scatter_swap(l, 1)
        put(GU, nm[l], d_gu)
        scatter_swap(l, 0)
        hooks[0]()
        d_mid = sum_wait(i)
        hidden = hid[l]
        scale_mid = rms_scale(hidden)
        unit = hidden * scale_mid
        small_rows[l] = jnp.zeros((16, D), f32)
        small_rows[l, 1:2] = jnp.sum(d_mid * unit, axis=0, keepdims=True)
        scaled = d_mid * rows_of[l, 1:2]
        d_hidden = wide(dy_ref[rows(t)]) + scale_mid * (
            scaled - unit * jnp.mean(scaled * unit, axis=-1, keepdims=True)
        )
        d_hid[...] = d_hidden
        share_start(i + 1, dh, d_hidden)
        hooks[1]()
        share_wait(i + 1, dh)
        dmix[...] = dot(dh[...], weight(l, OUT))
        hooks[5]()
        d_pre, d_gain = mixer_backward(l)
        d_rank = low(dot_back(d_pre, rank_up[l]))
        partial = dot_back(dqkvg[...], weight(l, QKVG)) + dot_back(d_rank, weight(l, SMALL))
        hooks[6]()
        sum_start(i + 2, partial)
        xin = wide(x_ref[...])
        small_rows[l, 0:1] = jnp.sum(partial * (xin * rms_scale(xin)), axis=0, keepdims=True)
        hooks[2]()
        put(OUT, dh[...], mixed[l])
        scatter_swap(l, 2)
        put(QKVG, normed[l], dqkvg[...])
        scatter_swap(l, 3)
        scatter_swap(l, 4)
        small_gradients(l, d_rank, d_pre, d_gain)
        hooks[3]()
        d_normed = sum_wait(i + 2)
        xin = wide(x_ref[rows(t)])
        scale_in = rms_scale(xin)
        unit = xin * scale_in
        scaled = d_normed * rows_of[l, 0:1]
        dx = d_hid[...] + scale_in * (scaled - unit * jnp.mean(scaled * unit, axis=-1, keepdims=True))
        share_start(i + 3, out_ref, dx)

    first_in, mid, late = (0, 1, 2), (3, 4), (5, 6, 7, 8)
    early = first_in + mid

    def first_weights():
        got_near.wait_recv()
        keep_near.wait()
        for j in (0, 1):
            gather_first(0, j)
        small_swap()
        got_e.wait_recv()
        keep_e.wait()
        gather_first(0, 2)
        for j in mid:
            gather_first(0, j)
        got_far.wait_recv()
        keep_far.wait()
        for j in late:
            gather_first(0, j)
        for j in (0, 1):
            gather_second(0, j)
        prepare()
        for j in early[2:]:
            gather_second(0, j)
        for j in first_in:
            gather_third(0, j)
        for j in late:
            gather_second(0, j)
        for j in early:
            gather_first(1, j)

    def each(step, l, which):
        def run():
            for j in which:
                step(l, j)

        return run

    small_rows[...] = jnp.zeros_like(small_rows)
    everything = early + late
    ahead, back = (0, 1), (1, 0)
    x0, cot = xbuf.at[0], xbuf.at[1]

    first_weights()
    small_whole(0)
    got_x.wait_recv()
    keep_x.wait()
    attention(0, 0, 0, x0, mid)
    attention(0, 1, 0, x0)
    middle(0, 0, 0, x0)
    each(gather_third, 0, late[:2])()
    middle(0, 1, 0, x0)
    each(gather_third, 0, late[2:])()
    each(gather_second, 1, early)()
    each(gather_first, 1, late)()
    for h in ahead:
        feed(0, h, 0)
        forward_down(0, h, 0)
    each(gather_third, 1, early)()
    each(gather_second, 1, late)()
    for h in ahead:
        forward_end(0, h, 0, x1)
    small_whole(1)
    for h in ahead:
        share_wait(3, h, x1)
        attention(1, h, 4, x1)
    each(gather_third, 1, late)()
    for h in ahead:
        middle(1, h, 4, x1)
    for h in ahead:
        feed(1, h, 4)

    of_gu, of_down, of_out, of_qkvg = (0, 1), (2, 3), (4, 5), (6, 7)
    ff, mix = of_down + of_gu, of_out + of_qkvg
    for h in back:
        feed_back(1, h, 8, cot)
    put(DOWN, cot[...], inner[1])
    each(scatter_swap, 1, of_down)()
    middle_back(1, 1, 8, cot)
    put(GU, nm[1], d_gu[...])
    each(scatter_swap, 1, of_gu)()
    middle_back(1, 0, 8, cot)
    for h in back:
        forward_down(1, h, 4)
    d_gain = [attention_back(1, h, 8, x1) for h in back]
    put(OUT, dh[...], mixed[1])
    each(scatter_swap, 1, of_out)()
    backward_end(1, 1, 8, x1, dy0)
    put(QKVG, normed[1], dqkvg[...])
    each(scatter_swap, 1, of_qkvg)()
    each(scatter_first, 1, ff)()
    backward_end(1, 0, 8, x1, dy0)
    small_gradients(1, d_gain[0] + d_gain[1])
    for h in back:
        share_wait(11, h, dy0)
        feed_back(0, h, 12, dy0)
    each(scatter_second, 1, ff)()
    put(DOWN, dy0[...], inner[0])
    each(scatter_swap, 0, of_down)()
    middle_back(0, 1, 12, dy0)
    put(GU, nm[0], d_gu[...])
    each(scatter_swap, 0, of_gu)()
    each(scatter_first, 1, mix)()
    middle_back(0, 0, 12, dy0)
    each(scatter_first, 0, ff)()
    each(scatter_third, 1, ff)()
    d_gain = []
    for h in back:
        forward_end(1, h, 4, res.at[1])
        d_gain.append(attention_back(0, h, 12, x0))
    each(scatter_second, 1, mix)()
    put(QKVG, normed[0], dqkvg[...])
    each(scatter_swap, 0, of_qkvg)()
    put(OUT, dh[...], mixed[0])
    each(scatter_swap, 0, of_out)()
    backward_end(0, 1, 12, x0, res.at[0])
    each(scatter_first, 0, of_qkvg + of_out)()
    small_gradients(0, d_gain[0] + d_gain[1])
    backward_end(0, 0, 12, x0, res.at[0])
    each(scatter_second, 0, ff)()
    small_sum(1)
    small_sum(0)
    small_swap_out.start()
    for h in back:
        share_wait(7, h, res.at[1])
    each(scatter_third, 1, mix)()
    for h in back:
        share_wait(15, h, res.at[0])
    give_end = remote(res.at[o], ends.at[0, c], e_sem.at[0], e_sem.at[1], section=o)
    got_end = remote(res.at[o], ends.at[0, o], e_sem.at[0], e_sem.at[1], section=o)
    give_end.start()
    each(scatter_second, 0, mix)()
    small_first()
    ends[0, c] = res[c]
    each(scatter_third, 0, ff)()
    small_second()
    each(scatter_third, 0, mix)()
    give_grad = remote(RF.at[o], og.at[c], e_sem.at[2], e_sem.at[3], section=o)
    got_grad = remote(RF.at[o], og.at[o], e_sem.at[2], e_sem.at[3], section=o)
    give_grad.start()
    og[c] = RF[c]
    got_end.wait_recv()
    small_third()
    got_grad.wait_recv()
    give_end.wait_send()
    give_grad.wait_send()
    swap_near.wait_send()
    swap_far.wait_send()
    swap_x.wait_send()
    swap_e.wait_send()
    for k in range(1, T):
        tile_copy(k)[0].wait_send()
    for l in range(2):
        for j, (_, _, axis) in enumerate(GATHER):
            for k in range(1, size[axis]):
                w_first(l, j, k)[0].wait_send()
            for k in range(1, size[1 - axis]):
                w_second(l, j, k)[0].wait_send()
            w_third(l, j)[0].wait_send()


def unpack(
    packed_ends,
    og,
    small,
    ends,
    g_norm_in,
    g_query,
    g_key,
    g_value,
    g_out_gate,
    g_rank_down,
    g_rank_up,
    g_rank_bias,
    g_head_gain,
    g_out,
    g_norm_mid,
    g_gate,
    g_up,
    g_down,
):
    R, B = 2 * og.shape[1], small.shape[0]
    ends[...] = wide(packed_ends[...])
    whole = lambda c0, n: og[:, :, c0 : c0 + n].reshape(R, n)
    g_query[0] = whole(0, 128)
    g_key[0] = whole(128, 128)
    g_value[0] = whole(256, 256)
    g_out_gate[0] = whole(512, 256)
    g_out[0] = whole(*OUT)
    g_gate[0, :, :FFM] = whole(GU[0], FFM)
    g_up[0, :, :FFM] = whole(GU[0] + FFM, FFM)
    both = whole(GU[0] + 2 * FFM, 128)
    g_gate[0, :, FFM:] = both[:, 0:64]
    g_up[0, :, FFM:] = pltpu.roll(both, 64, 1)[:, 0:64]
    g_down[0] = whole(*DOWN)[:, 0:FFD]
    total = small[...]
    g_rank_down[0] = total[:, 0 : g_rank_down.shape[2]]
    lane = lax.broadcasted_iota(jnp.int32, (B, 128), 1)
    turn = lane == lax.broadcasted_iota(jnp.int32, (B, 128), 0)
    for at, ref in (
        (AT_IN, g_norm_in),
        (AT_MID, g_norm_mid),
        (AT_GAIN, g_head_gain),
        (AT_BIAS, g_rank_bias),
    ):
        row = jnp.sum(jnp.where(turn, total[:, at : at + 1], 0.0), axis=0, keepdims=True)
        ref[...] = row[:, 0 : ref.shape[1]]
    turned = pltpu.roll(total[0:8], 64, 1)[0:1]
    g_rank_up[0] = jnp.where(lane[0:1] < 64, turned, total[1:2])


def on_device(X, Z, *operands):
    T = lax.axis_size("tensor")
    D = operands[0].shape[-1]
    R = operands[3].shape[1]
    H, TL, B, N = R // 2, TOK // T, R // T, X * Z
    top = max(X, Z)
    scratch = [
        pltpu.VMEM((2, X, Z, 2, H, WIDE), bf16),
        pltpu.VMEM((R, WIDE), bf16),
        pltpu.VMEM((T, B, 128), bf16),
        pltpu.VMEM((max(B, 8), 128), f32),
        pltpu.VMEM((D, HV), bf16),
        pltpu.VMEM((D, HK), bf16),
        pltpu.VMEM((2, 128, D), bf16),
        pltpu.VMEM((2, 16, D), f32),
        pltpu.VMEM((2, 1, HV), f32),
        pltpu.VMEM((2, 1, HK), f32),
        pltpu.VMEM((2, 128, HK), bf16),
        pltpu.VMEM((TOK, TOK), f32),
        pltpu.VMEM((TOK, 128), f32),
        pltpu.VMEM((2, TOK, D), bf16),
        pltpu.VMEM((TOK, D), bf16),
        pltpu.VMEM((2, TOK, D), bf16),
        pltpu.VMEM((2, TOK, D), bf16),
        pltpu.VMEM((2, TOK, 768), f32),
        pltpu.VMEM((2, TOK, HK), f32),
        pltpu.VMEM((2, TOK, HK), f32),
        pltpu.VMEM((2, 2, TOK // 2, TOK // 2), bf16),
        pltpu.VMEM((2, BLOCKS - 1, HV, HK), f32),
        pltpu.VMEM((2, TOK, HV), f32),
        pltpu.VMEM((2, TOK, HV), bf16),
        pltpu.VMEM((2, 2, TL // 2, D), f32),
        pltpu.VMEM((2, TL // 2, D), f32),
        pltpu.VMEM((2, TOK, GU[1]), f32),
        pltpu.VMEM((2, TOK, DOWN[1]), bf16),
        pltpu.VMEM((2, TOK, 128), bf16),
        pltpu.VMEM((TOK, D), bf16),
        pltpu.VMEM((TOK, D), bf16),
        pltpu.VMEM((2, TOK, D), bf16),
        pltpu.VMEM((3, TOK, D), bf16),
        pltpu.VMEM((3, 2, T - 1, TL // 2, D), bf16),
        pltpu.VMEM((X, Z, 2, H, SMALL[0]), bf16),
        pltpu.VMEM((2, X, Z, H, SMALL[0]), bf16),
        pltpu.VMEM((2, top - 1, top, H, SMALL[0]), bf16),
        pltpu.VMEM((2, top - 1, H, SMALL[0]), bf16),
        pltpu.VMEM((2, top, H, SMALL[0]), bf16),
        pltpu.VMEM((2, H, SMALL[0]), f32),
        pltpu.VMEM((TOK, 768), bf16),
        pltpu.VMEM((TOK, GU[1]), bf16),
        pltpu.VMEM((TOK, 128), bf16),
        pltpu.VMEM((TOK, 128), bf16),
        pltpu.VMEM((HV, HK), f32),
        pltpu.VMEM((2, 16, D), f32),
        pltpu.VMEM((2, X, Z, T, B, 128), bf16),
        pltpu.VMEM((2, X, Z, B, 128), bf16),
        pltpu.VMEM((2, T - 1, X, Z, B, 128), bf16),
        pltpu.VMEM((X, Z, B, 128), bf16),
        pltpu.VMEM((X, Z, B, 128), bf16),
        pltpu.VMEM((X - 1, Z, B, 128), bf16),
        pltpu.VMEM((Z - 1, B, 128), bf16),
        pltpu.SemaphoreType.DMA((12,)),
        pltpu.SemaphoreType.DMA((2, len(GATHER), 7)),
        pltpu.SemaphoreType.DMA((2, len(GATHER), 7)),
        pltpu.SemaphoreType.DMA((16, 2, T - 1)),
        pltpu.SemaphoreType.DMA((16, 2, T - 1)),
        pltpu.SemaphoreType.DMA((2, len(SCATTER), 7)),
        pltpu.SemaphoreType.DMA((2, len(SCATTER), 7)),
        pltpu.SemaphoreType.DMA((4,)),
        pltpu.SemaphoreType.DMA((2, T - 1)),
        pltpu.SemaphoreType.DMA((2, 2, T - 1)),
        pltpu.SemaphoreType.DMA((7, 2)),
    ]
    flipped = lambda a: a.transpose(0, 2, 1)
    operands = list(operands)
    operands[11], operands[15] = flipped(operands[11]), flipped(operands[15])
    vmem = pl.BlockSpec(memory_space=pltpu.VMEM)
    smem = pl.BlockSpec(memory_space=pltpu.SMEM)
    packed = pl.pallas_call(
        functools.partial(kernel, X, Z, T),
        out_shape=(
            jax.ShapeDtypeStruct((1, 2, TOK, D), bf16),
            jax.ShapeDtypeStruct((2, H, SMALL[0]), f32),
            jax.ShapeDtypeStruct((B, 128), f32),
        ),
        in_specs=[vmem, smem] + [vmem] * (len(operands) - 2),
        out_specs=(vmem,) * 3,
        scratch_shapes=scratch,
        compiler_params=pltpu.CompilerParams(
            collective_id=0, has_side_effects=True, vmem_limit_bytes=64 * 1024 * 1024 - 65536
        ),
    )(*operands)
    outs = (jax.ShapeDtypeStruct((1, 2, TOK, D), f32),) + tuple(
        jax.ShapeDtypeStruct(operands[k].shape, f32) for k in range(2, 16)
    )
    results = list(
        pl.pallas_call(
            unpack,
            out_shape=outs,
            in_specs=[vmem] * 3,
            out_specs=(vmem,) * len(outs),
            compiler_params=pltpu.CompilerParams(vmem_limit_bytes=32 * 1024 * 1024),
        )(*packed)
    )
    results[10], results[14] = flipped(results[10]), flipped(results[14])
    return tuple(results)


def solution(mesh):
    count = mesh.shape["dp"]
    side = {16: 4, 4: 2}[count]
    in_specs = (
        P("section", None, "dp", None),
        P("dp", None),
        P("section", ("dp", "tensor")),
        P("section", "dp", "tensor"),
        P("section", "dp", "tensor"),
        P("section", "dp", "tensor"),
        P("section", "dp", "tensor"),
        P("section", ("dp", "tensor"), None),
        P("section", "dp", "tensor"),
        P("section", ("dp", "tensor")),
        P("section", ("dp", "tensor")),
        P("section", "tensor", "dp"),
        P("section", ("dp", "tensor")),
        P("section", "dp", "tensor"),
        P("section", "dp", "tensor"),
        P("section", "tensor", "dp"),
    )
    out_specs = (
        P("section", None, "dp", None),
        P("section", ("dp", "tensor")),
        P("section", "dp", "tensor"),
        P("section", "dp", "tensor"),
        P("section", "dp", "tensor"),
        P("section", "dp", "tensor"),
        P("section", ("dp", "tensor"), None),
        P("section", "dp", "tensor"),
        P("section", ("dp", "tensor")),
        P("section", ("dp", "tensor")),
        P("section", "tensor", "dp"),
        P("section", ("dp", "tensor")),
        P("section", "dp", "tensor"),
        P("section", "dp", "tensor"),
        P("section", "tensor", "dp"),
    )
    return jax.shard_map(
        functools.partial(on_device, side, count // side),
        mesh=mesh,
        in_specs=in_specs,
        out_specs=out_specs,
        check_vma=False,
    )
```
